32 devices in a mesh: batch: 8 (over y, x, core), tensor: 4 (over z).
Axes of the slice: x: 2, y: 2, z: 4, core: 2. Of those that a mesh axis runs over, the one named last changes fastest.
Arguments:
- hidden_in: bfloat16 [16384, 1024], P('batch'), may hold values from -6 to 6
- skip_state: bfloat16 [16384, 1024], P('batch'), may hold values from -6 to 6
- lengths: int32 [16], P('batch'), may hold values from 64 to 1024, as said below
- w_skip: bfloat16 [2048, 1024], P('tensor'), may hold values from -0.125 to 0.125
- b_skip: float32 [1024], replicated, may hold values from -3 to 3
- norm1_gain: float32 [1024], replicated, may hold values from 0.25 to 1.75
- norm1_bias: float32 [1024], replicated, may hold values from -3 to 3
- w_qkv: bfloat16 [3, 1024, 1024], P(None, None, 'tensor'), may hold values from -0.1875 to 0.1875
- b_qv: float32 [2, 1024], P(None, 'tensor'), may hold values from -3 to 3
- w_out: bfloat16 [1024, 1024], P('tensor'), may hold values from -0.5 to 0.5
- b_out: float32 [1024], replicated, may hold values from -3 to 3
- norm2_gain: float32 [1024], replicated, may hold values from 0.25 to 1.75
- norm2_bias: float32 [1024], replicated, may hold values from -3 to 3
- w_up: bfloat16 [1024, 4096], P(None, 'tensor'), may hold values from -0.1875 to 0.1875
- b_up: float32 [4096], P('tensor'), may hold values from -3 to 3
- w_down: bfloat16 [4096, 1024], P('tensor'), may hold values from -0.09375 to 0.09375
- b_down: float32 [1024], replicated, may hold values from -3 to 3
- cotangent: bfloat16 [16384, 1024], P('batch'), may hold values from -6 to 6
Outputs:
- output: bfloat16 [16384, 1024], P('batch')
- grad_hidden: bfloat16 [16384, 1024], P('batch')
- grad_skip: bfloat16 [16384, 1024], P('batch')
- grad_w_skip: float32 [2048, 1024], P('tensor')
- grad_b_skip: float32 [1024], replicated
- grad_norm1_gain: float32 [1024], replicated
- grad_norm1_bias: float32 [1024], replicated
- grad_w_qkv: float32 [3, 1024, 1024], P(None, None, 'tensor')
- grad_b_qv: float32 [2, 1024], P(None, 'tensor')
- grad_w_out: float32 [1024, 1024], P('tensor')
- grad_b_out: float32 [1024], replicated
- grad_norm2_gain: float32 [1024], replicated
- grad_norm2_bias: float32 [1024], replicated
- grad_w_up: float32 [1024, 4096], P(None, 'tensor')
- grad_b_up: float32 [4096], P('tensor')
- grad_w_down: float32 [4096, 1024], P('tensor')
- grad_b_down: float32 [1024], replicated
The draws below stay inside these ranges and needn't reach their ends.
Inputs may be any that keep to these rules, and one draw needn't show every extreme that they name: `lengths`: frames of each utterance, each padded to 1024 slots; in every draw exactly one utterance of all 16 has 1024 frames and one has 64.
All inputs are finite; a program needn't handle non-finite values.
Results may differ from the reference program's by a relative error of at most 0.035.
Values may be sent and summed in bfloat16 or wider, within the bound.
No kernel may reach another device: no remote copies, remote signals or barrier semaphores. Data moves between devices by JAX's collectives and lax.ppermute only.
A program may use at most 256 MiB of HBM per device.

```python
import math
import jax
import jax.numpy as jnp
from jax import lax

D = 1024
HEADS = 16
HEAD_DIM = 64
FF = 4096
LEN = 1024
UTTS = 16
TOKENS = 16384
N_TENSOR = 4


def draw_lengths(key, part):
    key = jax.random.fold_in(key, 7)
    subkeys = jax.random.split(key, 5)
    shorter = jax.random.randint(subkeys[0], (UTTS,), LEN // 16 + 1, LEN // 3 + 1)
    longer = LEN - jax.random.randint(subkeys[1], (UTTS,), 1, LEN // 8 + 1)
    picker = jax.random.randint(subkeys[2], (UTTS,), 0, 8)
    chosen = jnp.where(picker == 0, longer, shorter)
    first_slot = jax.random.randint(subkeys[3], (), 0, UTTS)
    second_slot = (first_slot + 1 + jax.random.randint(subkeys[4], (), 0, UTTS - 1)) % UTTS
    chosen = chosen.at[first_slot].set(LEN).at[second_slot].set(LEN // 16)
    return chosen.astype(jnp.int32)


def levels(rng, dims, cuts, smallest, high):
    level, own = 1.0, jax.random.fold_in(rng, 6)
    for dim, blocks in cuts:
        steps = jnp.exp(jax.random.uniform(jax.random.fold_in(own, dim), (blocks,), jnp.float32, smallest / len(cuts), high / len(cuts)))
        level = level * jnp.repeat(steps, dims[dim] // blocks).reshape([-1 if axis == dim else 1 for axis in range(len(dims))])
    return level


def gaussian(key, extent, scale, most, cuts=(), kind=jnp.bfloat16):
    values = scale * jax.random.normal(key, extent, jnp.float32)
    if cuts:
        values = values * levels(key, extent, cuts, -0.22, 0.18)
    return jnp.clip(values, -most, most).astype(kind)


def setup_inputs(seed: int = 0) -> dict:
    key_of = jax.random.split(jax.random.key(seed), 19)
    return {
        "hidden_in": gaussian(key_of[0], (TOKENS, D), 1.0, 6.0, ((0, 8),)),
        "skip_state": gaussian(key_of[1], (TOKENS, D), 1.0, 6.0, ((0, 8),)),
        "lengths": draw_lengths(jax.random.fold_in(key_of[18], 71), 0),
        "w_skip": gaussian(key_of[3], (2 * D, D), (2 * D) ** -0.5, 0.125, ((0, 4),)),
        "b_skip": gaussian(key_of[4], (D,), 0.3, 3.0, (), jnp.float32),
        "norm1_gain": jnp.clip(1.0 + 0.15 * jax.random.normal(key_of[5], (D,), jnp.float32), 0.25, 1.75),
        "norm1_bias": gaussian(key_of[6], (D,), 0.3, 3.0, (), jnp.float32),
        "w_qkv": gaussian(key_of[7], (3, D, D), D ** -0.5, 0.1875, ((2, 4),)),
        "b_qv": gaussian(key_of[8], (2, D), 0.3, 3.0, ((1, 4),), jnp.float32),
        "w_out": gaussian(key_of[9], (D, D), (D // 8) ** -0.5, 0.5, ((0, 4),)),
        "b_out": gaussian(key_of[10], (D,), 0.3, 3.0, (), jnp.float32),
        "norm2_gain": jnp.clip(1.0 + 0.15 * jax.random.normal(key_of[11], (D,), jnp.float32), 0.25, 1.75),
        "norm2_bias": gaussian(key_of[12], (D,), 0.3, 3.0, (), jnp.float32),
        "w_up": gaussian(key_of[13], (D, FF), D ** -0.5, 0.1875, ((1, 4),)),
        "b_up": gaussian(key_of[14], (FF,), 0.3, 3.0, ((0, 4),), jnp.float32),
        "w_down": gaussian(key_of[15], (FF, D), FF ** -0.5, 0.09375, ((0, 4),)),
        "b_down": gaussian(key_of[16], (D,), 0.3, 3.0, (), jnp.float32),
        "cotangent": gaussian(key_of[17], (TOKENS, D), 1.0, 6.0, ((0, 8),)),
    }


@jax.custom_vjp
def low(v):
    return lax.optimization_barrier(v.astype(jnp.bfloat16)).astype(jnp.float32)

@jax.custom_vjp
def low_back(v):
    return v

def low_keep(v):
    return (low(v), None)

def low_pass(kept, grad):
    return (grad,)

def back_keep(v):
    return (v, None)

def back_low(kept, grad):
    return (low(grad),)
low.defvjp(low_keep, low_pass)
low_back.defvjp(back_keep, back_low)
highest = lax.Precision.HIGHEST
norm_eps = 1e-05
masked_score = -1e+30

def product(left, right):
    return jnp.dot(left, right, precision=highest, preferred_element_type=jnp.float32)

def layer_norm(values, gain, shift):
    centred = values - lax.optimization_barrier(jnp.mean(values, axis=-1, keepdims=True))
    variance = lax.optimization_barrier(jnp.mean(centred * centred, axis=-1, keepdims=True))
    return centred * lax.rsqrt(variance + norm_eps) * gain + shift

def gelu_tanh(values):
    return jax.nn.gelu(values, approximate=True)

def alibi_slopes(first_head, head_count):
    head_index = first_head + jnp.arange(head_count, dtype=jnp.int32) + 1
    return jnp.exp2(-8.0 * head_index.astype(jnp.float32) / HEADS)

def forward_group(params, hidden_rows, skip_rows, group_lengths):
    w_skip, b_skip, norm1_gain, norm1_bias, w_qkv, b_qv, w_out, b_out, norm2_gain, norm2_bias, w_up, b_up, w_down, b_down = params
    shards = N_TENSOR
    group_size = group_lengths.shape[0]
    row_count = hidden_rows.shape[0]
    feature_block = 2 * D // shards
    column_block = D // shards
    hidden_block = FF // shards
    heads_local = HEADS // shards
    score_scale = HEAD_DIM ** (-0.5)
    positions = jnp.arange(LEN, dtype=jnp.int32)
    distance = jnp.abs(positions[:, None] - positions[None, :]).astype(jnp.float32)
    valid = positions[None, :] < group_lengths[:, None]
    joined = jnp.concatenate([hidden_rows, skip_rows], axis=1)
    skip_terms = []
    for shard in range(shards):
        features = low_back(joined[:, shard * feature_block:(shard + 1) * feature_block])
        skip_terms.append(low(product(features, w_skip[shard * feature_block:(shard + 1) * feature_block])))
    state_zero = low_back(sum(skip_terms)) + b_skip
    normed_one = low(layer_norm(state_zero, norm1_gain, norm1_bias))
    shape_heads = (group_size, LEN, heads_local, HEAD_DIM)
    attn_terms = []
    for shard in range(shards):
        first_col = shard * column_block
        last_col = first_col + column_block
        normed_view = low_back(normed_one)
        queries = low(low_back(product(normed_view, w_qkv[0][:, first_col:last_col]) + b_qv[0][first_col:last_col]))
        keys_all = low(low_back(product(normed_view, w_qkv[1][:, first_col:last_col])))
        values_all = low(low_back(product(normed_view, w_qkv[2][:, first_col:last_col]) + b_qv[1][first_col:last_col]))
        scores = jnp.einsum('gqhe,gkhe->ghqk', queries.reshape(shape_heads), keys_all.reshape(shape_heads), precision=highest) * score_scale
        slopes = alibi_slopes(shard * heads_local, heads_local)
        scores = low_back(scores - slopes[None, :, None, None] * distance[None, None])
        scores = jnp.where(valid[:, None, None, :], scores, masked_score)
        weights = low(jax.nn.softmax(scores, axis=-1))
        mixed = jnp.einsum('ghqk,gkhe->gqhe', weights, values_all.reshape(shape_heads), precision=highest)
        mixed = mixed * valid[:, :, None, None].astype(jnp.float32)
        mixed = low(low_back(mixed.reshape(row_count, column_block)))
        attn_terms.append(low(product(mixed, w_out[first_col:last_col])))
    state_one = state_zero + low_back(sum(attn_terms)) + b_out
    normed_two = low(layer_norm(state_one, norm2_gain, norm2_bias))
    ffn_terms = []
    for shard in range(shards):
        first_unit = shard * hidden_block
        last_unit = first_unit + hidden_block
        normed_part = low_back(normed_two)
        pre_act = low_back(product(normed_part, w_up[:, first_unit:last_unit]) + b_up[first_unit:last_unit])
        activated = low(gelu_tanh(pre_act))
        ffn_terms.append(low(product(activated, w_down[first_unit:last_unit])))
    return state_one + low_back(sum(ffn_terms)) + b_down

def reference(hidden_in, skip_state, lengths, w_skip, b_skip, norm1_gain, norm1_bias, w_qkv, b_qv, w_out, b_out, norm2_gain, norm2_bias, w_up, b_up, w_down, b_down, cotangent):
    params = tuple((item.astype(jnp.float32) for item in (w_skip, b_skip, norm1_gain, norm1_bias, w_qkv, b_qv, w_out, b_out, norm2_gain, norm2_bias, w_up, b_up, w_down, b_down)))
    group_size = math.gcd(UTTS, max(1, 4096 // LEN))
    group_count = UTTS // group_size
    hidden_groups = hidden_in.astype(jnp.float32).reshape(group_count, group_size * LEN, D)
    skip_groups = skip_state.astype(jnp.float32).reshape(group_count, group_size * LEN, D)
    length_groups = lengths.astype(jnp.int32).reshape(group_count, group_size)
    checked = jax.checkpoint(forward_group)

    def whole(param_set, hidden_set, skip_set):
        return lax.map(lambda item: checked(param_set, item[0], item[1], item[2]), (hidden_set, skip_set, length_groups))
    result, pullback = jax.vjp(whole, params, hidden_groups, skip_groups)
    cotangent_groups = cotangent.astype(jnp.float32).reshape(group_count, group_size * LEN, D)
    grad_params, grad_hidden, grad_skip = pullback(cotangent_groups)
    return (result.reshape(TOKENS, D).astype(jnp.bfloat16), grad_hidden.reshape(TOKENS, D).astype(jnp.bfloat16), grad_skip.reshape(TOKENS, D).astype(jnp.bfloat16), grad_params[0], grad_params[1], grad_params[2], grad_params[3], grad_params[4], grad_params[5], grad_params[6], grad_params[7], grad_params[8], grad_params[9], grad_params[10], grad_params[11], grad_params[12], grad_params[13])
```

```python
import functools

import jax
import jax.numpy as jnp
from jax import lax
from jax.experimental import pallas as pl
from jax.experimental.pallas import tpu as pltpu
from jax.sharding import PartitionSpec as P

HEADS = 16
HEAD_DIM = 64
GROUP = 8
TILE = 256
LOG2E = 1.4426950408889634
LN2 = 0.6931471805599453
GELU_C = 0.7978845608028654
GELU_A = 0.044715

norm_eps = 1e-05
masked_score = -1e30
bf16 = jnp.bfloat16
f32 = jnp.float32

NT = (((1,), (1,)), ((), ()))
TN = (((0,), (0,)), ((), ()))

PIECES = [0, 2, 4, 6, 1, 3, 5, 7]
COUNT = len(PIECES)


def dot(a, b):
    return jnp.dot(a, b, preferred_element_type=f32)


def dot_nt(a, b):
    return lax.dot_general(a, b, NT, preferred_element_type=f32)


def dot_tn(a, b):
    return lax.dot_general(a, b, TN, preferred_element_type=f32)


def params(ndim, mib=60):
    return pltpu.CompilerParams(
        vmem_limit_bytes=mib * 1024 * 1024, dimension_semantics=("arbitrary",) * ndim
    )


def cost(flops, moved):
    return pl.CostEstimate(flops=int(flops), bytes_accessed=int(moved), transcendentals=0)


def along(x, k):
    n = lax.axis_size("tensor")
    return lax.ppermute(x, "tensor", [(i, (i + k) % n) for i in range(n)])


def across(x, m):
    n = lax.axis_size("batch")
    return lax.ppermute(x, "batch", [(i, i ^ m) for i in range(n)])


def from_chips(held):
    return [held, across(held, 2), across(held, 4), across(held, 6)]


def from_cores(held):
    return held + [across(x, 1) for x in held]


def after(x, *earlier):
    return lax.optimization_barrier((x,) + earlier)[0]


def start_loads(info, refs, own, targets, sem):
    for first, rows, own_first, dest, place in targets:
        off = pl.multiple_of(place(info[0], 0), 16)
        pltpu.make_async_copy(
            own.at[pl.ds(own_first, rows * GROUP)], dest.at[pl.ds(off, rows * GROUP)], sem
        ).start()
    for ref, m in zip(refs, PIECES):
        for kk in range(3):
            src_t = (info[0] + 3 - kk) & 3
            src_b = info[1] ^ m
            for first, rows, _, dest, place in targets:
                off = pl.multiple_of(place(src_t, src_b), 16)
                pltpu.make_async_copy(
                    ref.at[kk, pl.ds(first, rows)], dest.at[pl.ds(off, rows)], sem
                ).start()


def wait_whole(dest, sem):
    pltpu.make_async_copy(dest, dest, sem).wait()


ANY = pl.BlockSpec(memory_space=pltpu.HBM)


def whole(shape):
    return pl.BlockSpec(shape, lambda *_: (0,) * len(shape))


def once(shape):
    return pl.BlockSpec(shape, lambda *_: (0,) * len(shape), pipeline_mode=pl.Buffered(1))


def normalise(v):
    mean = jnp.mean(v, axis=-1, keepdims=True)
    centred = v - mean
    r = lax.rsqrt(jnp.mean(centred * centred, axis=-1, keepdims=True) + norm_eps)
    return centred * r, r


def norm_back(grad, n, r, gain):
    e = grad * gain
    return r * (
        e
        - jnp.mean(e, axis=-1, keepdims=True)
        - n * jnp.mean(e * n, axis=-1, keepdims=True)
    )


def tile_length(info, i, tiles_per):
    u = i // tiles_per
    return (i - u * tiles_per) * TILE, info[2 + u]


def skip_targets(w):
    shard = w.shape[0] // 4
    piece = shard // GROUP
    return [(0, piece, 0, w, lambda t, b: t * shard + b * piece)]


def out_targets(w, first):
    shard = w.shape[0] // 4
    piece = shard // GROUP
    return [(first, piece, 0, w, lambda t, b: t * shard + b * piece)]


def skip_kernel(info, hid, skp, b_skip, gain, bias, *rest):
    own, refs, (state, normed, w, sem) = rest[0], rest[1 : 1 + COUNT], rest[1 + COUNT :]

    @pl.when(pl.program_id(0) == 0)
    def _():
        start_loads(info, refs, own, skip_targets(w), sem)
        wait_whole(w, sem)

    width = hid.shape[1]
    total = dot(hid[...], w[:width]) + dot(skp[...], w[width:]) + b_skip[...]
    state[...] = total.astype(bf16)
    n, _ = normalise(total)
    normed[...] = (n * gain[...] + bias[...]).astype(bf16)


def skip_call(info, hid, skp, b_skip, gain, bias, own, pieces):
    rows, d = hid.shape
    row = pl.BlockSpec((TILE, d), lambda i, s: (i, 0))
    return pl.pallas_call(
        skip_kernel,
        grid_spec=pltpu.PrefetchScalarGridSpec(
            num_scalar_prefetch=1,
            grid=(rows // TILE,),
            in_specs=[row, row, whole((1, d)), whole((1, d)), whole((1, d))] + [ANY] * (1 + COUNT),
            out_specs=[row, row],
            scratch_shapes=[pltpu.VMEM((2 * d, d), bf16), pltpu.SemaphoreType.DMA],
        ),
        out_shape=[jax.ShapeDtypeStruct((rows, d), bf16)] * 2,
        compiler_params=params(1),
        cost_estimate=cost(4 * rows * d * d, rows * d * 10 + 4 * d * d),
        name="skip_norm",
    )(info, hid, skp, b_skip, gain, bias, own, *pieces)


def qkv_targets(w):
    d = w.shape[0] // 3
    shard = d // 4
    part = shard // GROUP
    return [
        (s * part, part, s * shard, w, lambda t, b, s=s: s * d + t * shard + b * part)
        for s in range(3)
    ]


def qkv_kernel(tiles_per, info, x, b_q, b_v, *rest):
    own, refs, (q, k, v, w, sem) = rest[0], rest[1 : 1 + COUNT], rest[1 + COUNT :]
    i = pl.program_id(0)
    d = x.shape[1]

    @pl.when(i == 0)
    def _():
        start_loads(info, refs, own, qkv_targets(w), sem)
        wait_whole(w, sem)

    first, length = tile_length(info, i, tiles_per)

    @pl.when(first < length)
    def _():
        xs = x[...]
        q[...] = ((dot_nt(xs, w[:d]) + b_q[...]) * (LOG2E * HEAD_DIM**-0.5)).astype(bf16)
        k[...] = dot_nt(xs, w[d : 2 * d]).astype(bf16)
        v[...] = (dot_nt(xs, w[2 * d :]) + b_v[...]).astype(bf16)


def qkv_call(info, x, b_q, b_v, own, pieces, tiles_per):
    rows, d = x.shape
    row = pl.BlockSpec((TILE, d), lambda i, s: (i, 0))
    return pl.pallas_call(
        functools.partial(qkv_kernel, tiles_per),
        grid_spec=pltpu.PrefetchScalarGridSpec(
            num_scalar_prefetch=1,
            grid=(rows // TILE,),
            in_specs=[row, whole((1, d)), whole((1, d))] + [ANY] * (1 + COUNT),
            out_specs=[row] * 3,
            scratch_shapes=[pltpu.VMEM((3 * d, d), bf16), pltpu.SemaphoreType.DMA],
        ),
        out_shape=[jax.ShapeDtypeStruct((rows, d), bf16)] * 3,
        compiler_params=params(1),
        cost_estimate=cost(4 * rows * d * d, rows * d * 8 + 6 * d * d),
        name="qkv",
    )(info, x, b_q, b_v, own, *pieces)


def slope2(head):
    return jnp.exp2(jnp.full((1, 1), -8.0 / HEADS, f32) * (head + 1).astype(f32)) * LOG2E


def attend_kernel(info, q, k, v, mixed, lse, dist):
    u, hp = pl.program_id(0), pl.program_id(1)
    seq = q.shape[0]
    tiles = seq // TILE
    length = info[2 + u]

    @pl.when((u == 0) & (hp == 0))
    def _():
        r = lax.broadcasted_iota(jnp.int32, dist.shape, 0)
        c = lax.broadcasted_iota(jnp.int32, dist.shape, 1)
        dist[...] = jnp.abs(r - c + (seq - TILE)).astype(f32)

    lane = lax.broadcasted_iota(jnp.int32, (TILE, 128), 1)
    used = (length + TILE - 1) // TILE

    for n in range(1, tiles + 1):

        @pl.when(used == n)
        def _(n=n):
            cols = n * TILE
            valid = (
                lax.broadcasted_iota(jnp.int32, (TILE, TILE), 1) + (cols - TILE) < length
            )

            def step(i, carry):
                row0 = pl.multiple_of(i * TILE, TILE)
                qs = q[pl.ds(row0, TILE), :]
                start = pl.multiple_of((seq - TILE) - row0, TILE)
                gap = dist[:, pl.ds(start, cols)]
                outs, sums = [], []
                for a in range(2):
                    qa = jnp.where((lane < 64) == (a == 0), qs, jnp.zeros_like(qs))
                    s = dot_nt(qa, k[:cols, :]) - slope2(2 * hp + a) * gap
                    last = jnp.where(valid, s[:, cols - TILE :], masked_score)
                    s = jnp.concatenate([s[:, : cols - TILE], last], axis=1) if n > 1 else last
                    m = jnp.max(s, axis=1, keepdims=True)
                    p = jnp.exp2(s - m)
                    total = jnp.sum(p, axis=1, keepdims=True)
                    outs.append(dot(p.astype(bf16), v[:cols, :]) * (1.0 / total))
                    sums.append(m + jnp.log2(total))
                o = jnp.where(lane < 64, outs[0], outs[1])
                pos = lax.broadcasted_iota(jnp.int32, (TILE, 128), 0) + row0
                mixed[pl.ds(row0, TILE), :] = jnp.where(pos < length, o, 0.0).astype(bf16)
                old = lse[pl.ds(row0, TILE), :]
                new = jnp.where(lane == 2 * hp, sums[0], old)
                lse[pl.ds(row0, TILE), :] = jnp.where(lane == 2 * hp + 1, sums[1], new)
                return carry

            lax.fori_loop(0, n, step, 0)
            if n < tiles:
                mixed[cols:, :] = jnp.zeros((seq - cols, 128), bf16)


def attend_call(info, q, k, v, seq):
    rows, d = q.shape
    utts = rows // seq
    blk = pl.BlockSpec((seq, 128), lambda u, h, s: (u, h))
    return pl.pallas_call(
        attend_kernel,
        grid_spec=pltpu.PrefetchScalarGridSpec(
            num_scalar_prefetch=1,
            grid=(utts, d // 128),
            in_specs=[blk] * 3,
            out_specs=[blk, pl.BlockSpec((seq, 128), lambda u, h, s: (u, 0))],
            scratch_shapes=[pltpu.VMEM((TILE, 2 * seq - TILE), f32)],
        ),
        out_shape=[
            jax.ShapeDtypeStruct((rows, d), bf16),
            jax.ShapeDtypeStruct((rows, 128), f32),
        ],
        compiler_params=params(2),
        cost_estimate=cost(rows * seq * d * 4, rows * d * 8),
        name="attend",
    )(info, q, k, v)


def attend_back_kernel(info, q, k, v, g, o, lse, dq, dk, dv, dist, akey, aval):
    u, hp = pl.program_id(0), pl.program_id(1)
    seq = q.shape[0]
    tiles = seq // TILE
    length = info[2 + u]

    @pl.when((u == 0) & (hp == 0))
    def _():
        r = lax.broadcasted_iota(jnp.int32, dist.shape, 0)
        c = lax.broadcasted_iota(jnp.int32, dist.shape, 1)
        dist[...] = jnp.abs(r - c - (seq - TILE)).astype(f32)

    lane = lax.broadcasted_iota(jnp.int32, (TILE, 128), 1)
    used = (length + TILE - 1) // TILE

    for n in range(1, tiles + 1):

        @pl.when(used == n)
        def _(n=n):
            cols = n * TILE
            valid = (
                lax.broadcasted_iota(jnp.int32, (TILE, TILE), 0) + (cols - TILE) < length
            )
            akey[:cols, :] = jnp.zeros((cols, 128), f32)
            aval[:cols, :] = jnp.zeros((cols, 128), f32)
            klane = lax.broadcasted_iota(jnp.int32, (cols, 128), 1)

            def step(i, carry):
                row0 = pl.multiple_of(i * TILE, TILE)
                qs = q[pl.ds(row0, TILE), :]
                gs = g[pl.ds(row0, TILE), :]
                start = pl.multiple_of((seq - TILE) - row0, TILE)
                gap = dist[pl.ds(start, cols), :]
                both = gs.astype(f32) * o[pl.ds(row0, TILE), :].astype(f32)
                hi = both.astype(bf16)
                lo = (both - hi.astype(f32)).astype(bf16)
                grads = []
                for a in range(2):
                    mine = (lane < 64) == (a == 0)
                    qa = jnp.where(mine, qs, jnp.zeros_like(qs))
                    ga = jnp.where(mine, gs, jnp.zeros_like(gs))
                    pick = jnp.where(
                        (lax.broadcasted_iota(jnp.int32, (8, 128), 1) < 64) == (a == 0), 1.0, 0.0
                    ).astype(bf16)
                    delta = (dot_nt(pick, hi) + dot_nt(pick, lo))[:1, :]
                    row = lse[pl.ds(2 * hp + a, 1), pl.ds(row0, TILE)]
                    s = dot_nt(k[:cols, :], qa) - (slope2(2 * hp + a) * gap + row)
                    last = jnp.where(valid, s[cols - TILE :, :], masked_score)
                    s = jnp.concatenate([s[: cols - TILE, :], last], axis=0) if n > 1 else last
                    p = jnp.exp2(s)
                    gw = dot_nt(v[:cols, :], ga)
                    ds = (p * (gw - delta)).astype(bf16)
                    aval[:cols, :] += dot(p.astype(bf16), ga)
                    akey[:cols, :] += dot(ds, qa)
                    ka = k[:cols, :]
                    ka = jnp.where((klane < 64) == (a == 0), ka, jnp.zeros_like(ka))
                    grads.append(dot_tn(ds, ka))
                dq[pl.ds(row0, TILE), :] = ((grads[0] + grads[1]) * HEAD_DIM**-0.5).astype(bf16)
                return carry

            lax.fori_loop(0, n, step, 0)
            dk[:cols, :] = (akey[:cols, :] * LN2).astype(bf16)
            dv[:cols, :] = aval[:cols, :].astype(bf16)
            if n < tiles:
                for ref in (dq, dk, dv):
                    ref[cols:, :] = jnp.zeros((seq - cols, 128), bf16)


def attend_back_call(info, q, k, v, g, o, lse, seq):
    rows, d = q.shape
    utts = rows // seq
    blk = pl.BlockSpec((seq, 128), lambda u, h, s: (u, h))
    return pl.pallas_call(
        attend_back_kernel,
        grid_spec=pltpu.PrefetchScalarGridSpec(
            num_scalar_prefetch=1,
            grid=(utts, d // 128),
            in_specs=[blk] * 5 + [pl.BlockSpec((HEADS, seq), lambda u, h, s: (0, u))],
            out_specs=[blk] * 3,
            scratch_shapes=[
                pltpu.VMEM((2 * seq - TILE, TILE), f32),
                pltpu.VMEM((seq, 128), f32),
                pltpu.VMEM((seq, 128), f32),
            ],
        ),
        out_shape=[jax.ShapeDtypeStruct((rows, d), bf16)] * 3,
        compiler_params=params(2),
        cost_estimate=cost(rows * seq * d * 10, rows * d * 16),
        name="attend_back",
    )(info, q, k, v, g, o, lse)


def mix_kernel(tiles_per, info, mixed, state, b_out, gain, bias, *rest):
    own, refs, (state_one, normed, w, total, sem) = rest[0], rest[1 : 1 + COUNT], rest[1 + COUNT :]
    part = (own.shape[0] // GROUP) * 2
    i = pl.program_id(0)
    d = mixed.shape[1]

    @pl.when(i == 0)
    def _():
        start_loads(info, refs, own, out_targets(w, part), sem)
        wait_whole(w, sem)

    first, length = tile_length(info, i, tiles_per)
    total[...] = state[...].astype(f32) + b_out[...]

    @pl.when(first < length)
    def _():
        total[...] += dot(mixed[...], w[...])

    n, _ = normalise(total[...])
    state_one[...] = total[...].astype(bf16)
    normed[...] = (n * gain[...] + bias[...]).astype(bf16)


def mix_call(info, mixed, state, b_out, gain, bias, own, pieces, tiles_per):
    rows, d = mixed.shape
    row = pl.BlockSpec((TILE, d), lambda i, s: (i, 0))
    return pl.pallas_call(
        functools.partial(mix_kernel, tiles_per),
        grid_spec=pltpu.PrefetchScalarGridSpec(
            num_scalar_prefetch=1,
            grid=(rows // TILE,),
            in_specs=[row, row] + [whole((1, d))] * 3 + [ANY] * (1 + COUNT),
            out_specs=[row, row],
            scratch_shapes=[
                pltpu.VMEM((d, d), bf16),
                pltpu.VMEM((TILE, d), f32),
                pltpu.SemaphoreType.DMA,
            ],
        ),
        out_shape=[jax.ShapeDtypeStruct((rows, d), bf16)] * 2,
        compiler_params=params(1),
        cost_estimate=cost(2 * rows * d * d, rows * d * 12),
        name="mix_norm",
    )(info, mixed, state, b_out, gain, bias, own, *pieces)


def gelu_both(pre):
    sq = pre * pre
    t = jnp.tanh(pre * (GELU_C + GELU_C * GELU_A * sq))
    h = 0.5 + 0.5 * t
    a = pre * h
    return a, h + a * (1.0 - h) * (2.0 * GELU_C + 6.0 * GELU_C * GELU_A * sq)


def ffn_own_kernel(
    info, x, c, w_up, w_down, b_up, grad, acc, g_up, g_down, g_bup, g_bdown, aup, adown, act, gpre
):
    i, tiles = pl.program_id(0), pl.num_programs(0)

    @pl.when(i == 0)
    def _():
        aup[...] = jnp.zeros_like(aup)
        adown[...] = jnp.zeros_like(adown)
        g_bup[...] = jnp.zeros_like(g_bup)
        g_bdown[...] = jnp.zeros_like(g_bdown)

    xs, cs = x[...], c[...]
    a, slope = gelu_both(dot(xs, w_up[...]) + b_up[...])
    gp = dot_nt(cs, w_down[...]) * slope
    act[...] = a.astype(bf16)
    gb = gp.astype(bf16)
    gpre[...] = gb
    grad[...] = dot_nt(gb, w_up[...]).astype(bf16)
    adown[...] += dot_tn(act[...], cs)
    aup[...] += dot_tn(xs, gpre[...])
    g_bup[...] += jnp.sum(gp, axis=0, keepdims=True)
    g_bdown[...] += jnp.sum(cs.astype(f32), axis=0, keepdims=True)

    own = tiles // 4

    @pl.when((i // own) == info[0])
    def _():
        out0 = pl.multiple_of(lax.rem(i, own) * TILE, TILE)
        acc[pl.ds(out0, TILE), :] = dot(act[...], w_down[...])

    @pl.when(i == tiles - 1)
    def _():
        g_up[...] = aup[...].astype(bf16)
        g_down[...] = adown[...].astype(bf16)


def ffn_own_call(info, x, c, w_up, w_down, b_up):
    rows, d = x.shape
    hid = b_up.shape[1]
    row = pl.BlockSpec((TILE, d), lambda i, s: (i, 0))
    return pl.pallas_call(
        ffn_own_kernel,
        grid_spec=pltpu.PrefetchScalarGridSpec(
            num_scalar_prefetch=1,
            grid=(rows // TILE,),
            in_specs=[row, row, once((d, hid)), once((hid, d)), whole((1, hid))],
            out_specs=[
                row, once((rows // 4, d)), once((d, hid)), once((hid, d)), whole((1, hid)),
                whole((1, d)),
            ],
            scratch_shapes=[
                pltpu.VMEM((d, hid), f32),
                pltpu.VMEM((hid, d), f32),
                pltpu.VMEM((TILE, hid), bf16),
                pltpu.VMEM((TILE, hid), bf16),
            ],
        ),
        out_shape=[
            jax.ShapeDtypeStruct((rows, d), bf16),
            jax.ShapeDtypeStruct((rows // 4, d), f32),
            jax.ShapeDtypeStruct((d, hid), bf16),
            jax.ShapeDtypeStruct((hid, d), bf16),
            jax.ShapeDtypeStruct((1, hid), f32),
            jax.ShapeDtypeStruct((1, d), f32),
        ],
        compiler_params=params(1),
        cost_estimate=cost(rows * d * hid * 2 * 5.25, rows * d * 8),
        name="ffn_own",
    )(info, x, c, w_up, w_down, b_up)


def ffn_rest_kernel(
    tiles_per, info, x, c, b_up, state, before, acc_in, gain, b_down, out_own, *rest
):
    ffn_refs, out_refs = rest[:COUNT], rest[COUNT : 2 * COUNT]
    out, half, g_mixed, vecs, w, w_out, grad, acc, act, sems, out_sem = rest[2 * COUNT :]
    k, i = pl.program_id(0), pl.program_id(1)
    blocks, tiles = pl.num_programs(0), pl.num_programs(1)
    hid = w.shape[1] // 2
    piece = hid // GROUP
    slot = lax.rem(k, 2)

    def load(kk, where):
        for ref, m in zip(ffn_refs, PIECES):
            off = pl.multiple_of((info[1] ^ m) * piece, 16)
            for part in range(2):
                pltpu.make_async_copy(
                    ref.at[kk, pl.ds(part * piece, piece)],
                    w.at[where, pl.ds(part * hid + off, piece)],
                    sems.at[where],
                ).start()

    @pl.when((k == 0) & (i == 0))
    def _():
        load(0, 0)
        vecs[...] = jnp.zeros_like(vecs)
        first = (out_own.shape[0] // GROUP) * 2
        start_loads(info, out_refs, out_own, out_targets(w_out, first), out_sem)

    @pl.when(i == 0)
    def _():
        wait_whole(w.at[slot], sems.at[slot])

        @pl.when(k + 1 < blocks)
        def _():
            load(k + 1, 1 - slot)

    @pl.when((k == blocks - 1) & (i == 0))
    def _():
        wait_whole(w_out, out_sem)

    row0 = pl.multiple_of(i * TILE, TILE)
    xs = x[pl.ds(row0, TILE), :]
    cs = c[pl.ds(row0, TILE), :]
    src_t = (info[0] + 3 - k) & 3
    a, slope = gelu_both(dot_nt(xs, w[slot, :hid]) + b_up[pl.ds(src_t, 1), :])
    gb = (dot_nt(cs, w[slot, hid:]) * slope).astype(bf16)
    act[...] = a.astype(bf16)
    part = dot(gb, w[slot, :hid])

    @pl.when(k == 0)
    def _():
        grad[pl.ds(row0, TILE), :] = before[...].astype(f32) + part

    @pl.when((k > 0) & (k < blocks - 1))
    def _():
        grad[pl.ds(row0, TILE), :] += part

    own = tiles // 4
    mine = (i // own) == info[0]
    out0 = pl.multiple_of(lax.rem(i, own) * TILE, TILE)

    @pl.when(mine & (k == 0))
    def _():
        acc[pl.ds(out0, TILE), :] = acc_in[pl.ds(out0, TILE), :] + dot(act[...], w[slot, hid:])

    @pl.when(mine & (k > 0))
    def _():
        acc[pl.ds(out0, TILE), :] += dot(act[...], w[slot, hid:])

    @pl.when(k == blocks - 1)
    def _():
        g2 = grad[pl.ds(row0, TILE), :] + part
        s1 = state[...].astype(f32)
        n, r = normalise(s1)
        g1 = cs.astype(f32) + norm_back(g2, n, r, gain[...])
        half[...] = g1.astype(bf16)
        vecs[0:1, :] += jnp.sum(g2 * n, axis=0, keepdims=True)
        vecs[1:2, :] += jnp.sum(g2, axis=0, keepdims=True)
        vecs[2:3, :] += jnp.sum(g1, axis=0, keepdims=True)

        first, length = tile_length(info, i, tiles_per)

        @pl.when(first < length)
        def _():
            pos = lax.broadcasted_iota(jnp.int32, (TILE, 1), 0) + first
            g_mixed[...] = jnp.where(
                pos < length, dot_nt(half[...], w_out[...]), 0.0
            ).astype(bf16)

        @pl.when(mine)
        def _():
            out[pl.ds(out0, TILE), :] = (
                s1 + acc[pl.ds(out0, TILE), :] + b_down[...]
            ).astype(bf16)


def ffn_rest_call(
    info, x, c, b_up, state, before, acc, gain, b_down, out_own, out_pieces, pieces, tiles_per
):
    rows, d = x.shape
    hid = b_up.shape[1]
    tiles = rows // TILE
    last = pl.BlockSpec((TILE, d), lambda k, i, s: (jnp.where(k == 2, i, 0), 0))
    early = pl.BlockSpec((TILE, d), lambda k, i, s: (jnp.where(k == 0, i, tiles - 1), 0))
    return pl.pallas_call(
        functools.partial(ffn_rest_kernel, tiles_per),
        grid_spec=pltpu.PrefetchScalarGridSpec(
            num_scalar_prefetch=1,
            grid=(3, tiles),
            in_specs=[
                once((rows, d)), once((rows, d)), whole((4, hid)), last, early,
                once((rows // 4, d)), whole((1, d)), whole((1, d)), ANY,
            ]
            + [ANY] * (2 * COUNT),
            out_specs=[once((rows // 4, d)), last, last, whole((8, d))],
            scratch_shapes=[
                pltpu.VMEM((2, 2 * hid, d), bf16),
                pltpu.VMEM((d, d), bf16),
                pltpu.VMEM((rows, d), f32),
                pltpu.VMEM((rows // 4, d), f32),
                pltpu.VMEM((TILE, hid), bf16),
                pltpu.SemaphoreType.DMA((2,)),
                pltpu.SemaphoreType.DMA,
            ],
        ),
        out_shape=[
            jax.ShapeDtypeStruct((rows // 4, d), bf16),
            jax.ShapeDtypeStruct((rows, d), bf16),
            jax.ShapeDtypeStruct((rows, d), bf16),
            jax.ShapeDtypeStruct((8, d), f32),
        ],
        compiler_params=params(2),
        cost_estimate=cost(rows * d * hid * 2 * 11, rows * d * 20),
        name="ffn_rest",
    )(info, x, c, b_up, state, before, acc, gain, b_down, out_own, *pieces, *out_pieces)


def norm_one_kernel(tiles_per, info, dq, dk, dv, state, gs, gain, *rest):
    own, refs, (half, vecs, w, grad, sem) = rest[0], rest[1 : 1 + COUNT], rest[1 + COUNT :]
    i = pl.program_id(0)
    d = dq.shape[1]

    @pl.when(i == 0)
    def _():
        start_loads(info, refs, own, qkv_targets(w), sem)
        vecs[...] = jnp.zeros_like(vecs)
        wait_whole(w, sem)

    first, length = tile_length(info, i, tiles_per)

    @pl.when(first < length)
    def _():
        grad[...] = (
            dot(dq[...], w[:d]) + dot(dk[...], w[d : 2 * d]) + dot(dv[...], w[2 * d :])
        )
        n, r = normalise(state[...].astype(f32))
        g1 = grad[...]
        g0 = gs[...].astype(f32) + norm_back(g1, n, r, gain[...])
        half[...] = g0.astype(bf16)
        vecs[0:1, :] += jnp.sum(g1 * n, axis=0, keepdims=True)
        vecs[1:2, :] += jnp.sum(g1, axis=0, keepdims=True)
        vecs[2:3, :] += jnp.sum(g0, axis=0, keepdims=True)

    @pl.when(first >= length)
    def _():
        half[...] = gs[...]
        vecs[2:3, :] += jnp.sum(gs[...].astype(f32), axis=0, keepdims=True)


def norm_one_call(info, dq, dk, dv, state, gs, gain, own, pieces, tiles_per):
    rows, d = dq.shape
    row = pl.BlockSpec((TILE, d), lambda i, s: (i, 0))
    return pl.pallas_call(
        functools.partial(norm_one_kernel, tiles_per),
        grid_spec=pltpu.PrefetchScalarGridSpec(
            num_scalar_prefetch=1,
            grid=(rows // TILE,),
            in_specs=[row] * 5 + [whole((1, d))] + [ANY] * (1 + COUNT),
            out_specs=[row, whole((8, d))],
            scratch_shapes=[
                pltpu.VMEM((3 * d, d), bf16),
                pltpu.VMEM((TILE, d), f32),
                pltpu.SemaphoreType.DMA,
            ],
        ),
        out_shape=[jax.ShapeDtypeStruct((rows, d), bf16), jax.ShapeDtypeStruct((8, d), f32)],
        compiler_params=params(1),
        cost_estimate=cost(6 * rows * d * d, rows * d * 16),
        name="norm_one_back",
    )(info, dq, dk, dv, state, gs, gain, own, *pieces)


def joined_kernel(info, half, o0, o1, o2, o3, *rest):
    own, refs = rest[0], rest[1 : 1 + COUNT]
    g_hid, g_skp, out, w, sem = rest[1 + COUNT :]
    d = half.shape[1]
    i = pl.program_id(0)

    @pl.when(i == 0)
    def _():
        start_loads(info, refs, own, skip_targets(w), sem)
        wait_whole(w, sem)

    h = half[...]
    g_hid[...] = dot_nt(h, w[:d]).astype(bf16)
    g_skp[...] = dot_nt(h, w[d:]).astype(bf16)
    source = (info[0] + 4 - i // (pl.num_programs(0) // 4)) & 3
    for k, ref in enumerate((o0, o1, o2, o3)):

        @pl.when(source == k)
        def _(ref=ref):
            out[...] = ref[...]


def joined_call(info, half, parts, own, pieces):
    rows, d = half.shape
    row = pl.BlockSpec((TILE, d), lambda i, s: (i, 0))
    per = rows // TILE // 4

    def part_spec(k):
        def index(i, s):
            at = i - ((s[0] + 4 - k) & 3) * per
            return jnp.clip(at, 0, per - 1), 0

        return pl.BlockSpec((TILE, d), index)

    return pl.pallas_call(
        joined_kernel,
        grid_spec=pltpu.PrefetchScalarGridSpec(
            num_scalar_prefetch=1,
            grid=(rows // TILE,),
            in_specs=[row] + [part_spec(k) for k in range(4)] + [ANY] * (1 + COUNT),
            out_specs=[row] * 3,
            scratch_shapes=[pltpu.VMEM((2 * d, d), bf16), pltpu.SemaphoreType.DMA],
        ),
        out_shape=[jax.ShapeDtypeStruct((rows, d), bf16)] * 3,
        compiler_params=params(1),
        cost_estimate=cost(4 * rows * d * d, rows * d * 6),
        name="joined_back",
    )(info, half, *parts, own, *pieces)


def outer(a, b):
    return lax.dot_general(a, b, TN, preferred_element_type=f32).astype(bf16)


def total_over_batch(x):
    n = lax.axis_size("batch")
    if n != GROUP:
        return lax.psum(x, "batch")
    me = lax.axis_index("batch")

    def part(array, index):
        return lax.dynamic_index_in_dim(array, index, 0, keepdims=False)

    total = part(x, me).astype(f32)
    for m in range(1, GROUP):
        total = total + across(part(x, me ^ m), m).astype(f32)
    total = total.astype(bf16)
    sums = jnp.stack([total] + [across(total, m) for m in range(1, GROUP)])
    return jnp.stack([part(sums, me ^ p) for p in range(GROUP)])


def outer(a, b):
    return lax.dot_general(a, b, TN, preferred_element_type=f32).astype(bf16)


def body(
    hidden_in,
    skip_state,
    lengths,
    w_skip,
    b_skip,
    norm1_gain,
    norm1_bias,
    w_qkv,
    b_qv,
    w_out,
    b_out,
    norm2_gain,
    norm2_bias,
    w_up,
    b_up,
    w_down,
    b_down,
    cotangent,
):
    tensor = lax.axis_index("tensor")
    member = lax.rem(lax.axis_index("batch"), GROUP)
    info = jnp.concatenate([jnp.stack([tensor, member]).astype(jnp.int32), lengths])
    rows, d = hidden_in.shape
    seq = rows // lengths.shape[0]
    tiles_per = seq // TILE
    columns = w_out.shape[0]

    def share(array, axis=0):
        size = array.shape[axis] // GROUP
        return lax.dynamic_slice_in_dim(array, member * size, size, axis)

    biases = jnp.concatenate([b_qv.reshape(-1), b_up])
    b_hi = biases.astype(bf16)
    b_mid = (biases - b_hi.astype(f32)).astype(bf16)
    b_low = (biases - b_hi.astype(f32) - b_mid.astype(f32)).astype(bf16)
    b_rows = jnp.concatenate([b_hi, b_mid, b_low])
    b_rows = jnp.pad(b_rows, (0, 16 * d - b_rows.size)).reshape(16, d)

    qkv_own = jnp.swapaxes(w_qkv, 1, 2)
    first_piece = jnp.concatenate([share(w_skip), share(w_out)], 0)
    qkv_piece = share(qkv_own, 1).reshape(-1, d)
    qkv_rows = qkv_piece.shape[0]
    qkv_piece = jnp.concatenate([qkv_piece, b_rows], 0)
    qkv_own = qkv_own.reshape(-1, d)
    up_piece = jnp.swapaxes(share(w_up, 1), 0, 1)
    ffn_piece = jnp.concatenate([up_piece, share(w_down)], 0)

    first_z = jnp.stack([along(first_piece, k) for k in (1, 2, 3)])
    qkv_z = [along(after(qkv_piece, first_z), k) for k in (1, 2, 3)]
    first_chips = from_chips(first_z)
    terms = jnp.stack([b_rows] + [x[qkv_rows:] for x in qkv_z]).reshape(4, -1).astype(f32)
    size = biases.size
    relative = terms[:, :size] + terms[:, size : 2 * size] + terms[:, 2 * size : 3 * size]
    all_biases = jnp.stack([relative[(tensor - j) & 3] for j in range(4)])
    b_q = all_biases[:, :columns].reshape(1, d)
    b_v = all_biases[:, columns : 2 * columns].reshape(1, d)
    b_up_all = all_biases[:, 2 * columns :]
    qkv_z = jnp.stack([x[:qkv_rows] for x in qkv_z])
    first_all = from_cores(first_chips)
    qkv_chips = from_chips(after(qkv_z, *first_chips))
    ffn_piece = after(ffn_piece, qkv_z)
    ffn_z = [along(ffn_piece, k) for k in (1, 2, 3)]
    def line(v):
        return v[None, :]

    state_zero, normed_one = skip_call(
        info, hidden_in, skip_state, line(b_skip), line(norm1_gain), line(norm1_bias),
        w_skip, first_all,
    )
    qkv_all = from_cores(list(lax.optimization_barrier((tuple(qkv_chips), normed_one))[0]))
    q, k, v = qkv_call(info, normed_one, b_q, b_v, qkv_own, qkv_all, tiles_per)
    ffn_z = jnp.stack(ffn_z)
    ffn_chips = from_chips(after(ffn_z, q))
    mixed, lse = attend_call(info, q, k, v, seq)
    lse = lse[:, :HEADS].T
    state_one, normed_two = mix_call(
        info, mixed, state_zero, line(b_out), line(norm2_gain), line(norm2_bias), w_out, first_all,
        tiles_per,
    )
    before, acc, g_up, g_down, g_bup, g_bdown = ffn_own_call(
        info, normed_two, cotangent, w_up, w_down, line(b_up)
    )
    ffn_all = from_cores(list(lax.optimization_barrier((tuple(ffn_chips), before))[0]))
    out_rows, half_one, grad_mixed, vecs_two = ffn_rest_call(
        info, normed_two, cotangent, b_up_all, state_one, before, acc, line(norm2_gain),
        line(b_down), w_out, first_all, ffn_all, tiles_per,
    )
    out_parts = [out_rows] + [along(out_rows, k) for k in (1, 2, 3)]
    g_up, g_down = lax.psum((g_up, g_down), "batch")

    first_col = tensor * columns

    def own(array):
        return lax.dynamic_slice_in_dim(array, first_col, columns, 1)

    g_out = outer(own(mixed), half_one)
    dq, dk, dv = attend_back_call(info, q, k, v, grad_mixed, mixed, lse, seq)
    half_zero, vecs_one = norm_one_call(
        info, dq, dk, dv, state_zero, half_one, line(norm1_gain), qkv_own, qkv_all, tiles_per
    )
    g_qkv = jnp.stack([outer(normed_one, own(x)) for x in (dq, dk, dv)])
    shard = w_skip.shape[0]
    joined = jnp.concatenate([hidden_in, skip_state], axis=1)
    features = lax.dynamic_slice_in_dim(joined, tensor * shard, shard, 1)
    g_skip = outer(features, half_zero)
    g_bqv = jnp.stack([jnp.sum(own(x), axis=0, dtype=f32) for x in (dq, dv)]).reshape(1, -1)
    g_bqv = jnp.pad(g_bqv, ((0, 0), (0, d - g_bqv.shape[1])))
    vectors = jnp.concatenate(
        [vecs_two[:3], g_bdown, vecs_one[:3], g_bqv, g_bup.reshape(-1, d)], axis=0
    )
    vectors = jnp.pad(vectors, ((0, 2 * GROUP - vectors.shape[0]), (0, 0))).astype(bf16)
    tied = lax.optimization_barrier((g_qkv, g_out, g_up, g_down))
    g_qkv, g_out = lax.psum((tied[0], tied[1]), "batch")
    g_up, g_down = tied[2], tied[3]
    last = jnp.concatenate([g_skip.reshape(GROUP, -1, d), vectors.reshape(GROUP, 2, d)], axis=1)
    last = total_over_batch(last).astype(f32)
    g_skip = last[:, :-2].reshape(-1, d)
    vectors = last[:, -2:].reshape(-1, d)
    grad_hidden, grad_skip, output = joined_call(info, half_zero, out_parts, w_skip, first_all)
    return (
        output,
        grad_hidden,
        grad_skip,
        g_skip,
        vectors[6],
        vectors[4],
        vectors[5],
        g_qkv.astype(f32),
        vectors[7, : 2 * columns].reshape(2, columns),
        g_out.astype(f32),
        vectors[2],
        vectors[0],
        vectors[1],
        g_up.astype(f32),
        vectors[8 : 8 + g_bup.size // d].reshape(-1),
        g_down.astype(f32),
        vectors[3],
    )


def solution(mesh):
    placed = (
        P("batch", None),
        P("batch", None),
        P("batch"),
        P("tensor", None),
        P(),
        P(),
        P(),
        P(None, None, "tensor"),
        P(None, "tensor"),
        P("tensor", None),
        P(),
        P(),
        P(),
        P(None, "tensor"),
        P("tensor"),
        P("tensor", None),
        P(),
        P("batch", None),
    )
    return jax.shard_map(
        body,
        mesh=mesh,
        in_specs=placed,
        out_specs=(
            P("batch", None),
            P("batch", None),
            P("batch", None),
            P("tensor", None),
            P(),
            P(),
            P(),
            P(None, None, "tensor"),
            P(None, "tensor"),
            P("tensor", None),
            P(),
            P(),
            P(),
            P(None, "tensor"),
            P("tensor"),
            P("tensor", None),
            P(),
        ),
        check_vma=False,
    )
```

```python
import functools

import jax
import jax.numpy as jnp
from jax import lax
from jax.experimental import pallas as pl
from jax.experimental.pallas import tpu as pltpu
from jax.sharding import PartitionSpec as P

HEADS = 16
HEAD_DIM = 64
GROUP = 8
TILE = 256
FFN_TILE = 512
LOG2E = 1.4426950408889634
LN2 = 0.6931471805599453
GELU_C = 0.7978845608028654
GELU_A = 0.044715

norm_eps = 1e-05
masked_score = -1e30
bf16 = jnp.bfloat16
f32 = jnp.float32

NT = (((1,), (1,)), ((), ()))
TN = (((0,), (0,)), ((), ()))

PIECES = [0, 2, 4, 6, 1, 3, 5, 7]
COUNT = len(PIECES)


def dot(a, b):
    return jnp.dot(a, b, preferred_element_type=f32)


def dot_nt(a, b):
    return lax.dot_general(a, b, NT, preferred_element_type=f32)


def dot_tn(a, b):
    return lax.dot_general(a, b, TN, preferred_element_type=f32)


def params(ndim, mib=60):
    return pltpu.CompilerParams(
        vmem_limit_bytes=mib * 1024 * 1024, dimension_semantics=("arbitrary",) * ndim
    )


def cost(flops, moved):
    return pl.CostEstimate(
        flops=int(flops) // 10, bytes_accessed=int(moved) // 10, transcendentals=0
    )


def along(x, k):
    n = lax.axis_size("tensor")
    return lax.ppermute(x, "tensor", [(i, (i + k) % n) for i in range(n)])


def across(x, m):
    n = lax.axis_size("batch")
    return lax.ppermute(x, "batch", [(i, i ^ m) for i in range(n)])


def from_chips(held):
    return [held, across(held, 2), across(held, 4), across(held, 6)]


def from_cores(held):
    return held + [across(x, 1) for x in held]


def after(x, *earlier):
    return lax.optimization_barrier((x,) + earlier)[0]


def start_loads(info, refs, own, targets, sem):
    for first, rows, own_first, dest, place in targets:
        off = pl.multiple_of(place(info[0], 0), 16)
        pltpu.make_async_copy(
            own.at[pl.ds(own_first, rows * GROUP)], dest.at[pl.ds(off, rows * GROUP)], sem
        ).start()
    for ref, m in zip(refs, PIECES):
        for kk in range(3):
            src_t = (info[0] + 3 - kk) & 3
            src_b = info[1] ^ m
            for first, rows, _, dest, place in targets:
                off = pl.multiple_of(place(src_t, src_b), 16)
                pltpu.make_async_copy(
                    ref.at[kk, pl.ds(first, rows)], dest.at[pl.ds(off, rows)], sem
                ).start()


def wait_whole(dest, sem):
    pltpu.make_async_copy(dest, dest, sem).wait()


ANY = pl.BlockSpec(memory_space=pltpu.HBM)


def whole(shape):
    return pl.BlockSpec(shape, lambda *_: (0,) * len(shape))


def once(shape):
    return pl.BlockSpec(shape, lambda *_: (0,) * len(shape), pipeline_mode=pl.Buffered(1))


def normalise(v):
    mean = jnp.mean(v, axis=-1, keepdims=True)
    centred = v - mean
    r = lax.rsqrt(jnp.mean(centred * centred, axis=-1, keepdims=True) + norm_eps)
    return centred * r, r


def norm_back(grad, n, r, gain):
    e = grad * gain
    return r * (
        e
        - jnp.mean(e, axis=-1, keepdims=True)
        - n * jnp.mean(e * n, axis=-1, keepdims=True)
    )


def tile_length(info, i, tiles_per, tile=TILE):
    u = i // tiles_per
    return (i - u * tiles_per) * tile, info[2 + u]


def skip_targets(w):
    shard = w.shape[0] // 4
    piece = shard // GROUP
    return [(0, piece, 0, w, lambda t, b: t * shard + b * piece)]


def out_targets(w, first):
    shard = w.shape[0] // 4
    piece = shard // GROUP
    return [(first, piece, 0, w, lambda t, b: t * shard + b * piece)]


def skip_kernel(info, hid, skp, b_skip, gain, bias, *rest):
    own, refs, (state, normed, w, sem) = rest[0], rest[1 : 1 + COUNT], rest[1 + COUNT :]

    @pl.when(pl.program_id(0) == 0)
    def _():
        start_loads(info, refs, own, skip_targets(w), sem)
        wait_whole(w, sem)

    width = hid.shape[1]
    total = dot(hid[...], w[:width]) + dot(skp[...], w[width:]) + b_skip[...]
    state[...] = total.astype(bf16)
    n, _ = normalise(total)
    normed[...] = (n * gain[...] + bias[...]).astype(bf16)


def skip_call(info, hid, skp, b_skip, gain, bias, own, pieces):
    rows, d = hid.shape
    row = pl.BlockSpec((TILE, d), lambda i, s: (i, 0))
    return pl.pallas_call(
        skip_kernel,
        grid_spec=pltpu.PrefetchScalarGridSpec(
            num_scalar_prefetch=1,
            grid=(rows // TILE,),
            in_specs=[row, row, whole((1, d)), whole((1, d)), whole((1, d))] + [ANY] * (1 + COUNT),
            out_specs=[row, row],
            scratch_shapes=[pltpu.VMEM((2 * d, d), bf16), pltpu.SemaphoreType.DMA],
        ),
        out_shape=[jax.ShapeDtypeStruct((rows, d), bf16)] * 2,
        compiler_params=params(1),
        cost_estimate=cost(4 * rows * d * d, rows * d * 10 + 4 * d * d),
        name="skip_norm",
    )(info, hid, skp, b_skip, gain, bias, own, *pieces)


def qkv_targets(w):
    d = w.shape[0] // 3
    shard = d // 4
    part = shard // GROUP
    return [
        (s * part, part, s * shard, w, lambda t, b, s=s: s * d + t * shard + b * part)
        for s in range(3)
    ]


def qkv_kernel(tiles_per, info, x, b_q, b_v, *rest):
    own, refs, (q, k, v, w, sem) = rest[0], rest[1 : 1 + COUNT], rest[1 + COUNT :]
    i = pl.program_id(0)
    d = x.shape[1]

    @pl.when(i == 0)
    def _():
        start_loads(info, refs, own, qkv_targets(w), sem)
        wait_whole(w, sem)

    first, length = tile_length(info, i, tiles_per)

    @pl.when(first < length)
    def _():
        xs = x[...]
        q[...] = ((dot_nt(xs, w[:d]) + b_q[...]) * (LOG2E * HEAD_DIM**-0.5)).astype(bf16)
        k[...] = dot_nt(xs, w[d : 2 * d]).astype(bf16)
        v[...] = (dot_nt(xs, w[2 * d :]) + b_v[...]).astype(bf16)


def qkv_call(info, x, b_q, b_v, own, pieces, tiles_per):
    rows, d = x.shape
    row = pl.BlockSpec((TILE, d), lambda i, s: (i, 0))
    return pl.pallas_call(
        functools.partial(qkv_kernel, tiles_per),
        grid_spec=pltpu.PrefetchScalarGridSpec(
            num_scalar_prefetch=1,
            grid=(rows // TILE,),
            in_specs=[row, whole((1, d)), whole((1, d))] + [ANY] * (1 + COUNT),
            out_specs=[row] * 3,
            scratch_shapes=[pltpu.VMEM((3 * d, d), bf16), pltpu.SemaphoreType.DMA],
        ),
        out_shape=[jax.ShapeDtypeStruct((rows, d), bf16)] * 3,
        compiler_params=params(1),
        cost_estimate=cost(4 * rows * d * d, rows * d * 8 + 6 * d * d),
        name="qkv",
    )(info, x, b_q, b_v, own, *pieces)


def slope2(head):
    return jnp.exp2(jnp.full((1, 1), -8.0 / HEADS, f32) * (head + 1).astype(f32)) * LOG2E


def attend_kernel(info, q, k, v, mixed, lse, dist):
    u, hp = pl.program_id(0), pl.program_id(1)
    seq = q.shape[0]
    tiles = seq // TILE
    length = info[2 + u]

    @pl.when((u == 0) & (hp == 0))
    def _():
        r = lax.broadcasted_iota(jnp.int32, dist.shape, 0)
        c = lax.broadcasted_iota(jnp.int32, dist.shape, 1)
        dist[...] = jnp.abs(r - c + (seq - TILE)).astype(f32)

    lane = lax.broadcasted_iota(jnp.int32, (TILE, 128), 1)
    used = (length + TILE - 1) // TILE

    for n in range(1, tiles + 1):

        @pl.when(used == n)
        def _(n=n):
            cols = n * TILE
            valid = (
                lax.broadcasted_iota(jnp.int32, (TILE, TILE), 1) + (cols - TILE) < length
            )

            def step(i, carry):
                row0 = pl.multiple_of(i * TILE, TILE)
                qs = q[pl.ds(row0, TILE), :]
                start = pl.multiple_of((seq - TILE) - row0, TILE)
                gap = dist[:, pl.ds(start, cols)]
                outs, sums, ss = [], [], []
                for a in range(2):
                    qa = jnp.where((lane < 64) == (a == 0), qs, jnp.zeros_like(qs))
                    ss.append(dot_nt(qa, k[:cols, :]))
                for a in range(2):
                    s = ss[a] - slope2(2 * hp + a) * gap
                    last = jnp.where(valid, s[:, cols - TILE :], masked_score)
                    s = jnp.concatenate([s[:, : cols - TILE], last], axis=1) if n > 1 else last
                    m = jnp.max(s, axis=1, keepdims=True)
                    p = jnp.exp2(s - m)
                    total = jnp.sum(p, axis=1, keepdims=True)
                    ss[a] = (p.astype(bf16), m, total)
                for a in range(2):
                    p, m, total = ss[a]
                    outs.append(dot(p, v[:cols, :]) * (1.0 / total))
                    sums.append(m + jnp.log2(total))
                o = jnp.where(lane < 64, outs[0], outs[1])
                pos = lax.broadcasted_iota(jnp.int32, (TILE, 128), 0) + row0
                mixed[pl.ds(row0, TILE), :] = jnp.where(pos < length, o, 0.0).astype(bf16)
                old = lse[pl.ds(row0, TILE), :]
                new = jnp.where(lane == 2 * hp, sums[0], old)
                lse[pl.ds(row0, TILE), :] = jnp.where(lane == 2 * hp + 1, sums[1], new)
                return carry

            lax.fori_loop(0, n, step, 0, unroll=True)
            if n < tiles:
                mixed[cols:, :] = jnp.zeros((seq - cols, 128), bf16)


def attend_call(info, q, k, v, seq):
    rows, d = q.shape
    utts = rows // seq
    blk = pl.BlockSpec((seq, 128), lambda u, h, s: (u, h))
    return pl.pallas_call(
        attend_kernel,
        grid_spec=pltpu.PrefetchScalarGridSpec(
            num_scalar_prefetch=1,
            grid=(utts, d // 128),
            in_specs=[blk] * 3,
            out_specs=[blk, pl.BlockSpec((seq, 128), lambda u, h, s: (u, 0))],
            scratch_shapes=[pltpu.VMEM((TILE, 2 * seq - TILE), f32)],
        ),
        out_shape=[
            jax.ShapeDtypeStruct((rows, d), bf16),
            jax.ShapeDtypeStruct((rows, 128), f32),
        ],
        compiler_params=params(2),
        cost_estimate=cost(rows * seq * d * 4, rows * d * 8),
        name="attend",
    )(info, q, k, v)


def attend_back_kernel(info, q, k, v, g, o, lse, dq, dk, dv, dist, akey, aval):
    u, hp = pl.program_id(0), pl.program_id(1)
    seq = q.shape[0]
    tiles = seq // TILE
    length = info[2 + u]

    @pl.when((u == 0) & (hp == 0))
    def _():
        r = lax.broadcasted_iota(jnp.int32, dist.shape, 0)
        c = lax.broadcasted_iota(jnp.int32, dist.shape, 1)
        dist[...] = jnp.abs(r - c - (seq - TILE)).astype(f32)

    lane = lax.broadcasted_iota(jnp.int32, (TILE, 128), 1)
    used = (length + TILE - 1) // TILE

    for n in range(1, tiles + 1):

        @pl.when(used == n)
        def _(n=n):
            cols = n * TILE
            valid = (
                lax.broadcasted_iota(jnp.int32, (TILE, TILE), 0) + (cols - TILE) < length
            )
            akey[:cols, :] = jnp.zeros((cols, 128), f32)
            aval[:cols, :] = jnp.zeros((cols, 128), f32)
            klane = lax.broadcasted_iota(jnp.int32, (cols, 128), 1)

            def step(i, carry):
                row0 = pl.multiple_of(i * TILE, TILE)
                qs = q[pl.ds(row0, TILE), :]
                gs = g[pl.ds(row0, TILE), :]
                start = pl.multiple_of((seq - TILE) - row0, TILE)
                gap = dist[pl.ds(start, cols), :]
                both = gs.astype(f32) * o[pl.ds(row0, TILE), :].astype(f32)
                hi = both.astype(bf16)
                lo = (both - hi.astype(f32)).astype(bf16)
                grads, held = [], []
                for a in range(2):
                    mine = (lane < 64) == (a == 0)
                    qa = jnp.where(mine, qs, jnp.zeros_like(qs))
                    ga = jnp.where(mine, gs, jnp.zeros_like(gs))
                    pick = jnp.where(
                        (lax.broadcasted_iota(jnp.int32, (8, 128), 1) < 64) == (a == 0), 1.0, 0.0
                    ).astype(bf16)
                    delta = (dot_nt(pick, hi) + dot_nt(pick, lo))[:1, :]
                    held.append((qa, ga, delta, dot_nt(k[:cols, :], qa), dot_nt(v[:cols, :], ga)))
                for a in range(2):
                    qa, ga, delta, s, gw = held[a]
                    row = lse[pl.ds(2 * hp + a, 1), pl.ds(row0, TILE)]
                    s = s - (slope2(2 * hp + a) * gap + row)
                    last = jnp.where(valid, s[cols - TILE :, :], masked_score)
                    s = jnp.concatenate([s[: cols - TILE, :], last], axis=0) if n > 1 else last
                    p = jnp.exp2(s)
                    ds = (p * (gw - delta)).astype(bf16)
                    held[a] = (qa, ga, p.astype(bf16), ds)
                aval[:cols, :] += dot(held[0][2], held[0][1]) + dot(held[1][2], held[1][1])
                akey[:cols, :] += dot(held[0][3], held[0][0]) + dot(held[1][3], held[1][0])
                for a in range(2):
                    ka = k[:cols, :]
                    ka = jnp.where((klane < 64) == (a == 0), ka, jnp.zeros_like(ka))
                    grads.append(dot_tn(held[a][3], ka))
                dq[pl.ds(row0, TILE), :] = ((grads[0] + grads[1]) * HEAD_DIM**-0.5).astype(bf16)
                return carry

            lax.fori_loop(0, n, step, 0, unroll=True)
            dk[:cols, :] = (akey[:cols, :] * LN2).astype(bf16)
            dv[:cols, :] = aval[:cols, :].astype(bf16)
            if n < tiles:
                for ref in (dq, dk, dv):
                    ref[cols:, :] = jnp.zeros((seq - cols, 128), bf16)


def attend_back_call(info, q, k, v, g, o, lse, seq):
    rows, d = q.shape
    utts = rows // seq
    blk = pl.BlockSpec((seq, 128), lambda u, h, s: (u, h))
    return pl.pallas_call(
        attend_back_kernel,
        grid_spec=pltpu.PrefetchScalarGridSpec(
            num_scalar_prefetch=1,
            grid=(utts, d // 128),
            in_specs=[blk] * 5 + [pl.BlockSpec((HEADS, seq), lambda u, h, s: (0, u))],
            out_specs=[blk] * 3,
            scratch_shapes=[
                pltpu.VMEM((2 * seq - TILE, TILE), f32),
                pltpu.VMEM((seq, 128), f32),
                pltpu.VMEM((seq, 128), f32),
            ],
        ),
        out_shape=[jax.ShapeDtypeStruct((rows, d), bf16)] * 3,
        compiler_params=params(2),
        cost_estimate=cost(rows * seq * d * 10, rows * d * 16),
        name="attend_back",
    )(info, q, k, v, g, o, lse)


def mix_kernel(tiles_per, info, mixed, state, b_out, gain, bias, *rest):
    own, refs, (state_one, normed, w, total, sem) = rest[0], rest[1 : 1 + COUNT], rest[1 + COUNT :]
    part = (own.shape[0] // GROUP) * 2
    i = pl.program_id(0)
    d = mixed.shape[1]

    @pl.when(i == 0)
    def _():
        start_loads(info, refs, own, out_targets(w, part), sem)
        wait_whole(w, sem)

    first, length = tile_length(info, i, tiles_per)
    total[...] = state[...].astype(f32) + b_out[...]

    @pl.when(first < length)
    def _():
        total[...] += dot(mixed[...], w[...])

    n, _ = normalise(total[...])
    state_one[...] = total[...].astype(bf16)
    normed[...] = (n * gain[...] + bias[...]).astype(bf16)


def mix_call(info, mixed, state, b_out, gain, bias, own, pieces, tiles_per):
    rows, d = mixed.shape
    row = pl.BlockSpec((TILE, d), lambda i, s: (i, 0))
    return pl.pallas_call(
        functools.partial(mix_kernel, tiles_per),
        grid_spec=pltpu.PrefetchScalarGridSpec(
            num_scalar_prefetch=1,
            grid=(rows // TILE,),
            in_specs=[row, row] + [whole((1, d))] * 3 + [ANY] * (1 + COUNT),
            out_specs=[row, row],
            scratch_shapes=[
                pltpu.VMEM((d, d), bf16),
                pltpu.VMEM((TILE, d), f32),
                pltpu.SemaphoreType.DMA,
            ],
        ),
        out_shape=[jax.ShapeDtypeStruct((rows, d), bf16)] * 2,
        compiler_params=params(1),
        cost_estimate=cost(2 * rows * d * d, rows * d * 12),
        name="mix_norm",
    )(info, mixed, state, b_out, gain, bias, own, *pieces)


def gelu_both(pre):
    sq = pre * pre
    t = jnp.tanh(pre * (GELU_C + GELU_C * GELU_A * sq))
    h = 0.5 + 0.5 * t
    a = pre * h
    return a, h + a * (1.0 - h) * (2.0 * GELU_C + 6.0 * GELU_C * GELU_A * sq)


def ffn_own_kernel(
    info, x, c, w_up, w_down, b_up, grad, acc, g_up, g_down, g_bup, g_bdown, aup, adown, act, gpre
):
    i, tiles = pl.program_id(0), pl.num_programs(0)

    @pl.when(i == 0)
    def _():
        aup[...] = jnp.zeros_like(aup)
        adown[...] = jnp.zeros_like(adown)
        g_bup[...] = jnp.zeros_like(g_bup)
        g_bdown[...] = jnp.zeros_like(g_bdown)

    xs, cs = x[...], c[...]
    cut = w_down.shape[0] // 2
    pre = [dot(xs, w_up[:, h * cut : (h + 1) * cut]) for h in range(2)]
    gact = [dot_nt(cs, w_down[h * cut : (h + 1) * cut]) for h in range(2)]
    for h in range(2):
        at = slice(h * cut, (h + 1) * cut)
        a, slope = gelu_both(pre[h] + b_up[:, at])
        gp = gact[h] * slope
        act[:, at] = a.astype(bf16)
        gpre[:, at] = gp.astype(bf16)
        g_bup[:, at] += jnp.sum(gp, axis=0, keepdims=True)
        adown[at, :] += dot_tn(act[:, at], cs)
        aup[:, at] += dot_tn(xs, gpre[:, at])
    grad[...] = dot_nt(gpre[...], w_up[...]).astype(bf16)
    g_bdown[...] += jnp.sum(cs.astype(f32), axis=0, keepdims=True)

    own = tiles // 4

    @pl.when((i // own) == info[0])
    def _():
        out0 = pl.multiple_of(lax.rem(i, own) * FFN_TILE, FFN_TILE)
        acc[pl.ds(out0, FFN_TILE), :] = dot(act[...], w_down[...])

    @pl.when(i == tiles - 1)
    def _():
        g_up[...] = aup[...].astype(bf16)
        g_down[...] = adown[...].astype(bf16)


def ffn_own_call(info, x, c, w_up, w_down, b_up):
    rows, d = x.shape
    hid = b_up.shape[1]
    row = pl.BlockSpec((FFN_TILE, d), lambda i, s: (i, 0))
    return pl.pallas_call(
        ffn_own_kernel,
        grid_spec=pltpu.PrefetchScalarGridSpec(
            num_scalar_prefetch=1,
            grid=(rows // FFN_TILE,),
            in_specs=[row, row, once((d, hid)), once((hid, d)), whole((1, hid))],
            out_specs=[
                row, once((rows // 4, d)), once((d, hid)), once((hid, d)), whole((1, hid)),
                whole((1, d)),
            ],
            scratch_shapes=[
                pltpu.VMEM((d, hid), f32),
                pltpu.VMEM((hid, d), f32),
                pltpu.VMEM((FFN_TILE, hid), bf16),
                pltpu.VMEM((FFN_TILE, hid), bf16),
            ],
        ),
        out_shape=[
            jax.ShapeDtypeStruct((rows, d), bf16),
            jax.ShapeDtypeStruct((rows // 4, d), f32),
            jax.ShapeDtypeStruct((d, hid), bf16),
            jax.ShapeDtypeStruct((hid, d), bf16),
            jax.ShapeDtypeStruct((1, hid), f32),
            jax.ShapeDtypeStruct((1, d), f32),
        ],
        compiler_params=params(1),
        cost_estimate=cost(rows * d * hid * 2 * 5.25, rows * d * 8),
        name="ffn_own",
    )(info, x, c, w_up, w_down, b_up)


def ffn_rest_kernel(
    tiles_per, info, x, c, b_up, state, before, acc_in, gain, b_down, out_own, *rest
):
    ffn_refs, out_refs = rest[:COUNT], rest[COUNT : 2 * COUNT]
    out, half, g_mixed, vecs, w, w_out, grad, acc, act, sems, out_sem = rest[2 * COUNT :]
    k, i = pl.program_id(0), pl.program_id(1)
    blocks, tiles = pl.num_programs(0), pl.num_programs(1)
    hid = w.shape[1] // 2
    piece = hid // GROUP
    slot = lax.rem(k, 2)

    def load(kk, where):
        for ref, m in zip(ffn_refs, PIECES):
            off = pl.multiple_of((info[1] ^ m) * piece, 16)
            for part in range(2):
                pltpu.make_async_copy(
                    ref.at[kk, pl.ds(part * piece, piece)],
                    w.at[where, pl.ds(part * hid + off, piece)],
                    sems.at[where],
                ).start()

    @pl.when((k == 0) & (i == 0))
    def _():
        load(0, 0)
        vecs[...] = jnp.zeros_like(vecs)
        first = (out_own.shape[0] // GROUP) * 2
        start_loads(info, out_refs, out_own, out_targets(w_out, first), out_sem)

    @pl.when(i == 0)
    def _():
        wait_whole(w.at[slot], sems.at[slot])

        @pl.when(k + 1 < blocks)
        def _():
            load(k + 1, 1 - slot)

    @pl.when((k == blocks - 1) & (i == 0))
    def _():
        wait_whole(w_out, out_sem)

    row0 = pl.multiple_of(i * FFN_TILE, FFN_TILE)
    xs = x[pl.ds(row0, FFN_TILE), :]
    cs = c[pl.ds(row0, FFN_TILE), :]
    src_t = (info[0] + 3 - k) & 3
    bias = b_up[pl.ds(src_t, 1), :]
    cut = hid // 4
    grads = []
    for h in range(4):
        at = slice(h * cut, (h + 1) * cut)
        a, slope = gelu_both(dot_nt(xs, w[slot, at]) + bias[:, at])
        act[:, at] = a.astype(bf16)
        gact = dot_nt(cs, w[slot, hid + h * cut : hid + (h + 1) * cut])
        grads.append((gact * slope).astype(bf16))
    part = dot(jnp.concatenate(grads, axis=1), w[slot, :hid])

    @pl.when(k == 0)
    def _():
        grad[pl.ds(row0, FFN_TILE), :] = before[...].astype(f32) + part

    @pl.when((k > 0) & (k < blocks - 1))
    def _():
        grad[pl.ds(row0, FFN_TILE), :] += part

    own = tiles // 4
    mine = (i // own) == info[0]
    out0 = pl.multiple_of(lax.rem(i, own) * FFN_TILE, FFN_TILE)

    @pl.when(mine & (k == 0))
    def _():
        acc[pl.ds(out0, FFN_TILE), :] = acc_in[pl.ds(out0, FFN_TILE), :] + dot(act[...], w[slot, hid:])

    @pl.when(mine & (k > 0))
    def _():
        acc[pl.ds(out0, FFN_TILE), :] += dot(act[...], w[slot, hid:])

    @pl.when(k == blocks - 1)
    def _():
        g2 = grad[pl.ds(row0, FFN_TILE), :] + part
        s1 = state[...].astype(f32)
        n, r = normalise(s1)
        g1 = cs.astype(f32) + norm_back(g2, n, r, gain[...])
        half[...] = g1.astype(bf16)
        vecs[0:1, :] += jnp.sum(g2 * n, axis=0, keepdims=True)
        vecs[1:2, :] += jnp.sum(g2, axis=0, keepdims=True)
        vecs[2:3, :] += jnp.sum(g1, axis=0, keepdims=True)

        first, length = tile_length(info, i, tiles_per * TILE // FFN_TILE, FFN_TILE)

        @pl.when(first < length)
        def _():
            pos = lax.broadcasted_iota(jnp.int32, (FFN_TILE, 1), 0) + first
            g_mixed[...] = jnp.where(
                pos < length, dot_nt(half[...], w_out[...]), 0.0
            ).astype(bf16)

        @pl.when(mine)
        def _():
            out[pl.ds(out0, FFN_TILE), :] = (
                s1 + acc[pl.ds(out0, FFN_TILE), :] + b_down[...]
            ).astype(bf16)


def ffn_rest_call(
    info, x, c, b_up, state, before, acc, gain, b_down, out_own, out_pieces, pieces, tiles_per
):
    rows, d = x.shape
    hid = b_up.shape[1]
    tiles = rows // FFN_TILE
    last = pl.BlockSpec((FFN_TILE, d), lambda k, i, s: (jnp.where(k == 2, i, 0), 0))
    early = pl.BlockSpec((FFN_TILE, d), lambda k, i, s: (jnp.where(k == 0, i, tiles - 1), 0))
    return pl.pallas_call(
        functools.partial(ffn_rest_kernel, tiles_per),
        grid_spec=pltpu.PrefetchScalarGridSpec(
            num_scalar_prefetch=1,
            grid=(3, tiles),
            in_specs=[
                once((rows, d)), once((rows, d)), whole((4, hid)), last, early,
                once((rows // 4, d)), whole((1, d)), whole((1, d)), ANY,
            ]
            + [ANY] * (2 * COUNT),
            out_specs=[once((rows // 4, d)), last, last, whole((8, d))],
            scratch_shapes=[
                pltpu.VMEM((2, 2 * hid, d), bf16),
                pltpu.VMEM((d, d), bf16),
                pltpu.VMEM((rows, d), f32),
                pltpu.VMEM((rows // 4, d), f32),
                pltpu.VMEM((FFN_TILE, hid), bf16),
                pltpu.SemaphoreType.DMA((2,)),
                pltpu.SemaphoreType.DMA,
            ],
        ),
        out_shape=[
            jax.ShapeDtypeStruct((rows // 4, d), bf16),
            jax.ShapeDtypeStruct((rows, d), bf16),
            jax.ShapeDtypeStruct((rows, d), bf16),
            jax.ShapeDtypeStruct((8, d), f32),
        ],
        compiler_params=params(2),
        cost_estimate=cost(rows * d * hid * 2 * 11, rows * d * 20),
        name="ffn_rest",
    )(info, x, c, b_up, state, before, acc, gain, b_down, out_own, *pieces, *out_pieces)


def norm_one_kernel(tiles_per, info, dq, dk, dv, state, gs, gain, *rest):
    own, refs, (half, vecs, w, grad, sem) = rest[0], rest[1 : 1 + COUNT], rest[1 + COUNT :]
    i = pl.program_id(0)
    d = dq.shape[1]

    @pl.when(i == 0)
    def _():
        start_loads(info, refs, own, qkv_targets(w), sem)
        vecs[...] = jnp.zeros_like(vecs)
        wait_whole(w, sem)

    first, length = tile_length(info, i, tiles_per)

    @pl.when(first < length)
    def _():
        grad[...] = (
            dot(dq[...], w[:d]) + dot(dk[...], w[d : 2 * d]) + dot(dv[...], w[2 * d :])
        )
        n, r = normalise(state[...].astype(f32))
        g1 = grad[...]
        g0 = gs[...].astype(f32) + norm_back(g1, n, r, gain[...])
        half[...] = g0.astype(bf16)
        vecs[0:1, :] += jnp.sum(g1 * n, axis=0, keepdims=True)
        vecs[1:2, :] += jnp.sum(g1, axis=0, keepdims=True)
        vecs[2:3, :] += jnp.sum(g0, axis=0, keepdims=True)

    @pl.when(first >= length)
    def _():
        half[...] = gs[...]
        vecs[2:3, :] += jnp.sum(gs[...].astype(f32), axis=0, keepdims=True)


def norm_one_call(info, dq, dk, dv, state, gs, gain, own, pieces, tiles_per):
    rows, d = dq.shape
    row = pl.BlockSpec((TILE, d), lambda i, s: (i, 0))
    return pl.pallas_call(
        functools.partial(norm_one_kernel, tiles_per),
        grid_spec=pltpu.PrefetchScalarGridSpec(
            num_scalar_prefetch=1,
            grid=(rows // TILE,),
            in_specs=[row] * 5 + [whole((1, d))] + [ANY] * (1 + COUNT),
            out_specs=[row, whole((8, d))],
            scratch_shapes=[
                pltpu.VMEM((3 * d, d), bf16),
                pltpu.VMEM((TILE, d), f32),
                pltpu.SemaphoreType.DMA,
            ],
        ),
        out_shape=[jax.ShapeDtypeStruct((rows, d), bf16), jax.ShapeDtypeStruct((8, d), f32)],
        compiler_params=params(1),
        cost_estimate=cost(6 * rows * d * d, rows * d * 16),
        name="norm_one_back",
    )(info, dq, dk, dv, state, gs, gain, own, *pieces)


def joined_kernel(side, info, half, *rest):
    parts, rest = (rest[:4], rest[4:]) if side == 0 else ((), rest)
    own, refs, rest = rest[0], rest[1 : 1 + COUNT], rest[1 + COUNT :]
    grad, out = (rest[0], rest[1]) if side == 0 else (rest[0], None)
    w, sem = rest[-2:]
    d = half.shape[1]
    i = pl.program_id(0)

    @pl.when(i == 0)
    def _():
        start_loads(info, refs, own, skip_targets(w), sem)
        wait_whole(w, sem)

    grad[...] = dot_nt(half[...], w[side * d : (side + 1) * d]).astype(bf16)
    source = (info[0] + 4 - i // (pl.num_programs(0) // 4)) & 3
    for k, ref in enumerate(parts):

        @pl.when(source == k)
        def _(ref=ref):
            out[...] = ref[...]


def joined_call(side, info, half, parts, own, pieces):
    rows, d = half.shape
    row = pl.BlockSpec((TILE, d), lambda i, s: (i, 0))
    per = rows // TILE // 4
    count = 2 if side == 0 else 1

    def part_spec(k):
        def index(i, s):
            at = i - ((s[0] + 4 - k) & 3) * per
            return jnp.clip(at, 0, per - 1), 0

        return pl.BlockSpec((TILE, d), index)

    return pl.pallas_call(
        functools.partial(joined_kernel, side),
        grid_spec=pltpu.PrefetchScalarGridSpec(
            num_scalar_prefetch=1,
            grid=(rows // TILE,),
            in_specs=[row] + [part_spec(k) for k in range(len(parts))] + [ANY] * (1 + COUNT),
            out_specs=[row] * count,
            scratch_shapes=[pltpu.VMEM((2 * d, d), bf16), pltpu.SemaphoreType.DMA],
        ),
        out_shape=[jax.ShapeDtypeStruct((rows, d), bf16)] * count,
        compiler_params=params(1),
        cost_estimate=cost(2 * rows * d * d, rows * d * 4),
        name="joined_back",
    )(info, half, *parts, own, *pieces)


def outer(a, b):
    return lax.dot_general(a, b, TN, preferred_element_type=f32).astype(bf16)


def part_of(array, index):
    return lax.dynamic_index_in_dim(array, index, 0, keepdims=False)


def in_order(mine, other, chip, core):
    blocks = []
    for h in range(2):
        for p in range(GROUP // 2):
            a, b = part_of(mine, chip ^ p), part_of(other, chip ^ p)
            blocks.append(jnp.where(core == h, a, b).astype(f32))
    return jnp.stack(blocks)


def sum_cores(x, core):
    x = x.reshape((2, GROUP // 2) + x.shape[1:])
    total = part_of(x, core).astype(f32) + across(part_of(x, 1 - core), 1).astype(f32)
    return total.astype(bf16)


def to_chips(kept, chip):
    return [across(part_of(kept, chip ^ (m // 2)), m) for m in (2, 4, 6)]


def sum_chips(kept, arrived, chip):
    total = part_of(kept, chip).astype(f32) + sum(x.astype(f32) for x in arrived)
    return total.astype(bf16)


def together(*values):
    return lax.optimization_barrier(values)


def body(
    hidden_in,
    skip_state,
    lengths,
    w_skip,
    b_skip,
    norm1_gain,
    norm1_bias,
    w_qkv,
    b_qv,
    w_out,
    b_out,
    norm2_gain,
    norm2_bias,
    w_up,
    b_up,
    w_down,
    b_down,
    cotangent,
):
    tensor = lax.axis_index("tensor")
    member = lax.rem(lax.axis_index("batch"), GROUP)
    info = jnp.concatenate([jnp.stack([tensor, member]).astype(jnp.int32), lengths])
    rows, d = hidden_in.shape
    seq = rows // lengths.shape[0]
    tiles_per = seq // TILE
    columns = w_out.shape[0]

    core, chip = member & 1, member >> 1
    first_col = tensor * columns

    def share(array, axis=0):
        size = array.shape[axis] // GROUP
        return lax.dynamic_slice_in_dim(array, member * size, size, axis)

    def line(v):
        return v[None, :]

    biases = jnp.concatenate([b_qv.reshape(-1), b_up])
    b_hi = biases.astype(bf16)
    b_mid = (biases - b_hi.astype(f32)).astype(bf16)
    b_low = (biases - b_hi.astype(f32) - b_mid.astype(f32)).astype(bf16)
    b_rows = jnp.concatenate([b_hi, b_mid, b_low])
    b_rows = jnp.pad(b_rows, (0, 16 * d - b_rows.size)).reshape(16, d)

    first_piece = jnp.concatenate([share(w_skip), share(w_out)], 0)
    first_z = jnp.stack([along(first_piece, k) for k in (1, 2, 3)])
    b_terms = jnp.stack([b_rows] + [along(b_rows, k) for k in (1, 2, 3)])

    qkv_own = jnp.swapaxes(w_qkv, 1, 2)
    qkv_piece = share(qkv_own, 1).reshape(-1, d)
    qkv_own = qkv_own.reshape(-1, d)
    up_piece = jnp.swapaxes(share(w_up, 1), 0, 1)
    ffn_piece = jnp.concatenate([up_piece, share(w_down)], 0)
    first_z, qkv_piece, qkv_own, ffn_piece, b_terms = together(
        first_z, qkv_piece, qkv_own, ffn_piece, b_terms
    )
    qkv_z = [along(qkv_piece, k) for k in (1, 2, 3)]
    first_chips, qkv_z, ffn_piece = together(tuple(from_chips(first_z)), tuple(qkv_z), ffn_piece)
    first_all = from_cores(list(first_chips))
    first_all, qkv_z, ffn_piece = together(tuple(first_all), qkv_z, ffn_piece)

    qkv_chips = from_chips(jnp.stack(qkv_z))
    up1, up3 = along(ffn_piece, 1), along(ffn_piece, 3)
    state_zero, normed_one = skip_call(
        info, hidden_in, skip_state, line(b_skip), line(norm1_gain), line(norm1_bias),
        w_skip, first_all,
    )
    terms = b_terms.reshape(4, -1).astype(f32)
    size = biases.size
    relative = terms[:, :size] + terms[:, size : 2 * size] + terms[:, 2 * size : 3 * size]
    all_biases = jnp.stack([relative[(tensor - j) & 3] for j in range(4)])
    b_q = all_biases[:, :columns].reshape(1, d)
    b_v = all_biases[:, columns : 2 * columns].reshape(1, d)
    b_up_all = all_biases[:, 2 * columns :]
    qkv_chips, up1, up3, state_zero, normed_one, b_q, b_v = together(
        tuple(qkv_chips), up1, up3, state_zero, normed_one, b_q, b_v
    )

    qkv_all = from_cores(list(qkv_chips))
    up2 = along(up1, 1)
    q, k, v = qkv_call(info, normed_one, b_q, b_v, qkv_own, qkv_all, tiles_per)
    q, k, v, up2 = together(q, k, v, up2)
    ffn_chips = from_chips(jnp.stack([up1, up2, up3]))
    mixed, lse = attend_call(info, q, k, v, seq)
    lse = lse[:, :HEADS].T
    state_one, normed_two = mix_call(
        info, mixed, state_zero, line(b_out), line(norm2_gain), line(norm2_bias), w_out, first_all,
        tiles_per,
    )
    state_one, normed_two, ffn_chips = together(state_one, normed_two, tuple(ffn_chips))
    ffn_all = from_cores(list(ffn_chips))
    before, acc, g_up, g_down, g_bup, g_bdown = ffn_own_call(
        info, normed_two, cotangent, w_up, w_down, line(b_up)
    )
    before, acc, ffn_all, g_up, g_down = together(before, acc, tuple(ffn_all), g_up, g_down)
    g_up = lax.psum(g_up, "batch")
    out_rows, half_one, grad_mixed, vecs_two = ffn_rest_call(
        info, normed_two, cotangent, b_up_all, state_one, before, acc, line(norm2_gain),
        line(b_down), w_out, first_all, ffn_all, tiles_per,
    )
    out_rows, half_one, grad_mixed, g_up, g_down = together(
        out_rows, half_one, grad_mixed, g_up, g_down
    )
    g_down = lax.psum(g_down, "batch")
    out1, out3 = along(out_rows, 1), along(out_rows, 3)

    def own(array):
        return lax.dynamic_slice_in_dim(array, first_col, columns, 1)

    dq, dk, dv = attend_back_call(info, q, k, v, grad_mixed, mixed, lse, seq)
    dq, dk, dv, g_down, half_one, out1, out3 = together(dq, dk, dv, g_down, half_one, out1, out3)
    out2 = along(out1, 1)
    g_out = outer(own(mixed), half_one)
    slices = jnp.concatenate([own(x) for x in (dq, dk, dv)], 1)
    g_qkv = outer(normed_one, slices)
    g_bqv = jnp.sum(slices, axis=0, dtype=f32)
    one_group = lax.axis_size("batch") == GROUP
    heads = g_qkv.reshape(GROUP, d // GROUP, 3 * columns)
    if one_group:
        kept_heads = sum_cores(heads, core)
        kept_heads, dq, half_one = together(kept_heads, dq, half_one)
        sent_heads = to_chips(kept_heads, chip)
    else:
        heads = lax.psum(heads, "batch")

    half_zero, vecs_one = norm_one_call(
        info, dq, dk, dv, state_zero, half_one, line(norm1_gain), qkv_own, qkv_all, tiles_per
    )
    half_zero, vecs_one, out2 = together(half_zero, vecs_one, out2)
    if one_group:
        sent_heads, half_zero = together(tuple(sent_heads), half_zero)
    shard = w_skip.shape[0]
    joined = jnp.concatenate([hidden_in, skip_state], axis=1)
    features = lax.dynamic_slice_in_dim(joined, tensor * shard, shard, 1)
    g_skip = outer(features, half_zero)
    g_bqv = jnp.concatenate([g_bqv[:columns], g_bqv[2 * columns :]])
    g_bqv = jnp.pad(line(g_bqv), ((0, 0), (0, d - g_bqv.size)))
    vectors = jnp.concatenate(
        [vecs_two[:3], g_bdown, vecs_one[:3], g_bqv, g_bup.reshape(-1, d)], axis=0
    )
    vectors = jnp.pad(vectors, ((0, 2 * GROUP - vectors.shape[0]), (0, 0))).astype(bf16)
    parts = [g_skip, g_out, vectors]
    last = jnp.concatenate([x.reshape(GROUP, -1, d) for x in parts], axis=1)
    if one_group:
        kept = sum_cores(last, core)
        kept, half_zero = together(kept, half_zero)
        sent = to_chips(kept, chip)
        total_heads = sum_chips(kept_heads, sent_heads, chip)
        out_parts = [out_rows, out1, out2, out3]
        grad_hidden, output = joined_call(0, info, half_zero, out_parts, w_skip, first_all)
        sent, total_heads, grad_hidden, output, half_zero = together(
            tuple(sent), total_heads, grad_hidden, output, half_zero
        )
        total, half_zero = together(sum_chips(kept, sent, chip), half_zero)
        sums, sums_heads = from_chips(total), from_chips(total_heads)
        (grad_skip,) = joined_call(1, info, half_zero, [], w_skip, first_all)
        sums, sums_heads, grad_skip, g_up, g_down = together(
            tuple(sums), tuple(sums_heads), grad_skip, g_up.astype(f32), g_down.astype(f32)
        )
        sums, sums_heads = jnp.stack(sums), jnp.stack(sums_heads)
        other, other_heads = across(sums, 1), across(sums_heads, 1)
        last = in_order(sums, other, chip, core)
        heads = in_order(sums_heads, other_heads, chip, core)
    else:
        last = lax.psum(last, "batch").astype(f32)
        heads = heads.astype(f32)
        out_parts = [out_rows, out1, out2, out3]
        grad_hidden, output = joined_call(0, info, half_zero, out_parts, w_skip, first_all)
        (grad_skip,) = joined_call(1, info, half_zero, [], w_skip, first_all)
        g_up, g_down = g_up.astype(f32), g_down.astype(f32)
    ends = [0]
    for x in parts:
        ends.append(ends[-1] + x.size // d // GROUP)
    g_skip, g_out, vectors = [
        last[:, a:b].reshape(-1, d) for a, b in zip(ends[:-1], ends[1:])
    ]
    heads = heads.reshape(d, 3 * columns)
    g_qkv = jnp.stack([heads[:, n * columns : (n + 1) * columns] for n in range(3)])
    return (
        output,
        grad_hidden,
        grad_skip,
        g_skip,
        vectors[6],
        vectors[4],
        vectors[5],
        g_qkv,
        vectors[7, : 2 * columns].reshape(2, columns),
        g_out,
        vectors[2],
        vectors[0],
        vectors[1],
        g_up,
        vectors[8 : 8 + g_bup.size // d].reshape(-1),
        g_down,
        vectors[3],
    )


def solution(mesh):
    placed = (
        P("batch", None),
        P("batch", None),
        P("batch"),
        P("tensor", None),
        P(),
        P(),
        P(),
        P(None, None, "tensor"),
        P(None, "tensor"),
        P("tensor", None),
        P(),
        P(),
        P(),
        P(None, "tensor"),
        P("tensor"),
        P("tensor", None),
        P(),
        P("batch", None),
    )
    return jax.shard_map(
        body,
        mesh=mesh,
        in_specs=placed,
        out_specs=(
            P("batch", None),
            P("batch", None),
            P("batch", None),
            P("tensor", None),
            P(),
            P(),
            P(),
            P(None, None, "tensor"),
            P(None, "tensor"),
            P("tensor", None),
            P(),
            P(),
            P(),
            P(None, "tensor"),
            P("tensor"),
            P("tensor", None),
            P(),
        ),
        check_vma=False,
    )
```

```python
import functools

import jax
import jax.numpy as jnp
from jax import lax
from jax.experimental import pallas as pl
from jax.experimental.pallas import tpu as pltpu
from jax.sharding import PartitionSpec as P

HEADS = 16
HEAD_DIM = 64
GROUP = 8
TILE = 256
FFN_TILE = 512
LOG2E = 1.4426950408889634
LN2 = 0.6931471805599453
GELU_C = 0.7978845608028654
GELU_A = 0.044715

norm_eps = 1e-05
masked_score = -1e30
bf16 = jnp.bfloat16
f32 = jnp.float32

NT = (((1,), (1,)), ((), ()))
TN = (((0,), (0,)), ((), ()))

PIECES = [0, 2, 4, 6, 1, 3, 5, 7]
COUNT = len(PIECES)


def dot(a, b):
    return jnp.dot(a, b, preferred_element_type=f32)


def dot_nt(a, b):
    return lax.dot_general(a, b, NT, preferred_element_type=f32)


def dot_tn(a, b):
    return lax.dot_general(a, b, TN, preferred_element_type=f32)


def params(ndim, mib=60):
    return pltpu.CompilerParams(
        vmem_limit_bytes=mib * 1024 * 1024, dimension_semantics=("arbitrary",) * ndim
    )


def cost(flops, moved):
    return pl.CostEstimate(
        flops=int(flops) // 10, bytes_accessed=int(moved) // 10, transcendentals=0
    )


def along(x, k):
    n = lax.axis_size("tensor")
    return lax.ppermute(x, "tensor", [(i, (i + k) % n) for i in range(n)])


def across(x, m):
    n = lax.axis_size("batch")
    return lax.ppermute(x, "batch", [(i, i ^ m) for i in range(n)])


def from_chips(held):
    return [held, across(held, 2), across(held, 4), across(held, 6)]


def from_cores(held):
    return held + [across(x, 1) for x in held]


def after(x, *earlier):
    return lax.optimization_barrier((x,) + earlier)[0]


def start_loads(info, refs, own, targets, sem):
    for first, rows, own_first, dest, place in targets:
        off = pl.multiple_of(place(info[0], 0), 16)
        pltpu.make_async_copy(
            own.at[pl.ds(own_first, rows * GROUP)], dest.at[pl.ds(off, rows * GROUP)], sem
        ).start()
    for ref, m in zip(refs, PIECES):
        for kk in range(3):
            src_t = (info[0] + 3 - kk) & 3
            src_b = info[1] ^ m
            for first, rows, _, dest, place in targets:
                off = pl.multiple_of(place(src_t, src_b), 16)
                pltpu.make_async_copy(
                    ref.at[kk, pl.ds(first, rows)], dest.at[pl.ds(off, rows)], sem
                ).start()


def wait_whole(dest, sem):
    pltpu.make_async_copy(dest, dest, sem).wait()


ANY = pl.BlockSpec(memory_space=pltpu.HBM)


def whole(shape):
    return pl.BlockSpec(shape, lambda *_: (0,) * len(shape))


def once(shape):
    return pl.BlockSpec(shape, lambda *_: (0,) * len(shape), pipeline_mode=pl.Buffered(1))


def normalise(v):
    mean = jnp.mean(v, axis=-1, keepdims=True)
    centred = v - mean
    r = lax.rsqrt(jnp.mean(centred * centred, axis=-1, keepdims=True) + norm_eps)
    return centred * r, r


def norm_back(grad, n, r, gain):
    e = grad * gain
    return r * (
        e
        - jnp.mean(e, axis=-1, keepdims=True)
        - n * jnp.mean(e * n, axis=-1, keepdims=True)
    )


def tile_length(info, i, tiles_per, tile=TILE):
    u = i // tiles_per
    return (i - u * tiles_per) * tile, info[2 + u]


def skip_targets(w):
    shard = w.shape[0] // 4
    piece = shard // GROUP
    return [(0, piece, 0, w, lambda t, b: t * shard + b * piece)]


def out_targets(w, first):
    shard = w.shape[0] // 4
    piece = shard // GROUP
    return [(first, piece, 0, w, lambda t, b: t * shard + b * piece)]


def skip_kernel(info, hid, skp, b_skip, gain, bias, *rest):
    own, refs, (state, normed, w, sem) = rest[0], rest[1 : 1 + COUNT], rest[1 + COUNT :]

    @pl.when(pl.program_id(0) == 0)
    def _():
        start_loads(info, refs, own, skip_targets(w), sem)
        wait_whole(w, sem)

    width = hid.shape[1]
    total = dot(hid[...], w[:width]) + dot(skp[...], w[width:]) + b_skip[...]
    state[...] = total.astype(bf16)
    n, _ = normalise(total)
    normed[...] = (n * gain[...] + bias[...]).astype(bf16)


def skip_call(info, hid, skp, b_skip, gain, bias, own, pieces):
    rows, d = hid.shape
    row = pl.BlockSpec((TILE, d), lambda i, s: (i, 0))
    return pl.pallas_call(
        skip_kernel,
        grid_spec=pltpu.PrefetchScalarGridSpec(
            num_scalar_prefetch=1,
            grid=(rows // TILE,),
            in_specs=[row, row, whole((1, d)), whole((1, d)), whole((1, d))] + [ANY] * (1 + COUNT),
            out_specs=[row, row],
            scratch_shapes=[pltpu.VMEM((2 * d, d), bf16), pltpu.SemaphoreType.DMA],
        ),
        out_shape=[jax.ShapeDtypeStruct((rows, d), bf16)] * 2,
        compiler_params=params(1),
        cost_estimate=cost(4 * rows * d * d, rows * d * 10 + 4 * d * d),
        name="skip_norm",
    )(info, hid, skp, b_skip, gain, bias, own, *pieces)


def qkv_targets(w):
    d = w.shape[0] // 3
    shard = d // 4
    part = shard // GROUP
    return [
        (s * part, part, s * shard, w, lambda t, b, s=s: s * d + t * shard + b * part)
        for s in range(3)
    ]


def qkv_kernel(tiles_per, info, x, b_q, b_v, *rest):
    own, refs, (q, k, v, w, sem) = rest[0], rest[1 : 1 + COUNT], rest[1 + COUNT :]
    i = pl.program_id(0)
    d = x.shape[1]

    @pl.when(i == 0)
    def _():
        start_loads(info, refs, own, qkv_targets(w), sem)
        wait_whole(w, sem)

    first, length = tile_length(info, i, tiles_per)

    @pl.when(first < length)
    def _():
        xs = x[...]
        q[...] = ((dot_nt(xs, w[:d]) + b_q[...]) * (LOG2E * HEAD_DIM**-0.5)).astype(bf16)
        k[...] = dot_nt(xs, w[d : 2 * d]).astype(bf16)
        v[...] = (dot_nt(xs, w[2 * d :]) + b_v[...]).astype(bf16)


def qkv_call(info, x, b_q, b_v, own, pieces, tiles_per):
    rows, d = x.shape
    row = pl.BlockSpec((TILE, d), lambda i, s: (i, 0))
    return pl.pallas_call(
        functools.partial(qkv_kernel, tiles_per),
        grid_spec=pltpu.PrefetchScalarGridSpec(
            num_scalar_prefetch=1,
            grid=(rows // TILE,),
            in_specs=[row, whole((1, d)), whole((1, d))] + [ANY] * (1 + COUNT),
            out_specs=[row] * 3,
            scratch_shapes=[pltpu.VMEM((3 * d, d), bf16), pltpu.SemaphoreType.DMA],
        ),
        out_shape=[jax.ShapeDtypeStruct((rows, d), bf16)] * 3,
        compiler_params=params(1),
        cost_estimate=cost(4 * rows * d * d, rows * d * 8 + 6 * d * d),
        name="qkv",
    )(info, x, b_q, b_v, own, *pieces)


def slope2(head):
    return jnp.exp2(jnp.full((1, 1), -8.0 / HEADS, f32) * (head + 1).astype(f32)) * LOG2E


def attend_kernel(info, q, k, v, mixed, lse, dist):
    u, hp = pl.program_id(0), pl.program_id(1)
    seq = q.shape[0]
    tiles = seq // TILE
    length = info[2 + u]

    @pl.when((u == 0) & (hp == 0))
    def _():
        r = lax.broadcasted_iota(jnp.int32, dist.shape, 0)
        c = lax.broadcasted_iota(jnp.int32, dist.shape, 1)
        dist[...] = jnp.abs(r - c - (seq - TILE)).astype(f32)

    lane = lax.broadcasted_iota(jnp.int32, (TILE, 128), 1)
    used = (length + TILE - 1) // TILE

    for n in range(1, tiles + 1):

        @pl.when(used == n)
        def _(n=n):
            cols = n * TILE
            valid = (
                lax.broadcasted_iota(jnp.int32, (TILE, TILE), 0) + (cols - TILE) < length
            )
            vt = v[:cols, :].astype(f32).T.astype(bf16)

            def step(i, carry):
                row0 = pl.multiple_of(i * TILE, TILE)
                qs = q[pl.ds(row0, TILE), :]
                start = pl.multiple_of((seq - TILE) - row0, TILE)
                gap = dist[pl.ds(start, cols), :]
                held, outs = [], []
                for a in range(2):
                    qa = jnp.where((lane < 64) == (a == 0), qs, jnp.zeros_like(qs))
                    held.append(dot_nt(k[:cols, :], qa))
                for a in range(2):
                    s = held[a] - slope2(2 * hp + a) * gap
                    last = jnp.where(valid, s[cols - TILE :, :], masked_score)
                    s = jnp.concatenate([s[: cols - TILE, :], last], axis=0) if n > 1 else last
                    m = jnp.max(s, axis=0, keepdims=True)
                    p = jnp.exp2(s - m)
                    total = jnp.sum(p, axis=0, keepdims=True)
                    held[a] = (p.astype(bf16), total)
                    lse[pl.ds(2 * hp + a, 1), pl.ds(row0, TILE)] = m + jnp.log2(total)
                for a in range(2):
                    p, total = held[a]
                    outs.append(dot(vt[a * 64 : (a + 1) * 64, :], p) * (1.0 / total))
                o = jnp.concatenate(outs, axis=0).T
                pos = lax.broadcasted_iota(jnp.int32, (TILE, 128), 0) + row0
                mixed[pl.ds(row0, TILE), :] = jnp.where(pos < length, o, 0.0).astype(bf16)
                return carry

            lax.fori_loop(0, n, step, 0, unroll=True)
            if n < tiles:
                mixed[cols:, :] = jnp.zeros((seq - cols, 128), bf16)


def attend_call(info, q, k, v, seq):
    rows, d = q.shape
    utts = rows // seq
    blk = pl.BlockSpec((seq, 128), lambda u, h, s: (u, h))
    return pl.pallas_call(
        attend_kernel,
        grid_spec=pltpu.PrefetchScalarGridSpec(
            num_scalar_prefetch=1,
            grid=(utts, d // 128),
            in_specs=[blk] * 3,
            out_specs=[blk, pl.BlockSpec((HEADS, seq), lambda u, h, s: (0, u))],
            scratch_shapes=[pltpu.VMEM((2 * seq - TILE, TILE), f32)],
        ),
        out_shape=[
            jax.ShapeDtypeStruct((rows, d), bf16),
            jax.ShapeDtypeStruct((HEADS, rows), f32),
        ],
        compiler_params=params(2),
        cost_estimate=cost(rows * seq * d * 4, rows * d * 8),
        name="attend",
    )(info, q, k, v)


def attend_back_kernel(info, q, k, v, g, o, lse, dq, dk, dv, dist, akey, aval):
    u, hp = pl.program_id(0), pl.program_id(1)
    seq = q.shape[0]
    tiles = seq // TILE
    length = info[2 + u]

    @pl.when((u == 0) & (hp == 0))
    def _():
        r = lax.broadcasted_iota(jnp.int32, dist.shape, 0)
        c = lax.broadcasted_iota(jnp.int32, dist.shape, 1)
        dist[...] = jnp.abs(r - c - (seq - TILE)).astype(f32)

    lane = lax.broadcasted_iota(jnp.int32, (TILE, 128), 1)
    used = (length + TILE - 1) // TILE

    for n in range(1, tiles + 1):

        @pl.when(used == n)
        def _(n=n):
            cols = n * TILE
            valid = (
                lax.broadcasted_iota(jnp.int32, (TILE, TILE), 0) + (cols - TILE) < length
            )
            akey[:cols, :] = jnp.zeros((cols, 128), f32)
            aval[:cols, :] = jnp.zeros((cols, 128), f32)
            kt = k[:cols, :].astype(f32).T.astype(bf16)

            def step(i, carry):
                row0 = pl.multiple_of(i * TILE, TILE)
                qs = q[pl.ds(row0, TILE), :]
                gs = g[pl.ds(row0, TILE), :]
                start = pl.multiple_of((seq - TILE) - row0, TILE)
                gap = dist[pl.ds(start, cols), :]
                both = gs.astype(f32) * o[pl.ds(row0, TILE), :].astype(f32)
                hi = both.astype(bf16)
                lo = (both - hi.astype(f32)).astype(bf16)
                grads, held = [], []
                for a in range(2):
                    mine = (lane < 64) == (a == 0)
                    qa = jnp.where(mine, qs, jnp.zeros_like(qs))
                    ga = jnp.where(mine, gs, jnp.zeros_like(gs))
                    pick = jnp.where(
                        (lax.broadcasted_iota(jnp.int32, (8, 128), 1) < 64) == (a == 0), 1.0, 0.0
                    ).astype(bf16)
                    delta = (dot_nt(pick, hi) + dot_nt(pick, lo))[:1, :]
                    held.append((qa, ga, delta, dot_nt(k[:cols, :], qa), dot_nt(v[:cols, :], ga)))
                for a in range(2):
                    qa, ga, delta, s, gw = held[a]
                    row = lse[pl.ds(2 * hp + a, 1), pl.ds(row0, TILE)]
                    s = s - (slope2(2 * hp + a) * gap + row)
                    last = jnp.where(valid, s[cols - TILE :, :], masked_score)
                    s = jnp.concatenate([s[: cols - TILE, :], last], axis=0) if n > 1 else last
                    p = jnp.exp2(s)
                    ds = (p * (gw - delta)).astype(bf16)
                    held[a] = (qa, ga, p.astype(bf16), ds)
                aval[:cols, :] += dot(held[0][2], held[0][1]) + dot(held[1][2], held[1][1])
                akey[:cols, :] += dot(held[0][3], held[0][0]) + dot(held[1][3], held[1][0])
                for a in range(2):
                    grads.append(dot(kt[a * 64 : (a + 1) * 64, :], held[a][3]))
                turned = jnp.concatenate(grads, axis=0) * HEAD_DIM**-0.5
                dq[pl.ds(row0, TILE), :] = turned.T.astype(bf16)
                return carry

            lax.fori_loop(0, n, step, 0, unroll=True)
            dk[:cols, :] = (akey[:cols, :] * LN2).astype(bf16)
            dv[:cols, :] = aval[:cols, :].astype(bf16)
            if n < tiles:
                for ref in (dq, dk, dv):
                    ref[cols:, :] = jnp.zeros((seq - cols, 128), bf16)


def attend_back_call(info, q, k, v, g, o, lse, seq):
    rows, d = q.shape
    utts = rows // seq
    blk = pl.BlockSpec((seq, 128), lambda u, h, s: (u, h))
    return pl.pallas_call(
        attend_back_kernel,
        grid_spec=pltpu.PrefetchScalarGridSpec(
            num_scalar_prefetch=1,
            grid=(utts, d // 128),
            in_specs=[blk] * 5 + [pl.BlockSpec((HEADS, seq), lambda u, h, s: (0, u))],
            out_specs=[blk] * 3,
            scratch_shapes=[
                pltpu.VMEM((2 * seq - TILE, TILE), f32),
                pltpu.VMEM((seq, 128), f32),
                pltpu.VMEM((seq, 128), f32),
            ],
        ),
        out_shape=[jax.ShapeDtypeStruct((rows, d), bf16)] * 3,
        compiler_params=params(2),
        cost_estimate=cost(rows * seq * d * 10, rows * d * 16),
        name="attend_back",
    )(info, q, k, v, g, o, lse)


def mix_kernel(tiles_per, info, mixed, state, b_out, gain, bias, *rest):
    own, refs, (state_one, normed, w, total, sem) = rest[0], rest[1 : 1 + COUNT], rest[1 + COUNT :]
    part = (own.shape[0] // GROUP) * 2
    i = pl.program_id(0)
    d = mixed.shape[1]

    @pl.when(i == 0)
    def _():
        start_loads(info, refs, own, out_targets(w, part), sem)
        wait_whole(w, sem)

    first, length = tile_length(info, i, tiles_per)
    total[...] = state[...].astype(f32) + b_out[...]

    @pl.when(first < length)
    def _():
        total[...] += dot(mixed[...], w[...])

    n, _ = normalise(total[...])
    state_one[...] = total[...].astype(bf16)
    normed[...] = (n * gain[...] + bias[...]).astype(bf16)


def mix_call(info, mixed, state, b_out, gain, bias, own, pieces, tiles_per):
    rows, d = mixed.shape
    row = pl.BlockSpec((TILE, d), lambda i, s: (i, 0))
    return pl.pallas_call(
        functools.partial(mix_kernel, tiles_per),
        grid_spec=pltpu.PrefetchScalarGridSpec(
            num_scalar_prefetch=1,
            grid=(rows // TILE,),
            in_specs=[row, row] + [whole((1, d))] * 3 + [ANY] * (1 + COUNT),
            out_specs=[row, row],
            scratch_shapes=[
                pltpu.VMEM((d, d), bf16),
                pltpu.VMEM((TILE, d), f32),
                pltpu.SemaphoreType.DMA,
            ],
        ),
        out_shape=[jax.ShapeDtypeStruct((rows, d), bf16)] * 2,
        compiler_params=params(1),
        cost_estimate=cost(2 * rows * d * d, rows * d * 12),
        name="mix_norm",
    )(info, mixed, state, b_out, gain, bias, own, *pieces)


def gelu_both(pre):
    sq = pre * pre
    t = jnp.tanh(pre * (GELU_C + GELU_C * GELU_A * sq))
    h = 0.5 + 0.5 * t
    a = pre * h
    return a, h + a * (1.0 - h) * (2.0 * GELU_C + 6.0 * GELU_C * GELU_A * sq)


def ffn_own_kernel(
    info, x, c, gact, w_up, w_down, b_up, grad, acc, g_up, g_down, g_bup, g_bdown, aup, adown, act, gpre
):
    i, tiles = pl.program_id(0), pl.num_programs(0)

    @pl.when(i == 0)
    def _():
        aup[...] = jnp.zeros_like(aup)
        adown[...] = jnp.zeros_like(adown)
        g_bup[...] = jnp.zeros_like(g_bup)
        g_bdown[...] = jnp.zeros_like(g_bdown)

    xs, cs = x[...], c[...]
    a, slope = gelu_both(dot(xs, w_up[...]) + b_up[...])
    act[...] = a.astype(bf16)
    gp = gact[...].astype(f32) * slope
    gpre[...] = gp.astype(bf16)
    g_bup[...] += jnp.sum(gp, axis=0, keepdims=True)
    adown[...] += dot_tn(act[...], cs)
    aup[...] += dot_tn(xs, gpre[...])
    grad[...] = dot_nt(gpre[...], w_up[...]).astype(bf16)
    g_bdown[...] += jnp.sum(cs.astype(f32), axis=0, keepdims=True)

    own = tiles // 4

    @pl.when((i // own) == info[0])
    def _():
        out0 = pl.multiple_of(lax.rem(i, own) * FFN_TILE, FFN_TILE)
        acc[pl.ds(out0, FFN_TILE), :] = dot(act[...], w_down[...])

    @pl.when(i == tiles - 1)
    def _():
        g_up[...] = aup[...].astype(bf16)
        g_down[...] = adown[...].astype(bf16)


def ffn_own_call(info, x, c, gact, w_up, w_down, b_up):
    rows, d = x.shape
    hid = b_up.shape[1]
    row = pl.BlockSpec((FFN_TILE, d), lambda i, s: (i, 0))
    hid_row = pl.BlockSpec((FFN_TILE, hid), lambda i, s: (i, 0))
    return pl.pallas_call(
        ffn_own_kernel,
        grid_spec=pltpu.PrefetchScalarGridSpec(
            num_scalar_prefetch=1,
            grid=(rows // FFN_TILE,),
            in_specs=[row, row, hid_row, once((d, hid)), once((hid, d)), whole((1, hid))],
            out_specs=[
                row, once((rows // 4, d)), once((d, hid)), once((hid, d)), whole((1, hid)),
                whole((1, d)),
            ],
            scratch_shapes=[
                pltpu.VMEM((d, hid), f32),
                pltpu.VMEM((hid, d), f32),
                pltpu.VMEM((FFN_TILE, hid), bf16),
                pltpu.VMEM((FFN_TILE, hid), bf16),
            ],
        ),
        out_shape=[
            jax.ShapeDtypeStruct((rows, d), bf16),
            jax.ShapeDtypeStruct((rows // 4, d), f32),
            jax.ShapeDtypeStruct((d, hid), bf16),
            jax.ShapeDtypeStruct((hid, d), bf16),
            jax.ShapeDtypeStruct((1, hid), f32),
            jax.ShapeDtypeStruct((1, d), f32),
        ],
        compiler_params=params(1),
        cost_estimate=cost(rows * d * hid * 2 * 5.25, rows * d * 8),
        name="ffn_own",
    )(info, x, c, gact, w_up, w_down, b_up)


def ffn_rest_kernel(
    tiles_per, info, x, c, b_up, state, before, acc_in, gain, b_down, out_own, *rest
):
    pair_refs, far_refs = rest[:COUNT], rest[COUNT : 2 * COUNT]
    out_refs, rest = rest[2 * COUNT : 3 * COUNT], rest[COUNT:]
    out, half, g_mixed, vecs, w, w_out, grad, acc, act, sems, out_sem = rest[2 * COUNT :]
    k, i = pl.program_id(0), pl.program_id(1)
    blocks, tiles = pl.num_programs(0), pl.num_programs(1)
    hid = w.shape[1] // 2
    piece = hid // GROUP
    slot = lax.rem(k, 2)

    def load(sources, where):
        for ref, m in zip(sources, PIECES):
            off = pl.multiple_of((info[1] ^ m) * piece, 16)
            for part in range(2):
                pltpu.make_async_copy(
                    ref.at[pl.ds(part * piece, piece)],
                    w.at[where, pl.ds(part * hid + off, piece)],
                    sems.at[where],
                ).start()

    @pl.when((k == 0) & (i == 0))
    def _():
        load([ref.at[0] for ref in pair_refs], 0)
        vecs[...] = jnp.zeros_like(vecs)
        first = (out_own.shape[0] // GROUP) * 2
        start_loads(info, out_refs, out_own, out_targets(w_out, first), out_sem)

    @pl.when(i == 0)
    def _():
        wait_whole(w.at[slot], sems.at[slot])

        @pl.when(k == 0)
        def _():
            load([ref.at[1] for ref in pair_refs], 1)

        @pl.when(k == 1)
        def _():
            load(far_refs, 0)

    @pl.when((k == blocks - 1) & (i == 0))
    def _():
        wait_whole(w_out, out_sem)

    row0 = pl.multiple_of(i * FFN_TILE, FFN_TILE)
    xs = x[pl.ds(row0, FFN_TILE), :]
    cs = c[pl.ds(row0, FFN_TILE), :]
    src_t = (info[0] + jnp.where(k == 2, 2, 3 - 2 * k)) & 3
    bias = b_up[pl.ds(src_t, 1), :]
    cut = hid // 4
    grads = []
    for h in range(4):
        at = slice(h * cut, (h + 1) * cut)
        a, slope = gelu_both(dot_nt(xs, w[slot, at]) + bias[:, at])
        act[:, at] = a.astype(bf16)
        gact = dot_nt(cs, w[slot, hid + h * cut : hid + (h + 1) * cut])
        grads.append((gact * slope).astype(bf16))
    part = dot(jnp.concatenate(grads, axis=1), w[slot, :hid])

    @pl.when(k == 0)
    def _():
        grad[pl.ds(row0, FFN_TILE), :] = before[...].astype(f32) + part

    @pl.when((k > 0) & (k < blocks - 1))
    def _():
        grad[pl.ds(row0, FFN_TILE), :] += part

    own = tiles // 4
    mine = (i // own) == info[0]
    out0 = pl.multiple_of(lax.rem(i, own) * FFN_TILE, FFN_TILE)

    @pl.when(mine & (k == 0))
    def _():
        acc[pl.ds(out0, FFN_TILE), :] = acc_in[pl.ds(out0, FFN_TILE), :] + dot(act[...], w[slot, hid:])

    @pl.when(mine & (k > 0))
    def _():
        acc[pl.ds(out0, FFN_TILE), :] += dot(act[...], w[slot, hid:])

    @pl.when(k == blocks - 1)
    def _():
        g2 = grad[pl.ds(row0, FFN_TILE), :] + part
        s1 = state[...].astype(f32)
        n, r = normalise(s1)
        g1 = cs.astype(f32) + norm_back(g2, n, r, gain[...])
        half[...] = g1.astype(bf16)
        vecs[0:1, :] += jnp.sum(g2 * n, axis=0, keepdims=True)
        vecs[1:2, :] += jnp.sum(g2, axis=0, keepdims=True)
        vecs[2:3, :] += jnp.sum(g1, axis=0, keepdims=True)

        first, length = tile_length(info, i, tiles_per * TILE // FFN_TILE, FFN_TILE)

        @pl.when(first < length)
        def _():
            pos = lax.broadcasted_iota(jnp.int32, (FFN_TILE, 1), 0) + first
            g_mixed[...] = jnp.where(
                pos < length, dot_nt(half[...], w_out[...]), 0.0
            ).astype(bf16)

        @pl.when(mine)
        def _():
            out[pl.ds(out0, FFN_TILE), :] = (
                s1 + acc[pl.ds(out0, FFN_TILE), :] + b_down[...]
            ).astype(bf16)


def ffn_rest_call(
    info, x, c, b_up, state, before, acc, gain, b_down, out_own, out_pieces, pieces, tiles_per
):
    rows, d = x.shape
    hid = b_up.shape[1]
    tiles = rows // FFN_TILE
    last = pl.BlockSpec((FFN_TILE, d), lambda k, i, s: (jnp.where(k == 2, i, 0), 0))
    early = pl.BlockSpec((FFN_TILE, d), lambda k, i, s: (jnp.where(k == 0, i, tiles - 1), 0))
    return pl.pallas_call(
        functools.partial(ffn_rest_kernel, tiles_per),
        grid_spec=pltpu.PrefetchScalarGridSpec(
            num_scalar_prefetch=1,
            grid=(3, tiles),
            in_specs=[
                once((rows, d)), once((rows, d)), whole((4, hid)), last, early,
                once((rows // 4, d)), whole((1, d)), whole((1, d)), ANY,
            ]
            + [ANY] * (3 * COUNT),
            out_specs=[once((rows // 4, d)), last, last, whole((8, d))],
            scratch_shapes=[
                pltpu.VMEM((2, 2 * hid, d), bf16),
                pltpu.VMEM((d, d), bf16),
                pltpu.VMEM((rows, d), f32),
                pltpu.VMEM((rows // 4, d), f32),
                pltpu.VMEM((FFN_TILE, hid), bf16),
                pltpu.SemaphoreType.DMA((2,)),
                pltpu.SemaphoreType.DMA,
            ],
        ),
        out_shape=[
            jax.ShapeDtypeStruct((rows // 4, d), bf16),
            jax.ShapeDtypeStruct((rows, d), bf16),
            jax.ShapeDtypeStruct((rows, d), bf16),
            jax.ShapeDtypeStruct((8, d), f32),
        ],
        compiler_params=params(2),
        cost_estimate=cost(rows * d * hid * 2 * 11, rows * d * 20),
        name="ffn_rest",
    )(info, x, c, b_up, state, before, acc, gain, b_down, out_own, *pieces, *out_pieces)


def norm_one_kernel(tiles_per, info, dq, dk, dv, state, gs, gain, *rest):
    own, refs, (half, vecs, w, grad, sem) = rest[0], rest[1 : 1 + COUNT], rest[1 + COUNT :]
    i = pl.program_id(0)
    d = dq.shape[1]

    @pl.when(i == 0)
    def _():
        start_loads(info, refs, own, qkv_targets(w), sem)
        vecs[...] = jnp.zeros_like(vecs)
        wait_whole(w, sem)

    first, length = tile_length(info, i, tiles_per)

    @pl.when(first < length)
    def _():
        grad[...] = (
            dot(dq[...], w[:d]) + dot(dk[...], w[d : 2 * d]) + dot(dv[...], w[2 * d :])
        )
        n, r = normalise(state[...].astype(f32))
        g1 = grad[...]
        g0 = gs[...].astype(f32) + norm_back(g1, n, r, gain[...])
        half[...] = g0.astype(bf16)
        vecs[0:1, :] += jnp.sum(g1 * n, axis=0, keepdims=True)
        vecs[1:2, :] += jnp.sum(g1, axis=0, keepdims=True)
        vecs[2:3, :] += jnp.sum(g0, axis=0, keepdims=True)

    @pl.when(first >= length)
    def _():
        half[...] = gs[...]
        vecs[2:3, :] += jnp.sum(gs[...].astype(f32), axis=0, keepdims=True)


def norm_one_call(info, dq, dk, dv, state, gs, gain, own, pieces, tiles_per):
    rows, d = dq.shape
    row = pl.BlockSpec((TILE, d), lambda i, s: (i, 0))
    return pl.pallas_call(
        functools.partial(norm_one_kernel, tiles_per),
        grid_spec=pltpu.PrefetchScalarGridSpec(
            num_scalar_prefetch=1,
            grid=(rows // TILE,),
            in_specs=[row] * 5 + [whole((1, d))] + [ANY] * (1 + COUNT),
            out_specs=[row, whole((8, d))],
            scratch_shapes=[
                pltpu.VMEM((3 * d, d), bf16),
                pltpu.VMEM((TILE, d), f32),
                pltpu.SemaphoreType.DMA,
            ],
        ),
        out_shape=[jax.ShapeDtypeStruct((rows, d), bf16), jax.ShapeDtypeStruct((8, d), f32)],
        compiler_params=params(1),
        cost_estimate=cost(6 * rows * d * d, rows * d * 16),
        name="norm_one_back",
    )(info, dq, dk, dv, state, gs, gain, own, *pieces)


def joined_kernel(side, info, half, *rest):
    parts, rest = (rest[:4], rest[4:]) if side == 0 else ((), rest)
    own, refs, rest = rest[0], rest[1 : 1 + COUNT], rest[1 + COUNT :]
    grad, out = (rest[0], rest[1]) if side == 0 else (rest[0], None)
    w, sem = rest[-2:]
    d = half.shape[1]
    i = pl.program_id(0)

    @pl.when(i == 0)
    def _():
        start_loads(info, refs, own, skip_targets(w), sem)
        wait_whole(w, sem)

    grad[...] = dot_nt(half[...], w[side * d : (side + 1) * d]).astype(bf16)
    source = (info[0] + 4 - i // (pl.num_programs(0) // 4)) & 3
    for k, ref in enumerate(parts):

        @pl.when(source == k)
        def _(ref=ref):
            out[...] = ref[...]


def joined_call(side, info, half, parts, own, pieces):
    rows, d = half.shape
    row = pl.BlockSpec((TILE, d), lambda i, s: (i, 0))
    per = rows // TILE // 4
    count = 2 if side == 0 else 1

    def part_spec(k):
        def index(i, s):
            at = i - ((s[0] + 4 - k) & 3) * per
            return jnp.clip(at, 0, per - 1), 0

        return pl.BlockSpec((TILE, d), index)

    return pl.pallas_call(
        functools.partial(joined_kernel, side),
        grid_spec=pltpu.PrefetchScalarGridSpec(
            num_scalar_prefetch=1,
            grid=(rows // TILE,),
            in_specs=[row] + [part_spec(k) for k in range(len(parts))] + [ANY] * (1 + COUNT),
            out_specs=[row] * count,
            scratch_shapes=[pltpu.VMEM((2 * d, d), bf16), pltpu.SemaphoreType.DMA],
        ),
        out_shape=[jax.ShapeDtypeStruct((rows, d), bf16)] * count,
        compiler_params=params(1),
        cost_estimate=cost(2 * rows * d * d, rows * d * 4),
        name="joined_back",
    )(info, half, *parts, own, *pieces)


def outer(a, b):
    return lax.dot_general(a, b, TN, preferred_element_type=f32).astype(bf16)


def part_of(array, index):
    return lax.dynamic_index_in_dim(array, index, 0, keepdims=False)


def in_order(mine, other, chip, core):
    blocks = []
    for h in range(2):
        for p in range(GROUP // 2):
            a, b = part_of(mine, chip ^ p), part_of(other, chip ^ p)
            blocks.append(jnp.where(core == h, a, b).astype(f32))
    return jnp.stack(blocks)


def sum_cores(x, core):
    x = x.reshape((2, GROUP // 2) + x.shape[1:])
    total = part_of(x, core).astype(f32) + across(part_of(x, 1 - core), 1).astype(f32)
    return total.astype(bf16)


def to_chips(kept, chip):
    return [across(part_of(kept, chip ^ (m // 2)), m) for m in (2, 4, 6)]


def sum_chips(kept, arrived, chip):
    total = part_of(kept, chip).astype(f32) + sum(x.astype(f32) for x in arrived)
    return total.astype(bf16)


def together(*values):
    return lax.optimization_barrier(values)


def body(
    hidden_in,
    skip_state,
    lengths,
    w_skip,
    b_skip,
    norm1_gain,
    norm1_bias,
    w_qkv,
    b_qv,
    w_out,
    b_out,
    norm2_gain,
    norm2_bias,
    w_up,
    b_up,
    w_down,
    b_down,
    cotangent,
):
    tensor = lax.axis_index("tensor")
    member = lax.rem(lax.axis_index("batch"), GROUP)
    info = jnp.concatenate([jnp.stack([tensor, member]).astype(jnp.int32), lengths])
    rows, d = hidden_in.shape
    seq = rows // lengths.shape[0]
    tiles_per = seq // TILE
    columns = w_out.shape[0]

    core, chip = member & 1, member >> 1
    first_col = tensor * columns

    def share(array, axis=0):
        size = array.shape[axis] // GROUP
        return lax.dynamic_slice_in_dim(array, member * size, size, axis)

    def line(v):
        return v[None, :]

    biases = jnp.concatenate([b_qv.reshape(-1), b_up])
    b_hi = biases.astype(bf16)
    b_mid = (biases - b_hi.astype(f32)).astype(bf16)
    b_low = (biases - b_hi.astype(f32) - b_mid.astype(f32)).astype(bf16)
    b_rows = jnp.concatenate([b_hi, b_mid, b_low])
    b_rows = jnp.pad(b_rows, (0, 16 * d - b_rows.size)).reshape(16, d)

    first_piece = jnp.concatenate([share(w_skip), share(w_out)], 0)
    first_z = jnp.stack([along(first_piece, k) for k in (1, 2, 3)])
    b_terms = jnp.stack([b_rows] + [along(b_rows, k) for k in (1, 2, 3)])

    qkv_own = jnp.swapaxes(w_qkv, 1, 2)
    qkv_piece = share(qkv_own, 1).reshape(-1, d)
    qkv_own = qkv_own.reshape(-1, d)
    up_piece = jnp.swapaxes(share(w_up, 1), 0, 1)
    ffn_piece = jnp.concatenate([up_piece, share(w_down)], 0)
    first_z, qkv_piece, qkv_own, ffn_piece, b_terms = together(
        first_z, qkv_piece, qkv_own, ffn_piece, b_terms
    )
    qkv_z = [along(qkv_piece, k) for k in (1, 2, 3)]
    grad_act = dot_nt(cotangent, w_down).astype(bf16)
    first_chips, qkv_z, ffn_piece, grad_act = together(
        tuple(from_chips(first_z)), tuple(qkv_z), ffn_piece, grad_act
    )
    first_all = from_cores(list(first_chips))
    first_all, qkv_z, ffn_piece = together(tuple(first_all), qkv_z, ffn_piece)

    qkv_chips = from_chips(jnp.stack(qkv_z))
    up1, up3 = along(ffn_piece, 1), along(ffn_piece, 3)
    state_zero, normed_one = skip_call(
        info, hidden_in, skip_state, line(b_skip), line(norm1_gain), line(norm1_bias),
        w_skip, first_all,
    )
    terms = b_terms.reshape(4, -1).astype(f32)
    size = biases.size
    relative = terms[:, :size] + terms[:, size : 2 * size] + terms[:, 2 * size : 3 * size]
    all_biases = jnp.stack([relative[(tensor - j) & 3] for j in range(4)])
    b_q = all_biases[:, :columns].reshape(1, d)
    b_v = all_biases[:, columns : 2 * columns].reshape(1, d)
    b_up_all = all_biases[:, 2 * columns :]
    qkv_chips, up1, up3, state_zero, normed_one, b_q, b_v = together(
        tuple(qkv_chips), up1, up3, state_zero, normed_one, b_q, b_v
    )

    qkv_all = from_cores(list(qkv_chips))
    up2 = along(up1, 1)
    pair_chips = from_chips(jnp.stack([up1, up3]))
    q, k, v = qkv_call(info, normed_one, b_q, b_v, qkv_own, qkv_all, tiles_per)
    q, k, v, up2 = together(q, k, v, up2)
    far_chips = from_chips(up2)
    mixed, lse = attend_call(info, q, k, v, seq)
    mixed, pair_chips = together(mixed, tuple(pair_chips))
    state_one, normed_two = mix_call(
        info, mixed, state_zero, line(b_out), line(norm2_gain), line(norm2_bias), w_out, first_all,
        tiles_per,
    )
    state_one, normed_two, far_chips = together(state_one, normed_two, tuple(far_chips))
    ffn_all = from_cores(list(pair_chips)) + from_cores(list(far_chips))
    before, acc, g_up, g_down, g_bup, g_bdown = ffn_own_call(
        info, normed_two, cotangent, grad_act, w_up, w_down, line(b_up)
    )
    before, acc, ffn_all, g_up, g_down = together(before, acc, tuple(ffn_all), g_up, g_down)
    g_up = lax.psum(g_up, "batch")
    out_rows, half_one, grad_mixed, vecs_two = ffn_rest_call(
        info, normed_two, cotangent, b_up_all, state_one, before, acc, line(norm2_gain),
        line(b_down), w_out, first_all, ffn_all, tiles_per,
    )
    out_rows, half_one, grad_mixed, g_up, g_down = together(
        out_rows, half_one, grad_mixed, g_up, g_down
    )
    g_down = lax.psum(g_down, "batch")
    out1, out3 = along(out_rows, 1), along(out_rows, 3)

    def own(array):
        return lax.dynamic_slice_in_dim(array, first_col, columns, 1)

    dq, dk, dv = attend_back_call(info, q, k, v, grad_mixed, mixed, lse, seq)
    dq, dk, dv, g_down, half_one, out1, out3 = together(dq, dk, dv, g_down, half_one, out1, out3)
    out2 = along(out1, 1)
    g_out = outer(own(mixed), half_one)
    slices = jnp.concatenate([own(x) for x in (dq, dk, dv)], 1)
    g_qkv = outer(normed_one, slices)
    g_bqv = jnp.sum(slices, axis=0, dtype=f32)
    one_group = lax.axis_size("batch") == GROUP
    heads = g_qkv.reshape(GROUP, d // GROUP, 3 * columns)
    if one_group:
        kept_heads = sum_cores(heads, core)
        kept_heads, dq, half_one = together(kept_heads, dq, half_one)
        sent_heads = to_chips(kept_heads, chip)
    else:
        heads = lax.psum(heads, "batch")

    half_zero, vecs_one = norm_one_call(
        info, dq, dk, dv, state_zero, half_one, line(norm1_gain), qkv_own, qkv_all, tiles_per
    )
    half_zero, vecs_one, out2 = together(half_zero, vecs_one, out2)
    if one_group:
        sent_heads, half_zero = together(tuple(sent_heads), half_zero)
    shard = w_skip.shape[0]
    joined = jnp.concatenate([hidden_in, skip_state], axis=1)
    features = lax.dynamic_slice_in_dim(joined, tensor * shard, shard, 1)
    g_skip = outer(features, half_zero)
    g_bqv = jnp.concatenate([g_bqv[:columns], g_bqv[2 * columns :]])
    g_bqv = jnp.pad(line(g_bqv), ((0, 0), (0, d - g_bqv.size)))
    vectors = jnp.concatenate(
        [vecs_two[:3], g_bdown, vecs_one[:3], g_bqv, g_bup.reshape(-1, d)], axis=0
    )
    vectors = jnp.pad(vectors, ((0, 2 * GROUP - vectors.shape[0]), (0, 0))).astype(bf16)
    parts = [g_skip, g_out, vectors]
    last = jnp.concatenate([x.reshape(GROUP, -1, d) for x in parts], axis=1)
    if one_group:
        kept = sum_cores(last, core)
        kept, half_zero = together(kept, half_zero)
        sent = to_chips(kept, chip)
        total_heads = sum_chips(kept_heads, sent_heads, chip)
        out_parts = [out_rows, out1, out2, out3]
        grad_hidden, output = joined_call(0, info, half_zero, out_parts, w_skip, first_all)
        sent, total_heads, grad_hidden, output, half_zero = together(
            tuple(sent), total_heads, grad_hidden, output, half_zero
        )
        total, half_zero = together(sum_chips(kept, sent, chip), half_zero)
        sums, sums_heads = from_chips(total), from_chips(total_heads)
        (grad_skip,) = joined_call(1, info, half_zero, [], w_skip, first_all)
        sums, sums_heads, grad_skip, g_up, g_down = together(
            tuple(sums), tuple(sums_heads), grad_skip, g_up.astype(f32), g_down.astype(f32)
        )
        sums, sums_heads = jnp.stack(sums), jnp.stack(sums_heads)
        other, other_heads = across(sums, 1), across(sums_heads, 1)
        last = in_order(sums, other, chip, core)
        heads = in_order(sums_heads, other_heads, chip, core)
    else:
        last = lax.psum(last, "batch").astype(f32)
        heads = heads.astype(f32)
        out_parts = [out_rows, out1, out2, out3]
        grad_hidden, output = joined_call(0, info, half_zero, out_parts, w_skip, first_all)
        (grad_skip,) = joined_call(1, info, half_zero, [], w_skip, first_all)
        g_up, g_down = g_up.astype(f32), g_down.astype(f32)
    ends = [0]
    for x in parts:
        ends.append(ends[-1] + x.size // d // GROUP)
    g_skip, g_out, vectors = [
        last[:, a:b].reshape(-1, d) for a, b in zip(ends[:-1], ends[1:])
    ]
    heads = heads.reshape(d, 3 * columns)
    g_qkv = jnp.stack([heads[:, n * columns : (n + 1) * columns] for n in range(3)])
    return (
        output,
        grad_hidden,
        grad_skip,
        g_skip,
        vectors[6],
        vectors[4],
        vectors[5],
        g_qkv,
        vectors[7, : 2 * columns].reshape(2, columns),
        g_out,
        vectors[2],
        vectors[0],
        vectors[1],
        g_up,
        vectors[8 : 8 + g_bup.size // d].reshape(-1),
        g_down,
        vectors[3],
    )


def solution(mesh):
    placed = (
        P("batch", None),
        P("batch", None),
        P("batch"),
        P("tensor", None),
        P(),
        P(),
        P(),
        P(None, None, "tensor"),
        P(None, "tensor"),
        P("tensor", None),
        P(),
        P(),
        P(),
        P(None, "tensor"),
        P("tensor"),
        P("tensor", None),
        P(),
        P("batch", None),
    )
    return jax.shard_map(
        body,
        mesh=mesh,
        in_specs=placed,
        out_specs=(
            P("batch", None),
            P("batch", None),
            P("batch", None),
            P("tensor", None),
            P(),
            P(),
            P(),
            P(None, None, "tensor"),
            P(None, "tensor"),
            P("tensor", None),
            P(),
            P(),
            P(),
            P(None, "tensor"),
            P("tensor"),
            P("tensor", None),
            P(),
        ),
        check_vma=False,
    )
```

```python
import functools

import jax
import jax.numpy as jnp
from jax import lax
from jax.experimental import pallas as pl
from jax.experimental.pallas import tpu as pltpu
from jax.sharding import PartitionSpec as P

HEADS = 16
HEAD_DIM = 64
GROUP = 8
TILE = 256
FFN_TILE = 512
LOG2E = 1.4426950408889634
LN2 = 0.6931471805599453
GELU_C = 0.7978845608028654
GELU_A = 0.044715

norm_eps = 1e-05
masked_score = -1e30
bf16 = jnp.bfloat16
f32 = jnp.float32

NT = (((1,), (1,)), ((), ()))
TN = (((0,), (0,)), ((), ()))

PIECES = [0, 2, 4, 6, 1, 3, 5, 7]
COUNT = len(PIECES)


def dot(a, b):
    return jnp.dot(a, b, preferred_element_type=f32)


def dot_nt(a, b):
    return lax.dot_general(a, b, NT, preferred_element_type=f32)


def dot_tn(a, b):
    return lax.dot_general(a, b, TN, preferred_element_type=f32)


def params(ndim, mib=60):
    return pltpu.CompilerParams(
        vmem_limit_bytes=mib * 1024 * 1024, dimension_semantics=("arbitrary",) * ndim
    )


def cost(flops, moved):
    return pl.CostEstimate(
        flops=int(flops) // 10, bytes_accessed=int(moved) // 10, transcendentals=0
    )


def along(x, k):
    n = lax.axis_size("tensor")
    return lax.ppermute(x, "tensor", [(i, (i + k) % n) for i in range(n)])


def across(x, m):
    n = lax.axis_size("batch")
    return lax.ppermute(x, "batch", [(i, i ^ m) for i in range(n)])


def from_chips(held):
    return [held, across(held, 2), across(held, 4), across(held, 6)]


def from_cores(held):
    return held + [across(x, 1) for x in held]


def after(x, *earlier):
    return lax.optimization_barrier((x,) + earlier)[0]


def start_loads(info, refs, own, targets, sem):
    for first, rows, own_first, dest, place in targets:
        off = pl.multiple_of(place(info[0], 0), 16)
        pltpu.make_async_copy(
            own.at[pl.ds(own_first, rows * GROUP)], dest.at[pl.ds(off, rows * GROUP)], sem
        ).start()
    for ref, m in zip(refs, PIECES):
        for kk in range(3):
            src_t = (info[0] + 3 - kk) & 3
            src_b = info[1] ^ m
            for first, rows, _, dest, place in targets:
                off = pl.multiple_of(place(src_t, src_b), 16)
                pltpu.make_async_copy(
                    ref.at[kk, pl.ds(first, rows)], dest.at[pl.ds(off, rows)], sem
                ).start()


def wait_whole(dest, sem):
    pltpu.make_async_copy(dest, dest, sem).wait()


ANY = pl.BlockSpec(memory_space=pltpu.HBM)


def whole(shape):
    return pl.BlockSpec(shape, lambda *_: (0,) * len(shape))


def once(shape):
    return pl.BlockSpec(shape, lambda *_: (0,) * len(shape), pipeline_mode=pl.Buffered(1))


def normalise(v):
    mean = jnp.mean(v, axis=-1, keepdims=True)
    centred = v - mean
    r = lax.rsqrt(jnp.mean(centred * centred, axis=-1, keepdims=True) + norm_eps)
    return centred * r, r


def norm_back(grad, n, r, gain):
    e = grad * gain
    return r * (
        e
        - jnp.mean(e, axis=-1, keepdims=True)
        - n * jnp.mean(e * n, axis=-1, keepdims=True)
    )


def tile_length(info, i, tiles_per, tile=TILE):
    u = i // tiles_per
    return (i - u * tiles_per) * tile, info[2 + u]


def skip_targets(w):
    shard = w.shape[0] // 4
    piece = shard // GROUP
    return [(0, piece, 0, w, lambda t, b: t * shard + b * piece)]


def load_halves(info, own, refs, w, sem):
    shard = own.shape[0]
    half = shard // 2
    core = info[1] & 1

    def start(ref, off):
        off = pl.multiple_of(off, 16)
        pltpu.make_async_copy(ref, w.at[pl.ds(off, ref.shape[0])], sem).start()

    start(own, info[0] * shard)
    for kk in range(3):
        first = ((info[0] + 3 - kk) & 3) * shard
        start(refs[kk], first + core * half)
        start(refs[3 + kk], first + (1 - core) * half)


def skip_kernel(info, hid, skp, b_skip, gain, bias, *rest):
    own, refs, (state, normed, w, sem) = rest[0], rest[1 : 1 + COUNT], rest[1 + COUNT :]

    @pl.when(pl.program_id(0) == 0)
    def _():
        start_loads(info, refs, own, skip_targets(w), sem)
        wait_whole(w, sem)

    width = hid.shape[1]
    total = dot(hid[...], w[:width]) + dot(skp[...], w[width:]) + b_skip[...]
    state[...] = total.astype(bf16)
    n, _ = normalise(total)
    normed[...] = (n * gain[...] + bias[...]).astype(bf16)


def skip_call(info, hid, skp, b_skip, gain, bias, own, pieces):
    rows, d = hid.shape
    row = pl.BlockSpec((TILE, d), lambda i, s: (i, 0))
    return pl.pallas_call(
        skip_kernel,
        grid_spec=pltpu.PrefetchScalarGridSpec(
            num_scalar_prefetch=1,
            grid=(rows // TILE,),
            in_specs=[row, row, whole((1, d)), whole((1, d)), whole((1, d))] + [ANY] * (1 + COUNT),
            out_specs=[row, row],
            scratch_shapes=[pltpu.VMEM((2 * d, d), bf16), pltpu.SemaphoreType.DMA],
        ),
        out_shape=[jax.ShapeDtypeStruct((rows, d), bf16)] * 2,
        compiler_params=params(1),
        cost_estimate=cost(4 * rows * d * d, rows * d * 10 + 4 * d * d),
        name="skip_norm",
    )(info, hid, skp, b_skip, gain, bias, own, *pieces)


def qkv_targets(w):
    d = w.shape[0] // 3
    shard = d // 4
    part = shard // GROUP
    return [
        (s * part, part, s * shard, w, lambda t, b, s=s: s * d + t * shard + b * part)
        for s in range(3)
    ]


def qkv_kernel(tiles_per, info, x, b_q, b_v, *rest):
    own, refs, (q, k, v, w, sem) = rest[0], rest[1 : 1 + COUNT], rest[1 + COUNT :]
    i = pl.program_id(0)
    d = x.shape[1]

    @pl.when(i == 0)
    def _():
        start_loads(info, refs, own, qkv_targets(w), sem)
        wait_whole(w, sem)

    first, length = tile_length(info, i, tiles_per)

    @pl.when(first < length)
    def _():
        xs = x[...]
        q[...] = ((dot_nt(xs, w[:d]) + b_q[...]) * (LOG2E * HEAD_DIM**-0.5)).astype(bf16)
        k[...] = dot_nt(xs, w[d : 2 * d]).astype(bf16)
        v[...] = (dot_nt(xs, w[2 * d :]) + b_v[...]).astype(bf16)


def qkv_call(info, x, b_q, b_v, own, pieces, tiles_per):
    rows, d = x.shape
    row = pl.BlockSpec((TILE, d), lambda i, s: (i, 0))
    return pl.pallas_call(
        functools.partial(qkv_kernel, tiles_per),
        grid_spec=pltpu.PrefetchScalarGridSpec(
            num_scalar_prefetch=1,
            grid=(rows // TILE,),
            in_specs=[row, whole((1, d)), whole((1, d))] + [ANY] * (1 + COUNT),
            out_specs=[row] * 3,
            scratch_shapes=[pltpu.VMEM((3 * d, d), bf16), pltpu.SemaphoreType.DMA],
        ),
        out_shape=[jax.ShapeDtypeStruct((rows, d), bf16)] * 3,
        compiler_params=params(1),
        cost_estimate=cost(4 * rows * d * d, rows * d * 8 + 6 * d * d),
        name="qkv",
    )(info, x, b_q, b_v, own, *pieces)


def slope2(head):
    return jnp.exp2(jnp.full((1, 1), -8.0 / HEADS, f32) * (head + 1).astype(f32)) * LOG2E


def attend_kernel(info, q, k, v, mixed, lse, dist):
    u, hp = pl.program_id(0), pl.program_id(1)
    seq = q.shape[0]
    tiles = seq // TILE
    length = info[2 + u]

    @pl.when((u == 0) & (hp == 0))
    def _():
        r = lax.broadcasted_iota(jnp.int32, dist.shape, 0)
        c = lax.broadcasted_iota(jnp.int32, dist.shape, 1)
        dist[...] = jnp.abs(r - c - (seq - TILE)).astype(f32)

    lane = lax.broadcasted_iota(jnp.int32, (TILE, 128), 1)
    used = (length + TILE - 1) // TILE

    for n in range(1, tiles + 1):

        @pl.when(used == n)
        def _(n=n):
            cols = n * TILE
            valid = (
                lax.broadcasted_iota(jnp.int32, (TILE, TILE), 0) + (cols - TILE) < length
            )
            vt = v[:cols, :].astype(f32).T.astype(bf16)

            ones = jnp.ones((16, cols), bf16)
            vts = [jnp.concatenate([vt[a * 64 : (a + 1) * 64, :], ones], axis=0) for a in range(2)]
            pick = jnp.where(
                lax.broadcasted_iota(jnp.int32, (8, 128), 1) // 64
                == lax.broadcasted_iota(jnp.int32, (8, 128), 0),
                1.0,
                0.0,
            ).astype(bf16)

            def longest(x):
                x = x[:cols, :].astype(f32)
                return jnp.max(dot_nt(pick, (x * x).astype(bf16)), axis=1, keepdims=True)

            small = jnp.max(longest(q) * longest(k)) < 3400.0

            def step(small, i):
                row0 = i * TILE
                qs = q[pl.ds(row0, TILE), :]
                gap = dist[pl.ds((seq - TILE) - row0, cols), :]
                held, outs = [], []
                for a in range(2):
                    qa = jnp.where((lane < 64) == (a == 0), qs, jnp.zeros_like(qs))
                    held.append(dot_nt(k[:cols, :], qa))
                for a in range(2):
                    s = held[a] - slope2(2 * hp + a) * gap
                    last = jnp.where(valid, s[cols - TILE :, :], masked_score)
                    s = jnp.concatenate([s[: cols - TILE, :], last], axis=0) if n > 1 else last
                    m = None if small else jnp.max(s, axis=0, keepdims=True)
                    held[a] = (jnp.exp2(s if small else s - m).astype(bf16), m)
                for a in range(2):
                    p, m = held[a]
                    o = dot(vts[a], p)
                    total = jnp.maximum(o[64:65, :], 1e-30)
                    outs.append(o[:64, :] * (1.0 / total))
                    total = jnp.log2(total) if small else m + jnp.log2(total)
                    lse[pl.ds(2 * hp + a, 1), pl.ds(row0, TILE)] = total
                o = jnp.concatenate(outs, axis=0).T
                pos = lax.broadcasted_iota(jnp.int32, (TILE, 128), 0) + row0
                mixed[pl.ds(row0, TILE), :] = jnp.where(pos < length, o, 0.0).astype(bf16)

            @pl.when(small)
            def _():
                for i in range(n):
                    step(True, i)

            @pl.when(jnp.logical_not(small))
            def _():
                for i in range(n):
                    step(False, i)

            if n < tiles:
                mixed[cols:, :] = jnp.zeros((seq - cols, 128), bf16)


def attend_call(info, q, k, v, seq):
    rows, d = q.shape
    utts = rows // seq
    blk = pl.BlockSpec((seq, 128), lambda u, h, s: (u, h))
    return pl.pallas_call(
        attend_kernel,
        grid_spec=pltpu.PrefetchScalarGridSpec(
            num_scalar_prefetch=1,
            grid=(utts, d // 128),
            in_specs=[blk] * 3,
            out_specs=[blk, pl.BlockSpec((HEADS, seq), lambda u, h, s: (0, u))],
            scratch_shapes=[pltpu.VMEM((2 * seq - TILE, TILE), f32)],
        ),
        out_shape=[
            jax.ShapeDtypeStruct((rows, d), bf16),
            jax.ShapeDtypeStruct((HEADS, rows), f32),
        ],
        compiler_params=params(2),
        cost_estimate=cost(rows * seq * d * 4, rows * d * 8),
        name="attend",
    )(info, q, k, v)


def attend_back_kernel(info, q, k, v, g, o, lse, dq, dk, dv, dist, akey, aval):
    u, hp = pl.program_id(0), pl.program_id(1)
    seq = q.shape[0]
    tiles = seq // TILE
    length = info[2 + u]

    @pl.when((u == 0) & (hp == 0))
    def _():
        r = lax.broadcasted_iota(jnp.int32, dist.shape, 0)
        c = lax.broadcasted_iota(jnp.int32, dist.shape, 1)
        dist[...] = jnp.abs(r - c - (seq - TILE)).astype(f32)

    lane = lax.broadcasted_iota(jnp.int32, (TILE, 128), 1)
    used = (length + TILE - 1) // TILE

    for n in range(1, tiles + 1):

        @pl.when(used == n)
        def _(n=n):
            cols = n * TILE
            valid = (
                lax.broadcasted_iota(jnp.int32, (TILE, TILE), 0) + (cols - TILE) < length
            )
            akey[:cols, :] = jnp.zeros((cols, 128), f32)
            aval[:cols, :] = jnp.zeros((cols, 128), f32)
            kt = k[:cols, :].astype(f32).T.astype(bf16)

            def step(i, carry):
                row0 = pl.multiple_of(i * TILE, TILE)
                qs = q[pl.ds(row0, TILE), :]
                gs = g[pl.ds(row0, TILE), :]
                start = pl.multiple_of((seq - TILE) - row0, TILE)
                gap = dist[pl.ds(start, cols), :]
                both = gs.astype(f32) * o[pl.ds(row0, TILE), :].astype(f32)
                hi = both.astype(bf16)
                lo = (both - hi.astype(f32)).astype(bf16)
                grads, held = [], []
                for a in range(2):
                    mine = (lane < 64) == (a == 0)
                    qa = jnp.where(mine, qs, jnp.zeros_like(qs))
                    ga = jnp.where(mine, gs, jnp.zeros_like(gs))
                    pick = jnp.where(
                        (lax.broadcasted_iota(jnp.int32, (8, 128), 1) < 64) == (a == 0), 1.0, 0.0
                    ).astype(bf16)
                    delta = (dot_nt(pick, hi) + dot_nt(pick, lo))[:1, :]
                    held.append((qa, ga, delta, dot_nt(k[:cols, :], qa), dot_nt(v[:cols, :], ga)))
                for a in range(2):
                    qa, ga, delta, s, gw = held[a]
                    row = lse[pl.ds(2 * hp + a, 1), pl.ds(row0, TILE)]
                    s = s - (slope2(2 * hp + a) * gap + row)
                    last = jnp.where(valid, s[cols - TILE :, :], masked_score)
                    s = jnp.concatenate([s[: cols - TILE, :], last], axis=0) if n > 1 else last
                    p = jnp.exp2(s)
                    ds = (p * (gw - delta)).astype(bf16)
                    held[a] = (qa, ga, p.astype(bf16), ds)
                aval[:cols, :] += dot(held[0][2], held[0][1]) + dot(held[1][2], held[1][1])
                akey[:cols, :] += dot(held[0][3], held[0][0]) + dot(held[1][3], held[1][0])
                for a in range(2):
                    grads.append(dot(kt[a * 64 : (a + 1) * 64, :], held[a][3]))
                turned = jnp.concatenate(grads, axis=0) * HEAD_DIM**-0.5
                dq[pl.ds(row0, TILE), :] = turned.T.astype(bf16)
                return carry

            lax.fori_loop(0, n, step, 0, unroll=True)
            dk[:cols, :] = (akey[:cols, :] * LN2).astype(bf16)
            dv[:cols, :] = aval[:cols, :].astype(bf16)
            if n < tiles:
                for ref in (dq, dk, dv):
                    ref[cols:, :] = jnp.zeros((seq - cols, 128), bf16)


def attend_back_call(info, q, k, v, g, o, lse, seq):
    rows, d = q.shape
    utts = rows // seq
    blk = pl.BlockSpec((seq, 128), lambda u, h, s: (u, h))
    return pl.pallas_call(
        attend_back_kernel,
        grid_spec=pltpu.PrefetchScalarGridSpec(
            num_scalar_prefetch=1,
            grid=(utts, d // 128),
            in_specs=[blk] * 5 + [pl.BlockSpec((HEADS, seq), lambda u, h, s: (0, u))],
            out_specs=[blk] * 3,
            scratch_shapes=[
                pltpu.VMEM((2 * seq - TILE, TILE), f32),
                pltpu.VMEM((seq, 128), f32),
                pltpu.VMEM((seq, 128), f32),
            ],
        ),
        out_shape=[jax.ShapeDtypeStruct((rows, d), bf16)] * 3,
        compiler_params=params(2),
        cost_estimate=cost(rows * seq * d * 10, rows * d * 16),
        name="attend_back",
    )(info, q, k, v, g, o, lse)


def mix_kernel(tiles_per, info, mixed, state, b_out, gain, bias, *rest):
    own, refs, (state_one, normed, w, total, sem) = rest[0], rest[1:7], rest[7:]
    i = pl.program_id(0)
    d = mixed.shape[1]

    @pl.when(i == 0)
    def _():
        load_halves(info, own, refs, w, sem)
        wait_whole(w, sem)

    first, length = tile_length(info, i, tiles_per)
    total[...] = state[...].astype(f32) + b_out[...]

    @pl.when(first < length)
    def _():
        total[...] += dot(mixed[...], w[...])

    n, _ = normalise(total[...])
    state_one[...] = total[...].astype(bf16)
    normed[...] = (n * gain[...] + bias[...]).astype(bf16)


def mix_call(info, mixed, state, b_out, gain, bias, own, pieces, tiles_per):
    rows, d = mixed.shape
    row = pl.BlockSpec((TILE, d), lambda i, s: (i, 0))
    return pl.pallas_call(
        functools.partial(mix_kernel, tiles_per),
        grid_spec=pltpu.PrefetchScalarGridSpec(
            num_scalar_prefetch=1,
            grid=(rows // TILE,),
            in_specs=[row, row] + [whole((1, d))] * 3 + [ANY] * 7,
            out_specs=[row, row],
            scratch_shapes=[
                pltpu.VMEM((d, d), bf16),
                pltpu.VMEM((TILE, d), f32),
                pltpu.SemaphoreType.DMA,
            ],
        ),
        out_shape=[jax.ShapeDtypeStruct((rows, d), bf16)] * 2,
        compiler_params=params(1),
        cost_estimate=cost(2 * rows * d * d, rows * d * 12),
        name="mix_norm",
    )(info, mixed, state, b_out, gain, bias, own, *pieces)


def gelu_both(pre):
    sq = pre * pre
    t = jnp.tanh(pre * (GELU_C + GELU_C * GELU_A * sq))
    h = 0.5 + 0.5 * t
    a = pre * h
    return a, h + a * (1.0 - h) * (2.0 * GELU_C + 6.0 * GELU_C * GELU_A * sq)


def ffn_own_kernel(
    info, x, c, gact, w_up, w_down, b_up, grad, acc, g_up, g_down, g_bup, g_bdown, aup, adown, act, gpre
):
    i, tiles = pl.program_id(0), pl.num_programs(0)

    @pl.when(i == 0)
    def _():
        aup[...] = jnp.zeros_like(aup)
        adown[...] = jnp.zeros_like(adown)
        g_bup[...] = jnp.zeros_like(g_bup)
        g_bdown[...] = jnp.zeros_like(g_bdown)

    xs, cs = x[...], c[...]
    a, slope = gelu_both(dot(xs, w_up[...]) + b_up[...])
    act[...] = a.astype(bf16)
    gp = gact[...].astype(f32) * slope
    gpre[...] = gp.astype(bf16)
    g_bup[...] += jnp.sum(gp, axis=0, keepdims=True)
    adown[...] += dot_tn(act[...], cs)
    aup[...] += dot_tn(xs, gpre[...])
    grad[...] = dot_nt(gpre[...], w_up[...]).astype(bf16)
    g_bdown[...] += jnp.sum(cs.astype(f32), axis=0, keepdims=True)

    own = tiles // 4

    @pl.when((i // own) == info[0])
    def _():
        out0 = pl.multiple_of(lax.rem(i, own) * FFN_TILE, FFN_TILE)
        acc[pl.ds(out0, FFN_TILE), :] = dot(act[...], w_down[...])

    @pl.when(i == tiles - 1)
    def _():
        g_up[...] = aup[...].astype(bf16)
        g_down[...] = adown[...].astype(bf16)


def ffn_own_call(info, x, c, gact, w_up, w_down, b_up):
    rows, d = x.shape
    hid = b_up.shape[1]
    row = pl.BlockSpec((FFN_TILE, d), lambda i, s: (i, 0))
    hid_row = pl.BlockSpec((FFN_TILE, hid), lambda i, s: (i, 0))
    return pl.pallas_call(
        ffn_own_kernel,
        grid_spec=pltpu.PrefetchScalarGridSpec(
            num_scalar_prefetch=1,
            grid=(rows // FFN_TILE,),
            in_specs=[row, row, hid_row, once((d, hid)), once((hid, d)), whole((1, hid))],
            out_specs=[
                row, once((rows // 4, d)), once((d, hid)), once((hid, d)), whole((1, hid)),
                whole((1, d)),
            ],
            scratch_shapes=[
                pltpu.VMEM((d, hid), f32),
                pltpu.VMEM((hid, d), f32),
                pltpu.VMEM((FFN_TILE, hid), bf16),
                pltpu.VMEM((FFN_TILE, hid), bf16),
            ],
        ),
        out_shape=[
            jax.ShapeDtypeStruct((rows, d), bf16),
            jax.ShapeDtypeStruct((rows // 4, d), f32),
            jax.ShapeDtypeStruct((d, hid), bf16),
            jax.ShapeDtypeStruct((hid, d), bf16),
            jax.ShapeDtypeStruct((1, hid), f32),
            jax.ShapeDtypeStruct((1, d), f32),
        ],
        compiler_params=params(1),
        cost_estimate=cost(rows * d * hid * 2 * 5.25, rows * d * 8),
        name="ffn_own",
    )(info, x, c, gact, w_up, w_down, b_up)


def ffn_rest_kernel(
    tiles_per, info, x, c, b_up, state, before, acc_in, gain, b_down, out_own, *rest
):
    pair_refs, far_refs = rest[:COUNT], rest[COUNT : 2 * COUNT]
    out_refs, rest = rest[2 * COUNT : 2 * COUNT + 6], rest[6:]
    out, half, g_mixed, vecs, w, w_out, grad, acc, act, sems, out_sem = rest[2 * COUNT :]
    k, i = pl.program_id(0), pl.program_id(1)
    blocks, tiles = pl.num_programs(0), pl.num_programs(1)
    hid = w.shape[1] // 2
    piece = hid // GROUP
    slot = lax.rem(k, 2)

    def load(sources, where):
        for ref, m in zip(sources, PIECES):
            off = pl.multiple_of((info[1] ^ m) * piece, 16)
            for part in range(2):
                pltpu.make_async_copy(
                    ref.at[pl.ds(part * piece, piece)],
                    w.at[where, pl.ds(part * hid + off, piece)],
                    sems.at[where],
                ).start()

    @pl.when((k == 0) & (i == 0))
    def _():
        load([ref.at[0] for ref in pair_refs], 0)
        vecs[...] = jnp.zeros_like(vecs)
        load_halves(info, out_own, out_refs, w_out, out_sem)

    @pl.when(i == 0)
    def _():
        wait_whole(w.at[slot], sems.at[slot])

        @pl.when(k == 0)
        def _():
            load([ref.at[1] for ref in pair_refs], 1)

        @pl.when(k == 1)
        def _():
            load(far_refs, 0)

    @pl.when((k == blocks - 1) & (i == 0))
    def _():
        wait_whole(w_out, out_sem)

    row0 = pl.multiple_of(i * FFN_TILE, FFN_TILE)
    xs = x[pl.ds(row0, FFN_TILE), :]
    cs = c[pl.ds(row0, FFN_TILE), :]
    src_t = (info[0] + jnp.where(k == 2, 2, 3 - 2 * k)) & 3
    bias = b_up[pl.ds(src_t, 1), :]
    cut = hid // 4
    grads = []
    for h in range(4):
        at = slice(h * cut, (h + 1) * cut)
        a, slope = gelu_both(dot_nt(xs, w[slot, at]) + bias[:, at])
        act[:, at] = a.astype(bf16)
        gact = dot_nt(cs, w[slot, hid + h * cut : hid + (h + 1) * cut])
        grads.append((gact * slope).astype(bf16))
    part = dot(jnp.concatenate(grads, axis=1), w[slot, :hid])

    @pl.when(k == 0)
    def _():
        grad[pl.ds(row0, FFN_TILE), :] = before[...].astype(f32) + part

    @pl.when((k > 0) & (k < blocks - 1))
    def _():
        grad[pl.ds(row0, FFN_TILE), :] += part

    own = tiles // 4
    mine = (i // own) == info[0]
    out0 = pl.multiple_of(lax.rem(i, own) * FFN_TILE, FFN_TILE)

    @pl.when(mine & (k == 0))
    def _():
        acc[pl.ds(out0, FFN_TILE), :] = acc_in[pl.ds(out0, FFN_TILE), :] + dot(act[...], w[slot, hid:])

    @pl.when(mine & (k > 0))
    def _():
        acc[pl.ds(out0, FFN_TILE), :] += dot(act[...], w[slot, hid:])

    @pl.when(k == blocks - 1)
    def _():
        g2 = grad[pl.ds(row0, FFN_TILE), :] + part
        s1 = state[...].astype(f32)
        n, r = normalise(s1)
        g1 = cs.astype(f32) + norm_back(g2, n, r, gain[...])
        half[...] = g1.astype(bf16)
        vecs[0:1, :] += jnp.sum(g2 * n, axis=0, keepdims=True)
        vecs[1:2, :] += jnp.sum(g2, axis=0, keepdims=True)
        vecs[2:3, :] += jnp.sum(g1, axis=0, keepdims=True)

        first, length = tile_length(info, i, tiles_per * TILE // FFN_TILE, FFN_TILE)

        @pl.when(first < length)
        def _():
            pos = lax.broadcasted_iota(jnp.int32, (FFN_TILE, 1), 0) + first
            g_mixed[...] = jnp.where(
                pos < length, dot_nt(half[...], w_out[...]), 0.0
            ).astype(bf16)

        @pl.when(mine)
        def _():
            out[pl.ds(out0, FFN_TILE), :] = (
                s1 + acc[pl.ds(out0, FFN_TILE), :] + b_down[...]
            ).astype(bf16)


def ffn_rest_call(
    info, x, c, b_up, state, before, acc, gain, b_down, out_own, out_pieces, pieces, tiles_per
):
    rows, d = x.shape
    hid = b_up.shape[1]
    tiles = rows // FFN_TILE
    last = pl.BlockSpec((FFN_TILE, d), lambda k, i, s: (jnp.where(k == 2, i, 0), 0))
    early = pl.BlockSpec((FFN_TILE, d), lambda k, i, s: (jnp.where(k == 0, i, tiles - 1), 0))
    return pl.pallas_call(
        functools.partial(ffn_rest_kernel, tiles_per),
        grid_spec=pltpu.PrefetchScalarGridSpec(
            num_scalar_prefetch=1,
            grid=(3, tiles),
            in_specs=[
                once((rows, d)), once((rows, d)), whole((4, hid)), last, early,
                once((rows // 4, d)), whole((1, d)), whole((1, d)), ANY,
            ]
            + [ANY] * (2 * COUNT + 6),
            out_specs=[once((rows // 4, d)), last, last, whole((8, d))],
            scratch_shapes=[
                pltpu.VMEM((2, 2 * hid, d), bf16),
                pltpu.VMEM((d, d), bf16),
                pltpu.VMEM((rows, d), f32),
                pltpu.VMEM((rows // 4, d), f32),
                pltpu.VMEM((FFN_TILE, hid), bf16),
                pltpu.SemaphoreType.DMA((2,)),
                pltpu.SemaphoreType.DMA,
            ],
        ),
        out_shape=[
            jax.ShapeDtypeStruct((rows // 4, d), bf16),
            jax.ShapeDtypeStruct((rows, d), bf16),
            jax.ShapeDtypeStruct((rows, d), bf16),
            jax.ShapeDtypeStruct((8, d), f32),
        ],
        compiler_params=params(2),
        cost_estimate=cost(rows * d * hid * 2 * 11, rows * d * 20),
        name="ffn_rest",
    )(info, x, c, b_up, state, before, acc, gain, b_down, out_own, *pieces, *out_pieces)


def norm_one_kernel(tiles_per, info, dq, dk, dv, state, gs, gain, *rest):
    own, refs, (half, vecs, w, grad, sem) = rest[0], rest[1 : 1 + COUNT], rest[1 + COUNT :]
    i = pl.program_id(0)
    d = dq.shape[1]

    @pl.when(i == 0)
    def _():
        start_loads(info, refs, own, qkv_targets(w), sem)
        vecs[...] = jnp.zeros_like(vecs)
        wait_whole(w, sem)

    first, length = tile_length(info, i, tiles_per)

    @pl.when(first < length)
    def _():
        grad[...] = (
            dot(dq[...], w[:d]) + dot(dk[...], w[d : 2 * d]) + dot(dv[...], w[2 * d :])
        )
        n, r = normalise(state[...].astype(f32))
        g1 = grad[...]
        g0 = gs[...].astype(f32) + norm_back(g1, n, r, gain[...])
        half[...] = g0.astype(bf16)
        vecs[0:1, :] += jnp.sum(g1 * n, axis=0, keepdims=True)
        vecs[1:2, :] += jnp.sum(g1, axis=0, keepdims=True)
        vecs[2:3, :] += jnp.sum(g0, axis=0, keepdims=True)

    @pl.when(first >= length)
    def _():
        half[...] = gs[...]
        vecs[2:3, :] += jnp.sum(gs[...].astype(f32), axis=0, keepdims=True)


def norm_one_call(info, dq, dk, dv, state, gs, gain, own, pieces, tiles_per):
    rows, d = dq.shape
    row = pl.BlockSpec((TILE, d), lambda i, s: (i, 0))
    return pl.pallas_call(
        functools.partial(norm_one_kernel, tiles_per),
        grid_spec=pltpu.PrefetchScalarGridSpec(
            num_scalar_prefetch=1,
            grid=(rows // TILE,),
            in_specs=[row] * 5 + [whole((1, d))] + [ANY] * (1 + COUNT),
            out_specs=[row, whole((8, d))],
            scratch_shapes=[
                pltpu.VMEM((3 * d, d), bf16),
                pltpu.VMEM((TILE, d), f32),
                pltpu.SemaphoreType.DMA,
            ],
        ),
        out_shape=[jax.ShapeDtypeStruct((rows, d), bf16), jax.ShapeDtypeStruct((8, d), f32)],
        compiler_params=params(1),
        cost_estimate=cost(6 * rows * d * d, rows * d * 16),
        name="norm_one_back",
    )(info, dq, dk, dv, state, gs, gain, own, *pieces)


def joined_kernel(side, info, half, *rest):
    parts, rest = (rest[:4], rest[4:]) if side == 0 else ((), rest)
    own, refs, rest = rest[0], rest[1 : 1 + COUNT], rest[1 + COUNT :]
    grad, out = (rest[0], rest[1]) if side == 0 else (rest[0], None)
    w, sem = rest[-2:]
    d = half.shape[1]
    i = pl.program_id(0)

    @pl.when(i == 0)
    def _():
        start_loads(info, refs, own, skip_targets(w), sem)
        wait_whole(w, sem)

    grad[...] = dot_nt(half[...], w[side * d : (side + 1) * d]).astype(bf16)
    source = (info[0] + 4 - i // (pl.num_programs(0) // 4)) & 3
    for k, ref in enumerate(parts):

        @pl.when(source == k)
        def _(ref=ref):
            out[...] = ref[...]


def joined_call(side, info, half, parts, own, pieces):
    rows, d = half.shape
    row = pl.BlockSpec((TILE, d), lambda i, s: (i, 0))
    per = rows // TILE // 4
    count = 2 if side == 0 else 1

    def part_spec(k):
        def index(i, s):
            at = i - ((s[0] + 4 - k) & 3) * per
            return jnp.clip(at, 0, per - 1), 0

        return pl.BlockSpec((TILE, d), index)

    return pl.pallas_call(
        functools.partial(joined_kernel, side),
        grid_spec=pltpu.PrefetchScalarGridSpec(
            num_scalar_prefetch=1,
            grid=(rows // TILE,),
            in_specs=[row] + [part_spec(k) for k in range(len(parts))] + [ANY] * (1 + COUNT),
            out_specs=[row] * count,
            scratch_shapes=[pltpu.VMEM((2 * d, d), bf16), pltpu.SemaphoreType.DMA],
        ),
        out_shape=[jax.ShapeDtypeStruct((rows, d), bf16)] * count,
        compiler_params=params(1),
        cost_estimate=cost(2 * rows * d * d, rows * d * 4),
        name="joined_back",
    )(info, half, *parts, own, *pieces)


def outer(a, b):
    return lax.dot_general(a, b, TN, preferred_element_type=f32).astype(bf16)


def part_of(array, index):
    return lax.dynamic_index_in_dim(array, index, 0, keepdims=False)


def in_order(mine, other, chip, core):
    blocks = []
    for h in range(2):
        for p in range(GROUP // 2):
            a, b = part_of(mine, chip ^ p), part_of(other, chip ^ p)
            blocks.append(jnp.where(core == h, a, b).astype(f32))
    return jnp.stack(blocks)


def sum_cores(x, core):
    x = x.reshape((2, GROUP // 2) + x.shape[1:])
    total = part_of(x, core).astype(f32) + across(part_of(x, 1 - core), 1).astype(f32)
    return total.astype(bf16)


def to_chips(kept, chip):
    return [across(part_of(kept, chip ^ (m // 2)), m) for m in (2, 4, 6)]


def sum_chips(kept, arrived, chip):
    total = part_of(kept, chip).astype(f32) + sum(x.astype(f32) for x in arrived)
    return total.astype(bf16)


def together(*values):
    return lax.optimization_barrier(values)


def body(
    hidden_in,
    skip_state,
    lengths,
    w_skip,
    b_skip,
    norm1_gain,
    norm1_bias,
    w_qkv,
    b_qv,
    w_out,
    b_out,
    norm2_gain,
    norm2_bias,
    w_up,
    b_up,
    w_down,
    b_down,
    cotangent,
):
    tensor = lax.axis_index("tensor")
    member = lax.rem(lax.axis_index("batch"), GROUP)
    info = jnp.concatenate([jnp.stack([tensor, member]).astype(jnp.int32), lengths])
    rows, d = hidden_in.shape
    seq = rows // lengths.shape[0]
    tiles_per = seq // TILE
    columns = w_out.shape[0]

    core, chip = member & 1, member >> 1
    first_col = tensor * columns

    def share(array, axis=0):
        size = array.shape[axis] // GROUP
        return lax.dynamic_slice_in_dim(array, member * size, size, axis)

    def line(v):
        return v[None, :]

    biases = jnp.concatenate([b_qv.reshape(-1), b_up])
    b_hi = biases.astype(bf16)
    b_mid = (biases - b_hi.astype(f32)).astype(bf16)
    b_low = (biases - b_hi.astype(f32) - b_mid.astype(f32)).astype(bf16)
    b_rows = jnp.concatenate([b_hi, b_mid, b_low])
    b_rows = jnp.pad(b_rows, (0, 16 * d - b_rows.size)).reshape(16, d)

    first_piece = share(w_skip)
    out_half = lax.dynamic_slice_in_dim(w_out, core * (columns // 2), columns // 2, 0)
    first_z = jnp.stack([along(first_piece, k) for k in (1, 2, 3)])
    b_terms = jnp.stack([b_rows] + [along(b_rows, k) for k in (1, 2, 3)])

    qkv_own = jnp.swapaxes(w_qkv, 1, 2)
    qkv_piece = share(qkv_own, 1).reshape(-1, d)
    qkv_own = qkv_own.reshape(-1, d)
    up_piece = jnp.swapaxes(share(w_up, 1), 0, 1)
    ffn_piece = jnp.concatenate([up_piece, share(w_down)], 0)
    first_z, qkv_piece, qkv_own, ffn_piece, b_terms = together(
        first_z, qkv_piece, qkv_own, ffn_piece, b_terms
    )
    qkv_z = [along(qkv_piece, k) for k in (1, 2, 3)]
    grad_act = dot_nt(cotangent, w_down).astype(bf16)
    first_chips, qkv_z, ffn_piece, grad_act = together(
        tuple(from_chips(first_z)), tuple(qkv_z), ffn_piece, grad_act
    )
    first_all = from_cores(list(first_chips))
    first_all, qkv_z, ffn_piece = together(tuple(first_all), qkv_z, ffn_piece)

    qkv_chips = from_chips(jnp.stack(qkv_z))
    up1, up3 = along(ffn_piece, 1), along(ffn_piece, 3)
    state_zero, normed_one = skip_call(
        info, hidden_in, skip_state, line(b_skip), line(norm1_gain), line(norm1_bias),
        w_skip, first_all,
    )
    terms = b_terms.reshape(4, -1).astype(f32)
    size = biases.size
    relative = terms[:, :size] + terms[:, size : 2 * size] + terms[:, 2 * size : 3 * size]
    all_biases = jnp.stack([relative[(tensor - j) & 3] for j in range(4)])
    b_q = all_biases[:, :columns].reshape(1, d)
    b_v = all_biases[:, columns : 2 * columns].reshape(1, d)
    b_up_all = all_biases[:, 2 * columns :]
    qkv_chips, up1, up3, state_zero, normed_one, b_q, b_v = together(
        tuple(qkv_chips), up1, up3, state_zero, normed_one, b_q, b_v
    )

    qkv_all = from_cores(list(qkv_chips))
    up2 = along(up1, 1)
    pair_chips = from_chips(jnp.stack([up1, up3]))
    q, k, v = qkv_call(info, normed_one, b_q, b_v, qkv_own, qkv_all, tiles_per)
    q, k, v, up2, out_half = together(q, k, v, up2, out_half)
    far_chips = from_chips(up2)
    out_near = [along(out_half, k) for k in (1, 2, 3)]
    mixed, lse = attend_call(info, q, k, v, seq)
    mixed, pair_chips, out_near = together(mixed, tuple(pair_chips), tuple(out_near))
    out_all = list(out_near) + [across(x, 1) for x in out_near]
    state_one, normed_two = mix_call(
        info, mixed, state_zero, line(b_out), line(norm2_gain), line(norm2_bias), w_out, out_all,
        tiles_per,
    )
    state_one, normed_two, far_chips = together(state_one, normed_two, tuple(far_chips))
    ffn_all = from_cores(list(pair_chips)) + from_cores(list(far_chips))
    before, acc, g_up, g_down, g_bup, g_bdown = ffn_own_call(
        info, normed_two, cotangent, grad_act, w_up, w_down, line(b_up)
    )
    before, acc, ffn_all, g_up, g_down = together(before, acc, tuple(ffn_all), g_up, g_down)
    g_up = lax.psum(g_up, "batch")
    out_rows, half_one, grad_mixed, vecs_two = ffn_rest_call(
        info, normed_two, cotangent, b_up_all, state_one, before, acc, line(norm2_gain),
        line(b_down), w_out, out_all, ffn_all, tiles_per,
    )
    out_rows, half_one, grad_mixed, g_up, g_down = together(
        out_rows, half_one, grad_mixed, g_up, g_down
    )
    g_down = lax.psum(g_down, "batch")
    out1, out3 = along(out_rows, 1), along(out_rows, 3)

    def own(array):
        return lax.dynamic_slice_in_dim(array, first_col, columns, 1)

    dq, dk, dv = attend_back_call(info, q, k, v, grad_mixed, mixed, lse, seq)
    dq, dk, dv, g_down, half_one, out1, out3 = together(dq, dk, dv, g_down, half_one, out1, out3)
    out2 = along(out1, 1)
    g_out = outer(own(mixed), half_one)
    slices = jnp.concatenate([own(x) for x in (dq, dk, dv)], 1)
    g_qkv = outer(normed_one, slices)
    g_bqv = jnp.sum(slices, axis=0, dtype=f32)
    one_group = lax.axis_size("batch") == GROUP
    heads = g_qkv.reshape(GROUP, d // GROUP, 3 * columns)
    if one_group:
        kept_heads = sum_cores(heads, core)
        kept_heads, dq, half_one = together(kept_heads, dq, half_one)
        sent_heads = to_chips(kept_heads, chip)
    else:
        heads = lax.psum(heads, "batch")

    half_zero, vecs_one = norm_one_call(
        info, dq, dk, dv, state_zero, half_one, line(norm1_gain), qkv_own, qkv_all, tiles_per
    )
    half_zero, vecs_one, out2 = together(half_zero, vecs_one, out2)
    if one_group:
        sent_heads, half_zero = together(tuple(sent_heads), half_zero)
    shard = w_skip.shape[0]
    joined = jnp.concatenate([hidden_in, skip_state], axis=1)
    features = lax.dynamic_slice_in_dim(joined, tensor * shard, shard, 1)
    g_skip = outer(features, half_zero)
    g_bqv = jnp.concatenate([g_bqv[:columns], g_bqv[2 * columns :]])
    g_bqv = jnp.pad(line(g_bqv), ((0, 0), (0, d - g_bqv.size)))
    vectors = jnp.concatenate(
        [vecs_two[:3], g_bdown, vecs_one[:3], g_bqv, g_bup.reshape(-1, d)], axis=0
    )
    vectors = jnp.pad(vectors, ((0, 2 * GROUP - vectors.shape[0]), (0, 0))).astype(bf16)
    parts = [g_skip, g_out, vectors]
    last = jnp.concatenate([x.reshape(GROUP, -1, d) for x in parts], axis=1)
    if one_group:
        kept = sum_cores(last, core)
        kept, half_zero = together(kept, half_zero)
        sent = to_chips(kept, chip)
        total_heads = sum_chips(kept_heads, sent_heads, chip)
        out_parts = [out_rows, out1, out2, out3]
        grad_hidden, output = joined_call(0, info, half_zero, out_parts, w_skip, first_all)
        sent, total_heads, grad_hidden, output, half_zero = together(
            tuple(sent), total_heads, grad_hidden, output, half_zero
        )
        total, half_zero = together(sum_chips(kept, sent, chip), half_zero)
        sums, sums_heads = from_chips(total), from_chips(total_heads)
        (grad_skip,) = joined_call(1, info, half_zero, [], w_skip, first_all)
        sums, sums_heads, grad_skip, g_up, g_down = together(
            tuple(sums), tuple(sums_heads), grad_skip, g_up.astype(f32), g_down.astype(f32)
        )
        sums, sums_heads = jnp.stack(sums), jnp.stack(sums_heads)
        other, other_heads = across(sums, 1), across(sums_heads, 1)
        last = in_order(sums, other, chip, core)
        heads = in_order(sums_heads, other_heads, chip, core)
    else:
        last = lax.psum(last, "batch").astype(f32)
        heads = heads.astype(f32)
        out_parts = [out_rows, out1, out2, out3]
        grad_hidden, output = joined_call(0, info, half_zero, out_parts, w_skip, first_all)
        (grad_skip,) = joined_call(1, info, half_zero, [], w_skip, first_all)
        g_up, g_down = g_up.astype(f32), g_down.astype(f32)
    ends = [0]
    for x in parts:
        ends.append(ends[-1] + x.size // d // GROUP)
    g_skip, g_out, vectors = [
        last[:, a:b].reshape(-1, d) for a, b in zip(ends[:-1], ends[1:])
    ]
    heads = heads.reshape(d, 3 * columns)
    g_qkv = jnp.stack([heads[:, n * columns : (n + 1) * columns] for n in range(3)])
    return (
        output,
        grad_hidden,
        grad_skip,
        g_skip,
        vectors[6],
        vectors[4],
        vectors[5],
        g_qkv,
        vectors[7, : 2 * columns].reshape(2, columns),
        g_out,
        vectors[2],
        vectors[0],
        vectors[1],
        g_up,
        vectors[8 : 8 + g_bup.size // d].reshape(-1),
        g_down,
        vectors[3],
    )


def solution(mesh):
    placed = (
        P("batch", None),
        P("batch", None),
        P("batch"),
        P("tensor", None),
        P(),
        P(),
        P(),
        P(None, None, "tensor"),
        P(None, "tensor"),
        P("tensor", None),
        P(),
        P(),
        P(),
        P(None, "tensor"),
        P("tensor"),
        P("tensor", None),
        P(),
        P("batch", None),
    )
    return jax.shard_map(
        body,
        mesh=mesh,
        in_specs=placed,
        out_specs=(
            P("batch", None),
            P("batch", None),
            P("batch", None),
            P("tensor", None),
            P(),
            P(),
            P(),
            P(None, None, "tensor"),
            P(None, "tensor"),
            P("tensor", None),
            P(),
            P(),
            P(),
            P(None, "tensor"),
            P("tensor"),
            P("tensor", None),
            P(),
        ),
        check_vma=False,
    )
```

```python
import functools

import jax
import jax.numpy as jnp
from jax import lax
from jax.experimental import pallas as pl
from jax.experimental.pallas import tpu as pltpu
from jax.sharding import PartitionSpec as P

HEADS = 16
HEAD_DIM = 64
GROUP = 8
TILE = 256
FFN_TILE = 512
LOG2E = 1.4426950408889634
LN2 = 0.6931471805599453
GELU_C = 0.7978845608028654
GELU_A = 0.044715

norm_eps = 1e-05
masked_score = -1e30
bf16 = jnp.bfloat16
f32 = jnp.float32

NT = (((1,), (1,)), ((), ()))
TN = (((0,), (0,)), ((), ()))

PIECES = [0, 2, 4, 6, 1, 3, 5, 7]
COUNT = len(PIECES)


def dot(a, b):
    return jnp.dot(a, b, preferred_element_type=f32)


def dot_nt(a, b):
    return lax.dot_general(a, b, NT, preferred_element_type=f32)


def dot_tn(a, b):
    return lax.dot_general(a, b, TN, preferred_element_type=f32)


def params(ndim, mib=60):
    return pltpu.CompilerParams(
        vmem_limit_bytes=mib * 1024 * 1024, dimension_semantics=("arbitrary",) * ndim
    )


def cost(flops, moved):
    return pl.CostEstimate(
        flops=int(flops) // 10, bytes_accessed=int(moved) // 10, transcendentals=0
    )


def along(x, k):
    n = lax.axis_size("tensor")
    return lax.ppermute(x, "tensor", [(i, (i + k) % n) for i in range(n)])


def across(x, m):
    n = lax.axis_size("batch")
    return lax.ppermute(x, "batch", [(i, i ^ m) for i in range(n)])


def from_chips(held):
    return [held, across(held, 2), across(held, 4), across(held, 6)]


def from_cores(held):
    return held + [across(x, 1) for x in held]


def after(x, *earlier):
    return lax.optimization_barrier((x,) + earlier)[0]


def start_loads(info, refs, own, targets, sem):
    for first, rows, own_first, dest, place in targets:
        off = pl.multiple_of(place(info[0], 0), 16)
        pltpu.make_async_copy(
            own.at[pl.ds(own_first, rows * GROUP)], dest.at[pl.ds(off, rows * GROUP)], sem
        ).start()
    for ref, m in zip(refs, PIECES):
        for kk in range(3):
            src_t = (info[0] + 3 - kk) & 3
            src_b = info[1] ^ m
            for first, rows, _, dest, place in targets:
                off = pl.multiple_of(place(src_t, src_b), 16)
                pltpu.make_async_copy(
                    ref.at[kk, pl.ds(first, rows)], dest.at[pl.ds(off, rows)], sem
                ).start()


def wait_whole(dest, sem):
    pltpu.make_async_copy(dest, dest, sem).wait()


ANY = pl.BlockSpec(memory_space=pltpu.HBM)


def whole(shape):
    return pl.BlockSpec(shape, lambda *_: (0,) * len(shape))


def once(shape):
    return pl.BlockSpec(shape, lambda *_: (0,) * len(shape), pipeline_mode=pl.Buffered(1))


def normalise(v):
    mean = jnp.mean(v, axis=-1, keepdims=True)
    centred = v - mean
    r = lax.rsqrt(jnp.mean(centred * centred, axis=-1, keepdims=True) + norm_eps)
    return centred * r, r


def norm_back(grad, n, r, gain):
    e = grad * gain
    return r * (
        e
        - jnp.mean(e, axis=-1, keepdims=True)
        - n * jnp.mean(e * n, axis=-1, keepdims=True)
    )


def tile_length(info, i, tiles_per, tile=TILE):
    u = i // tiles_per
    return (i - u * tiles_per) * tile, info[2 + u]


def skip_targets(w):
    shard = w.shape[0] // 4
    piece = shard // GROUP
    return [(0, piece, 0, w, lambda t, b: t * shard + b * piece)]


def out_targets(w, first):
    shard = w.shape[0] // 4
    piece = shard // GROUP
    return [(first, piece, 0, w, lambda t, b: t * shard + b * piece)]


def skip_kernel(info, hid, skp, b_skip, gain, bias, *rest):
    own, refs, (state, normed, w, sem) = rest[0], rest[1 : 1 + COUNT], rest[1 + COUNT :]

    @pl.when(pl.program_id(0) == 0)
    def _():
        start_loads(info, refs, own, skip_targets(w), sem)
        wait_whole(w, sem)

    width = hid.shape[1]
    total = dot(hid[...], w[:width]) + dot(skp[...], w[width:]) + b_skip[...]
    state[...] = total.astype(bf16)
    n, _ = normalise(total)
    normed[...] = (n * gain[...] + bias[...]).astype(bf16)


def skip_call(info, hid, skp, b_skip, gain, bias, own, pieces):
    rows, d = hid.shape
    row = pl.BlockSpec((TILE, d), lambda i, s: (i, 0))
    return pl.pallas_call(
        skip_kernel,
        grid_spec=pltpu.PrefetchScalarGridSpec(
            num_scalar_prefetch=1,
            grid=(rows // TILE,),
            in_specs=[row, row, whole((1, d)), whole((1, d)), whole((1, d))] + [ANY] * (1 + COUNT),
            out_specs=[row, row],
            scratch_shapes=[pltpu.VMEM((2 * d, d), bf16), pltpu.SemaphoreType.DMA],
        ),
        out_shape=[jax.ShapeDtypeStruct((rows, d), bf16)] * 2,
        compiler_params=params(1),
        cost_estimate=cost(4 * rows * d * d, rows * d * 10 + 4 * d * d),
        name="skip_norm",
    )(info, hid, skp, b_skip, gain, bias, own, *pieces)


def qkv_targets(w):
    d = w.shape[0] // 3
    shard = d // 4
    part = shard // GROUP
    return [
        (s * part, part, s * shard, w, lambda t, b, s=s: s * d + t * shard + b * part)
        for s in range(3)
    ]


def qkv_kernel(tiles_per, info, x, b_q, b_v, *rest):
    own, refs, (q, k, v, w, sem) = rest[0], rest[1 : 1 + COUNT], rest[1 + COUNT :]
    i = pl.program_id(0)
    d = x.shape[1]

    @pl.when(i == 0)
    def _():
        start_loads(info, refs, own, qkv_targets(w), sem)
        wait_whole(w, sem)

    first, length = tile_length(info, i, tiles_per)

    @pl.when(first < length)
    def _():
        xs = x[...]
        q[...] = ((dot_nt(xs, w[:d]) + b_q[...]) * (LOG2E * HEAD_DIM**-0.5)).astype(bf16)
        k[...] = dot_nt(xs, w[d : 2 * d]).astype(bf16)
        v[...] = (dot_nt(xs, w[2 * d :]) + b_v[...]).astype(bf16)


def qkv_call(info, x, b_q, b_v, own, pieces, tiles_per):
    rows, d = x.shape
    row = pl.BlockSpec((TILE, d), lambda i, s: (i, 0))
    return pl.pallas_call(
        functools.partial(qkv_kernel, tiles_per),
        grid_spec=pltpu.PrefetchScalarGridSpec(
            num_scalar_prefetch=1,
            grid=(rows // TILE,),
            in_specs=[row, whole((1, d)), whole((1, d))] + [ANY] * (1 + COUNT),
            out_specs=[row] * 3,
            scratch_shapes=[pltpu.VMEM((3 * d, d), bf16), pltpu.SemaphoreType.DMA],
        ),
        out_shape=[jax.ShapeDtypeStruct((rows, d), bf16)] * 3,
        compiler_params=params(1),
        cost_estimate=cost(4 * rows * d * d, rows * d * 8 + 6 * d * d),
        name="qkv",
    )(info, x, b_q, b_v, own, *pieces)


def slope2(head):
    return jnp.exp2(jnp.full((1, 1), -8.0 / HEADS, f32) * (head + 1).astype(f32)) * LOG2E


def attend_kernel(info, q, k, v, mixed, lse, dist):
    u, hp = pl.program_id(0), pl.program_id(1)
    seq = q.shape[0]
    tiles = seq // TILE
    length = info[2 + u]

    @pl.when((u == 0) & (hp == 0))
    def _():
        r = lax.broadcasted_iota(jnp.int32, dist.shape, 0)
        c = lax.broadcasted_iota(jnp.int32, dist.shape, 1)
        dist[...] = jnp.abs(r - c - (seq - TILE)).astype(f32)

    lane = lax.broadcasted_iota(jnp.int32, (TILE, 128), 1)
    used = (length + TILE - 1) // TILE

    for n in range(1, tiles + 1):

        @pl.when(used == n)
        def _(n=n):
            cols = n * TILE
            valid = (
                lax.broadcasted_iota(jnp.int32, (TILE, TILE), 0) + (cols - TILE) < length
            )
            vt = v[:cols, :].astype(f32).T.astype(bf16)

            ones = jnp.ones((16, cols), bf16)
            vts = [jnp.concatenate([vt[a * 64 : (a + 1) * 64, :], ones], axis=0) for a in range(2)]
            pick = jnp.where(
                lax.broadcasted_iota(jnp.int32, (8, 128), 1) // 64
                == lax.broadcasted_iota(jnp.int32, (8, 128), 0),
                1.0,
                0.0,
            ).astype(bf16)

            def longest(x):
                x = x[:cols, :].astype(f32)
                return jnp.max(dot_nt(pick, (x * x).astype(bf16)), axis=1, keepdims=True)

            small = jnp.max(longest(q) * longest(k)) < 3400.0

            def step(small, i):
                row0 = i * TILE
                qs = q[pl.ds(row0, TILE), :]
                gap = dist[pl.ds((seq - TILE) - row0, cols), :]
                held, outs = [], []
                for a in range(2):
                    qa = jnp.where((lane < 64) == (a == 0), qs, jnp.zeros_like(qs))
                    held.append(dot_nt(k[:cols, :], qa))
                for a in range(2):
                    s = held[a] - slope2(2 * hp + a) * gap
                    last = jnp.where(valid, s[cols - TILE :, :], masked_score)
                    s = jnp.concatenate([s[: cols - TILE, :], last], axis=0) if n > 1 else last
                    m = None if small else jnp.max(s, axis=0, keepdims=True)
                    held[a] = (jnp.exp2(s if small else s - m).astype(bf16), m)
                for a in range(2):
                    p, m = held[a]
                    o = dot(vts[a], p)
                    total = jnp.maximum(o[64:65, :], 1e-30)
                    outs.append(o[:64, :] * (1.0 / total))
                    total = jnp.log2(total) if small else m + jnp.log2(total)
                    lse[pl.ds(2 * hp + a, 1), pl.ds(row0, TILE)] = total
                o = jnp.concatenate(outs, axis=0).T
                pos = lax.broadcasted_iota(jnp.int32, (TILE, 128), 0) + row0
                mixed[pl.ds(row0, TILE), :] = jnp.where(pos < length, o, 0.0).astype(bf16)

            @pl.when(small)
            def _():
                for i in range(n):
                    step(True, i)

            @pl.when(jnp.logical_not(small))
            def _():
                for i in range(n):
                    step(False, i)

            if n < tiles:
                mixed[cols:, :] = jnp.zeros((seq - cols, 128), bf16)


def attend_call(info, q, k, v, seq):
    rows, d = q.shape
    utts = rows // seq
    blk = pl.BlockSpec((seq, 128), lambda u, h, s: (u, h))
    return pl.pallas_call(
        attend_kernel,
        grid_spec=pltpu.PrefetchScalarGridSpec(
            num_scalar_prefetch=1,
            grid=(utts, d // 128),
            in_specs=[blk] * 3,
            out_specs=[blk, pl.BlockSpec((HEADS, seq), lambda u, h, s: (0, u))],
            scratch_shapes=[pltpu.VMEM((2 * seq - TILE, TILE), f32)],
        ),
        out_shape=[
            jax.ShapeDtypeStruct((rows, d), bf16),
            jax.ShapeDtypeStruct((HEADS, rows), f32),
        ],
        compiler_params=params(2),
        cost_estimate=cost(rows * seq * d * 4, rows * d * 8),
        name="attend",
    )(info, q, k, v)


def attend_back_kernel(info, q, k, v, g, o, lse, dq, dk, dv, dist, akey, aval):
    u, hp = pl.program_id(0), pl.program_id(1)
    seq = q.shape[0]
    tiles = seq // TILE
    length = info[2 + u]

    @pl.when((u == 0) & (hp == 0))
    def _():
        r = lax.broadcasted_iota(jnp.int32, dist.shape, 0)
        c = lax.broadcasted_iota(jnp.int32, dist.shape, 1)
        dist[...] = jnp.abs(r - c - (seq - TILE)).astype(f32)

    lane = lax.broadcasted_iota(jnp.int32, (TILE, 128), 1)
    used = (length + TILE - 1) // TILE

    for n in range(1, tiles + 1):

        @pl.when(used == n)
        def _(n=n):
            cols = n * TILE
            valid = (
                lax.broadcasted_iota(jnp.int32, (TILE, TILE), 0) + (cols - TILE) < length
            )
            akey[:cols, :] = jnp.zeros((cols, 128), f32)
            aval[:cols, :] = jnp.zeros((cols, 128), f32)
            kt = k[:cols, :].astype(f32).T.astype(bf16)

            def step(i, carry):
                row0 = pl.multiple_of(i * TILE, TILE)
                qs = q[pl.ds(row0, TILE), :]
                gs = g[pl.ds(row0, TILE), :]
                start = pl.multiple_of((seq - TILE) - row0, TILE)
                gap = dist[pl.ds(start, cols), :]
                both = gs.astype(f32) * o[pl.ds(row0, TILE), :].astype(f32)
                hi = both.astype(bf16)
                lo = (both - hi.astype(f32)).astype(bf16)
                grads, held = [], []
                for a in range(2):
                    mine = (lane < 64) == (a == 0)
                    qa = jnp.where(mine, qs, jnp.zeros_like(qs))
                    ga = jnp.where(mine, gs, jnp.zeros_like(gs))
                    pick = jnp.where(
                        (lax.broadcasted_iota(jnp.int32, (8, 128), 1) < 64) == (a == 0), 1.0, 0.0
                    ).astype(bf16)
                    delta = (dot_nt(pick, hi) + dot_nt(pick, lo))[:1, :]
                    held.append((qa, ga, delta, dot_nt(k[:cols, :], qa), dot_nt(v[:cols, :], ga)))
                for a in range(2):
                    qa, ga, delta, s, gw = held[a]
                    row = lse[pl.ds(2 * hp + a, 1), pl.ds(row0, TILE)]
                    s = s - (slope2(2 * hp + a) * gap + row)
                    last = jnp.where(valid, s[cols - TILE :, :], masked_score)
                    s = jnp.concatenate([s[: cols - TILE, :], last], axis=0) if n > 1 else last
                    p = jnp.exp2(s)
                    ds = (p * (gw - delta)).astype(bf16)
                    held[a] = (qa, ga, p.astype(bf16), ds)
                aval[:cols, :] += dot(held[0][2], held[0][1]) + dot(held[1][2], held[1][1])
                akey[:cols, :] += dot(held[0][3], held[0][0]) + dot(held[1][3], held[1][0])
                for a in range(2):
                    grads.append(dot(kt[a * 64 : (a + 1) * 64, :], held[a][3]))
                turned = jnp.concatenate(grads, axis=0) * HEAD_DIM**-0.5
                dq[pl.ds(row0, TILE), :] = turned.T.astype(bf16)
                return carry

            lax.fori_loop(0, n, step, 0, unroll=True)
            dk[:cols, :] = (akey[:cols, :] * LN2).astype(bf16)
            dv[:cols, :] = aval[:cols, :].astype(bf16)
            if n < tiles:
                for ref in (dq, dk, dv):
                    ref[cols:, :] = jnp.zeros((seq - cols, 128), bf16)


def attend_back_call(info, q, k, v, g, o, lse, seq):
    rows, d = q.shape
    utts = rows // seq
    blk = pl.BlockSpec((seq, 128), lambda u, h, s: (u, h))
    return pl.pallas_call(
        attend_back_kernel,
        grid_spec=pltpu.PrefetchScalarGridSpec(
            num_scalar_prefetch=1,
            grid=(utts, d // 128),
            in_specs=[blk] * 5 + [pl.BlockSpec((HEADS, seq), lambda u, h, s: (0, u))],
            out_specs=[blk] * 3,
            scratch_shapes=[
                pltpu.VMEM((2 * seq - TILE, TILE), f32),
                pltpu.VMEM((seq, 128), f32),
                pltpu.VMEM((seq, 128), f32),
            ],
        ),
        out_shape=[jax.ShapeDtypeStruct((rows, d), bf16)] * 3,
        compiler_params=params(2),
        cost_estimate=cost(rows * seq * d * 10, rows * d * 16),
        name="attend_back",
    )(info, q, k, v, g, o, lse)


def mix_kernel(tiles_per, info, mixed, state, b_out, gain, bias, *rest):
    own, refs, (state_one, normed, w, total, sem) = rest[0], rest[1 : 1 + COUNT], rest[1 + COUNT :]
    part = (own.shape[0] // GROUP) * 3
    i = pl.program_id(0)
    d = mixed.shape[1]

    @pl.when(i == 0)
    def _():
        start_loads(info, refs, own, out_targets(w, part), sem)
        wait_whole(w, sem)

    first, length = tile_length(info, i, tiles_per)
    total[...] = state[...].astype(f32) + b_out[...]

    @pl.when(first < length)
    def _():
        total[...] += dot(mixed[...], w[...])

    n, _ = normalise(total[...])
    state_one[...] = total[...].astype(bf16)
    normed[...] = (n * gain[...] + bias[...]).astype(bf16)


def mix_call(info, mixed, state, b_out, gain, bias, own, pieces, tiles_per):
    rows, d = mixed.shape
    row = pl.BlockSpec((TILE, d), lambda i, s: (i, 0))
    return pl.pallas_call(
        functools.partial(mix_kernel, tiles_per),
        grid_spec=pltpu.PrefetchScalarGridSpec(
            num_scalar_prefetch=1,
            grid=(rows // TILE,),
            in_specs=[row, row] + [whole((1, d))] * 3 + [ANY] * (1 + COUNT),
            out_specs=[row, row],
            scratch_shapes=[
                pltpu.VMEM((d, d), bf16),
                pltpu.VMEM((TILE, d), f32),
                pltpu.SemaphoreType.DMA,
            ],
        ),
        out_shape=[jax.ShapeDtypeStruct((rows, d), bf16)] * 2,
        compiler_params=params(1),
        cost_estimate=cost(2 * rows * d * d, rows * d * 12),
        name="mix_norm",
    )(info, mixed, state, b_out, gain, bias, own, *pieces)


def gelu_both(pre):
    sq = pre * pre
    t = jnp.tanh(pre * (GELU_C + GELU_C * GELU_A * sq))
    h = 0.5 + 0.5 * t
    a = pre * h
    return a, h + a * (1.0 - h) * (2.0 * GELU_C + 6.0 * GELU_C * GELU_A * sq)


def ffn_own_kernel(
    info, x, c, gact, w_up, w_down, b_up, grad, acc, g_up, g_down, g_bup, g_bdown, aup, adown, act, gpre
):
    i, tiles = pl.program_id(0), pl.num_programs(0)

    @pl.when(i == 0)
    def _():
        aup[...] = jnp.zeros_like(aup)
        adown[...] = jnp.zeros_like(adown)
        g_bup[...] = jnp.zeros_like(g_bup)
        g_bdown[...] = jnp.zeros_like(g_bdown)

    xs, cs = x[...], c[...]
    a, slope = gelu_both(dot(xs, w_up[...]) + b_up[...])
    act[...] = a.astype(bf16)
    gp = gact[...].astype(f32) * slope
    gpre[...] = gp.astype(bf16)
    g_bup[...] += jnp.sum(gp, axis=0, keepdims=True)
    adown[...] += dot_tn(act[...], cs)
    aup[...] += dot_tn(xs, gpre[...])
    grad[...] = dot_nt(gpre[...], w_up[...]).astype(bf16)
    g_bdown[...] += jnp.sum(cs.astype(f32), axis=0, keepdims=True)

    own = tiles // 4

    @pl.when((i // own) == info[0])
    def _():
        out0 = pl.multiple_of(lax.rem(i, own) * FFN_TILE, FFN_TILE)
        acc[pl.ds(out0, FFN_TILE), :] = dot(act[...], w_down[...])

    @pl.when(i == tiles - 1)
    def _():
        g_up[...] = aup[...].astype(bf16)
        g_down[...] = adown[...].astype(bf16)


def ffn_own_call(info, x, c, gact, w_up, w_down, b_up):
    rows, d = x.shape
    hid = b_up.shape[1]
    row = pl.BlockSpec((FFN_TILE, d), lambda i, s: (i, 0))
    hid_row = pl.BlockSpec((FFN_TILE, hid), lambda i, s: (i, 0))
    return pl.pallas_call(
        ffn_own_kernel,
        grid_spec=pltpu.PrefetchScalarGridSpec(
            num_scalar_prefetch=1,
            grid=(rows // FFN_TILE,),
            in_specs=[row, row, hid_row, once((d, hid)), once((hid, d)), whole((1, hid))],
            out_specs=[
                row, once((rows // 4, d)), once((d, hid)), once((hid, d)), whole((1, hid)),
                whole((1, d)),
            ],
            scratch_shapes=[
                pltpu.VMEM((d, hid), f32),
                pltpu.VMEM((hid, d), f32),
                pltpu.VMEM((FFN_TILE, hid), bf16),
                pltpu.VMEM((FFN_TILE, hid), bf16),
            ],
        ),
        out_shape=[
            jax.ShapeDtypeStruct((rows, d), bf16),
            jax.ShapeDtypeStruct((rows // 4, d), f32),
            jax.ShapeDtypeStruct((d, hid), bf16),
            jax.ShapeDtypeStruct((hid, d), bf16),
            jax.ShapeDtypeStruct((1, hid), f32),
            jax.ShapeDtypeStruct((1, d), f32),
        ],
        compiler_params=params(1),
        cost_estimate=cost(rows * d * hid * 2 * 5.25, rows * d * 8),
        name="ffn_own",
    )(info, x, c, gact, w_up, w_down, b_up)


def ffn_rest_kernel(
    tiles_per, info, x, c, b_up, state, before, acc_in, gain, b_down, out_own, *rest
):
    pair_refs, far_refs = rest[:COUNT], rest[COUNT : 2 * COUNT]
    out_refs, rest = rest[2 * COUNT : 3 * COUNT], rest[COUNT:]
    out, half, g_mixed, vecs, w, w_out, grad, acc, act, sems, out_sem = rest[2 * COUNT :]
    k, i = pl.program_id(0), pl.program_id(1)
    blocks, tiles = pl.num_programs(0), pl.num_programs(1)
    hid = w.shape[1] // 2
    piece = hid // GROUP
    slot = lax.rem(k, 2)

    def load(sources, where):
        for ref, m in zip(sources, PIECES):
            off = pl.multiple_of((info[1] ^ m) * piece, 16)
            for part in range(2):
                pltpu.make_async_copy(
                    ref.at[pl.ds(part * piece, piece)],
                    w.at[where, pl.ds(part * hid + off, piece)],
                    sems.at[where],
                ).start()

    @pl.when((k == 0) & (i == 0))
    def _():
        load([ref.at[0] for ref in pair_refs], 0)
        vecs[...] = jnp.zeros_like(vecs)
        first = (out_own.shape[0] // GROUP) * 3
        start_loads(info, out_refs, out_own, out_targets(w_out, first), out_sem)

    @pl.when(i == 0)
    def _():
        wait_whole(w.at[slot], sems.at[slot])

        @pl.when(k == 0)
        def _():
            load([ref.at[1] for ref in pair_refs], 1)

        @pl.when(k == 1)
        def _():
            load(far_refs, 0)

    @pl.when((k == blocks - 1) & (i == 0))
    def _():
        wait_whole(w_out, out_sem)

    row0 = pl.multiple_of(i * FFN_TILE, FFN_TILE)
    xs = x[pl.ds(row0, FFN_TILE), :]
    cs = c[pl.ds(row0, FFN_TILE), :]
    src_t = (info[0] + jnp.where(k == 2, 2, 3 - 2 * k)) & 3
    bias = b_up[pl.ds(src_t, 1), :]
    cut = hid // 4
    grads = []
    for h in range(4):
        at = slice(h * cut, (h + 1) * cut)
        a, slope = gelu_both(dot_nt(xs, w[slot, at]) + bias[:, at])
        act[:, at] = a.astype(bf16)
        gact = dot_nt(cs, w[slot, hid + h * cut : hid + (h + 1) * cut])
        grads.append((gact * slope).astype(bf16))
    part = dot(jnp.concatenate(grads, axis=1), w[slot, :hid])

    @pl.when(k == 0)
    def _():
        grad[pl.ds(row0, FFN_TILE), :] = before[...].astype(f32) + part

    @pl.when((k > 0) & (k < blocks - 1))
    def _():
        grad[pl.ds(row0, FFN_TILE), :] += part

    own = tiles // 4
    mine = (i // own) == info[0]
    out0 = pl.multiple_of(lax.rem(i, own) * FFN_TILE, FFN_TILE)

    @pl.when(mine & (k == 0))
    def _():
        acc[pl.ds(out0, FFN_TILE), :] = acc_in[pl.ds(out0, FFN_TILE), :] + dot(act[...], w[slot, hid:])

    @pl.when(mine & (k > 0))
    def _():
        acc[pl.ds(out0, FFN_TILE), :] += dot(act[...], w[slot, hid:])

    @pl.when(k == blocks - 1)
    def _():
        g2 = grad[pl.ds(row0, FFN_TILE), :] + part
        s1 = state[...].astype(f32)
        n, r = normalise(s1)
        g1 = cs.astype(f32) + norm_back(g2, n, r, gain[...])
        half[...] = g1.astype(bf16)
        vecs[0:1, :] += jnp.sum(g2 * n, axis=0, keepdims=True)
        vecs[1:2, :] += jnp.sum(g2, axis=0, keepdims=True)
        vecs[2:3, :] += jnp.sum(g1, axis=0, keepdims=True)

        first, length = tile_length(info, i, tiles_per * TILE // FFN_TILE, FFN_TILE)

        @pl.when(first < length)
        def _():
            pos = lax.broadcasted_iota(jnp.int32, (FFN_TILE, 1), 0) + first
            g_mixed[...] = jnp.where(
                pos < length, dot_nt(half[...], w_out[...]), 0.0
            ).astype(bf16)

        @pl.when(mine)
        def _():
            out[pl.ds(out0, FFN_TILE), :] = (
                s1 + acc[pl.ds(out0, FFN_TILE), :] + b_down[...]
            ).astype(bf16)


def ffn_rest_call(
    info, x, c, b_up, state, before, acc, gain, b_down, out_own, out_pieces, pieces, tiles_per
):
    rows, d = x.shape
    hid = b_up.shape[1]
    tiles = rows // FFN_TILE
    last = pl.BlockSpec((FFN_TILE, d), lambda k, i, s: (jnp.where(k == 2, i, 0), 0))
    early = pl.BlockSpec((FFN_TILE, d), lambda k, i, s: (jnp.where(k == 0, i, tiles - 1), 0))
    return pl.pallas_call(
        functools.partial(ffn_rest_kernel, tiles_per),
        grid_spec=pltpu.PrefetchScalarGridSpec(
            num_scalar_prefetch=1,
            grid=(3, tiles),
            in_specs=[
                once((rows, d)), once((rows, d)), whole((4, hid)), last, early,
                once((rows // 4, d)), whole((1, d)), whole((1, d)), ANY,
            ]
            + [ANY] * (3 * COUNT),
            out_specs=[once((rows // 4, d)), last, last, whole((8, d))],
            scratch_shapes=[
                pltpu.VMEM((2, 2 * hid, d), bf16),
                pltpu.VMEM((d, d), bf16),
                pltpu.VMEM((rows, d), f32),
                pltpu.VMEM((rows // 4, d), f32),
                pltpu.VMEM((FFN_TILE, hid), bf16),
                pltpu.SemaphoreType.DMA((2,)),
                pltpu.SemaphoreType.DMA,
            ],
        ),
        out_shape=[
            jax.ShapeDtypeStruct((rows // 4, d), bf16),
            jax.ShapeDtypeStruct((rows, d), bf16),
            jax.ShapeDtypeStruct((rows, d), bf16),
            jax.ShapeDtypeStruct((8, d), f32),
        ],
        compiler_params=params(2),
        cost_estimate=cost(rows * d * hid * 2 * 11, rows * d * 20),
        name="ffn_rest",
    )(info, x, c, b_up, state, before, acc, gain, b_down, out_own, *pieces, *out_pieces)


def norm_one_kernel(tiles_per, info, dq, dk, dv, state, gs, gain, *rest):
    own, refs, (half, vecs, w, grad, sem) = rest[0], rest[1 : 1 + COUNT], rest[1 + COUNT :]
    i = pl.program_id(0)
    d = dq.shape[1]

    @pl.when(i == 0)
    def _():
        start_loads(info, refs, own, qkv_targets(w), sem)
        vecs[...] = jnp.zeros_like(vecs)
        wait_whole(w, sem)

    first, length = tile_length(info, i, tiles_per)

    @pl.when(first < length)
    def _():
        grad[...] = (
            dot(dq[...], w[:d]) + dot(dk[...], w[d : 2 * d]) + dot(dv[...], w[2 * d :])
        )
        n, r = normalise(state[...].astype(f32))
        g1 = grad[...]
        g0 = gs[...].astype(f32) + norm_back(g1, n, r, gain[...])
        half[...] = g0.astype(bf16)
        vecs[0:1, :] += jnp.sum(g1 * n, axis=0, keepdims=True)
        vecs[1:2, :] += jnp.sum(g1, axis=0, keepdims=True)
        vecs[2:3, :] += jnp.sum(g0, axis=0, keepdims=True)

    @pl.when(first >= length)
    def _():
        half[...] = gs[...]
        vecs[2:3, :] += jnp.sum(gs[...].astype(f32), axis=0, keepdims=True)


def norm_one_call(info, dq, dk, dv, state, gs, gain, own, pieces, tiles_per):
    rows, d = dq.shape
    row = pl.BlockSpec((TILE, d), lambda i, s: (i, 0))
    return pl.pallas_call(
        functools.partial(norm_one_kernel, tiles_per),
        grid_spec=pltpu.PrefetchScalarGridSpec(
            num_scalar_prefetch=1,
            grid=(rows // TILE,),
            in_specs=[row] * 5 + [whole((1, d))] + [ANY] * (1 + COUNT),
            out_specs=[row, whole((8, d))],
            scratch_shapes=[
                pltpu.VMEM((3 * d, d), bf16),
                pltpu.VMEM((TILE, d), f32),
                pltpu.SemaphoreType.DMA,
            ],
        ),
        out_shape=[jax.ShapeDtypeStruct((rows, d), bf16), jax.ShapeDtypeStruct((8, d), f32)],
        compiler_params=params(1),
        cost_estimate=cost(6 * rows * d * d, rows * d * 16),
        name="norm_one_back",
    )(info, dq, dk, dv, state, gs, gain, own, *pieces)


def joined_kernel(side, info, half, *rest):
    parts, rest = (rest[:4], rest[4:]) if side == 0 else ((), rest)
    own, refs, rest = rest[0], rest[1 : 1 + COUNT], rest[1 + COUNT :]
    grad, out = (rest[0], rest[1]) if side == 0 else (rest[0], None)
    w, sem = rest[-2:]
    d = half.shape[1]
    i = pl.program_id(0)

    @pl.when(i == 0)
    def _():
        start_loads(info, refs, own, skip_targets(w), sem)
        wait_whole(w, sem)

    grad[...] = dot_nt(half[...], w[side * d : (side + 1) * d]).astype(bf16)
    source = (info[0] + 4 - i // (pl.num_programs(0) // 4)) & 3
    for k, ref in enumerate(parts):

        @pl.when(source == k)
        def _(ref=ref):
            out[...] = ref[...]


def joined_call(side, info, half, parts, own, pieces):
    rows, d = half.shape
    row = pl.BlockSpec((TILE, d), lambda i, s: (i, 0))
    per = rows // TILE // 4
    count = 2 if side == 0 else 1

    def part_spec(k):
        def index(i, s):
            at = i - ((s[0] + 4 - k) & 3) * per
            return jnp.clip(at, 0, per - 1), 0

        return pl.BlockSpec((TILE, d), index)

    return pl.pallas_call(
        functools.partial(joined_kernel, side),
        grid_spec=pltpu.PrefetchScalarGridSpec(
            num_scalar_prefetch=1,
            grid=(rows // TILE,),
            in_specs=[row] + [part_spec(k) for k in range(len(parts))] + [ANY] * (1 + COUNT),
            out_specs=[row] * count,
            scratch_shapes=[pltpu.VMEM((2 * d, d), bf16), pltpu.SemaphoreType.DMA],
        ),
        out_shape=[jax.ShapeDtypeStruct((rows, d), bf16)] * count,
        compiler_params=params(1),
        cost_estimate=cost(2 * rows * d * d, rows * d * 4),
        name="joined_back",
    )(info, half, *parts, own, *pieces)


def outer(a, b):
    return lax.dot_general(a, b, TN, preferred_element_type=f32).astype(bf16)


def part_of(array, index):
    return lax.dynamic_index_in_dim(array, index, 0, keepdims=False)


def in_order(mine, other, chip, core):
    blocks = []
    for h in range(2):
        for p in range(GROUP // 2):
            a, b = part_of(mine, chip ^ p), part_of(other, chip ^ p)
            blocks.append(jnp.where(core == h, a, b).astype(f32))
    return jnp.stack(blocks)


def sum_cores(x, core):
    x = x.reshape((2, GROUP // 2) + x.shape[1:])
    total = part_of(x, core).astype(f32) + across(part_of(x, 1 - core), 1).astype(f32)
    return total.astype(bf16)


def to_chips(kept, chip):
    return [across(part_of(kept, chip ^ (m // 2)), m) for m in (2, 4, 6)]


def sum_chips(kept, arrived, chip):
    total = part_of(kept, chip).astype(f32) + sum(x.astype(f32) for x in arrived)
    return total.astype(bf16)


def together(*values):
    return lax.optimization_barrier(values)


def body(
    hidden_in,
    skip_state,
    lengths,
    w_skip,
    b_skip,
    norm1_gain,
    norm1_bias,
    w_qkv,
    b_qv,
    w_out,
    b_out,
    norm2_gain,
    norm2_bias,
    w_up,
    b_up,
    w_down,
    b_down,
    cotangent,
):
    tensor = lax.axis_index("tensor")
    member = lax.rem(lax.axis_index("batch"), GROUP)
    info = jnp.concatenate([jnp.stack([tensor, member]).astype(jnp.int32), lengths])
    rows, d = hidden_in.shape
    seq = rows // lengths.shape[0]
    tiles_per = seq // TILE
    columns = w_out.shape[0]

    core, chip = member & 1, member >> 1
    first_col = tensor * columns

    def share(array, axis=0):
        size = array.shape[axis] // GROUP
        return lax.dynamic_slice_in_dim(array, member * size, size, axis)

    def line(v):
        return v[None, :]

    biases = jnp.concatenate([b_qv.reshape(-1), b_up])
    b_hi = biases.astype(bf16)
    b_mid = (biases - b_hi.astype(f32)).astype(bf16)
    b_low = (biases - b_hi.astype(f32) - b_mid.astype(f32)).astype(bf16)
    b_rows = jnp.concatenate([b_hi, b_mid, b_low])
    b_rows = jnp.pad(b_rows, (0, 16 * d - b_rows.size)).reshape(16, d)

    first_piece = share(w_skip)
    first_z = jnp.stack([along(first_piece, k) for k in (1, 2, 3)])
    b_terms = jnp.stack([b_rows] + [along(b_rows, k) for k in (1, 2, 3)])

    qkv_own = jnp.swapaxes(w_qkv, 1, 2)
    qkv_piece = jnp.concatenate([share(qkv_own, 1).reshape(-1, d), share(w_out)], 0)
    qkv_own = qkv_own.reshape(-1, d)
    up_piece = jnp.swapaxes(share(w_up, 1), 0, 1)
    ffn_piece = jnp.concatenate([up_piece, share(w_down)], 0)
    first_z, qkv_piece, qkv_own, ffn_piece, b_terms = together(
        first_z, qkv_piece, qkv_own, ffn_piece, b_terms
    )
    qkv_z = [along(qkv_piece, k) for k in (1, 2, 3)]
    grad_act = dot_nt(cotangent, w_down).astype(bf16)
    first_chips, qkv_z, ffn_piece, grad_act = together(
        tuple(from_chips(first_z)), tuple(qkv_z), ffn_piece, grad_act
    )
    first_all = from_cores(list(first_chips))
    first_all, qkv_z, ffn_piece = together(tuple(first_all), qkv_z, ffn_piece)

    qkv_chips = from_chips(jnp.stack(qkv_z))
    up1, up3 = along(ffn_piece, 1), along(ffn_piece, 3)
    state_zero, normed_one = skip_call(
        info, hidden_in, skip_state, line(b_skip), line(norm1_gain), line(norm1_bias),
        w_skip, first_all,
    )
    terms = b_terms.reshape(4, -1).astype(f32)
    size = biases.size
    relative = terms[:, :size] + terms[:, size : 2 * size] + terms[:, 2 * size : 3 * size]
    all_biases = jnp.stack([relative[(tensor - j) & 3] for j in range(4)])
    b_q = all_biases[:, :columns].reshape(1, d)
    b_v = all_biases[:, columns : 2 * columns].reshape(1, d)
    b_up_all = all_biases[:, 2 * columns :]
    qkv_chips, up1, up3, state_zero, normed_one, b_q, b_v = together(
        tuple(qkv_chips), up1, up3, state_zero, normed_one, b_q, b_v
    )

    qkv_all = from_cores(list(qkv_chips))
    up2 = along(up1, 1)
    pair_chips = from_chips(jnp.stack([up1, up3]))
    q, k, v = qkv_call(info, normed_one, b_q, b_v, qkv_own, qkv_all, tiles_per)
    q, k, v, up2 = together(q, k, v, up2)
    far_chips = from_chips(up2)
    mixed, lse = attend_call(info, q, k, v, seq)
    mixed, pair_chips = together(mixed, tuple(pair_chips))
    state_one, normed_two = mix_call(
        info, mixed, state_zero, line(b_out), line(norm2_gain), line(norm2_bias), w_out, qkv_all,
        tiles_per,
    )
    state_one, normed_two, far_chips = together(state_one, normed_two, tuple(far_chips))
    ffn_all = from_cores(list(pair_chips)) + from_cores(list(far_chips))
    before, acc, g_up, g_down, g_bup, g_bdown = ffn_own_call(
        info, normed_two, cotangent, grad_act, w_up, w_down, line(b_up)
    )
    before, acc, ffn_all, g_up, g_down = together(before, acc, tuple(ffn_all), g_up, g_down)
    g_up = lax.psum(g_up, "batch")
    out_rows, half_one, grad_mixed, vecs_two = ffn_rest_call(
        info, normed_two, cotangent, b_up_all, state_one, before, acc, line(norm2_gain),
        line(b_down), w_out, qkv_all, ffn_all, tiles_per,
    )
    out_rows, half_one, grad_mixed, g_up, g_down = together(
        out_rows, half_one, grad_mixed, g_up, g_down
    )
    g_down = lax.psum(g_down, "batch")
    out1, out3 = along(out_rows, 1), along(out_rows, 3)

    def own(array):
        return lax.dynamic_slice_in_dim(array, first_col, columns, 1)

    dq, dk, dv = attend_back_call(info, q, k, v, grad_mixed, mixed, lse, seq)
    dq, dk, dv, g_down, half_one, out1, out3 = together(dq, dk, dv, g_down, half_one, out1, out3)
    out2 = along(out1, 1)
    g_out = outer(own(mixed), half_one)
    slices = jnp.concatenate([own(x) for x in (dq, dk, dv)], 1)
    g_qkv = outer(normed_one, slices)
    g_bqv = jnp.sum(slices, axis=0, dtype=f32)
    one_group = lax.axis_size("batch") == GROUP
    heads = g_qkv.reshape(GROUP, d // GROUP, 3 * columns)
    if one_group:
        kept_heads = sum_cores(heads, core)
        kept_heads, dq, half_one = together(kept_heads, dq, half_one)
        sent_heads = to_chips(kept_heads, chip)
    else:
        heads = lax.psum(heads, "batch")

    half_zero, vecs_one = norm_one_call(
        info, dq, dk, dv, state_zero, half_one, line(norm1_gain), qkv_own, qkv_all, tiles_per
    )
    half_zero, vecs_one, out2 = together(half_zero, vecs_one, out2)
    if one_group:
        sent_heads, half_zero = together(tuple(sent_heads), half_zero)
    shard = w_skip.shape[0]
    joined = jnp.concatenate([hidden_in, skip_state], axis=1)
    features = lax.dynamic_slice_in_dim(joined, tensor * shard, shard, 1)
    g_skip = outer(features, half_zero)
    g_bqv = jnp.concatenate([g_bqv[:columns], g_bqv[2 * columns :]])
    g_bqv = jnp.pad(line(g_bqv), ((0, 0), (0, d - g_bqv.size)))
    vectors = jnp.concatenate(
        [vecs_two[:3], g_bdown, vecs_one[:3], g_bqv, g_bup.reshape(-1, d)], axis=0
    )
    vectors = jnp.pad(vectors, ((0, 2 * GROUP - vectors.shape[0]), (0, 0))).astype(bf16)
    parts = [g_skip, g_out, vectors]
    last = jnp.concatenate([x.reshape(GROUP, -1, d) for x in parts], axis=1)
    if one_group:
        kept = sum_cores(last, core)
        kept, half_zero = together(kept, half_zero)
        sent = to_chips(kept, chip)
        total_heads = sum_chips(kept_heads, sent_heads, chip)
        out_parts = [out_rows, out1, out2, out3]
        grad_hidden, output = joined_call(0, info, half_zero, out_parts, w_skip, first_all)
        sent, total_heads, grad_hidden, output, half_zero = together(
            tuple(sent), total_heads, grad_hidden, output, half_zero
        )
        total, half_zero = together(sum_chips(kept, sent, chip), half_zero)
        sums, sums_heads = from_chips(total), from_chips(total_heads)
        (grad_skip,) = joined_call(1, info, half_zero, [], w_skip, first_all)
        sums, sums_heads, grad_skip, g_up, g_down = together(
            tuple(sums), tuple(sums_heads), grad_skip, g_up.astype(f32), g_down.astype(f32)
        )
        sums, sums_heads = jnp.stack(sums), jnp.stack(sums_heads)
        other, other_heads = across(sums, 1), across(sums_heads, 1)
        last = in_order(sums, other, chip, core)
        heads = in_order(sums_heads, other_heads, chip, core)
    else:
        last = lax.psum(last, "batch").astype(f32)
        heads = heads.astype(f32)
        out_parts = [out_rows, out1, out2, out3]
        grad_hidden, output = joined_call(0, info, half_zero, out_parts, w_skip, first_all)
        (grad_skip,) = joined_call(1, info, half_zero, [], w_skip, first_all)
        g_up, g_down = g_up.astype(f32), g_down.astype(f32)
    ends = [0]
    for x in parts:
        ends.append(ends[-1] + x.size // d // GROUP)
    g_skip, g_out, vectors = [
        last[:, a:b].reshape(-1, d) for a, b in zip(ends[:-1], ends[1:])
    ]
    heads = heads.reshape(d, 3 * columns)
    g_qkv = jnp.stack([heads[:, n * columns : (n + 1) * columns] for n in range(3)])
    return (
        output,
        grad_hidden,
        grad_skip,
        g_skip,
        vectors[6],
        vectors[4],
        vectors[5],
        g_qkv,
        vectors[7, : 2 * columns].reshape(2, columns),
        g_out,
        vectors[2],
        vectors[0],
        vectors[1],
        g_up,
        vectors[8 : 8 + g_bup.size // d].reshape(-1),
        g_down,
        vectors[3],
    )


def solution(mesh):
    placed = (
        P("batch", None),
        P("batch", None),
        P("batch"),
        P("tensor", None),
        P(),
        P(),
        P(),
        P(None, None, "tensor"),
        P(None, "tensor"),
        P("tensor", None),
        P(),
        P(),
        P(),
        P(None, "tensor"),
        P("tensor"),
        P("tensor", None),
        P(),
        P("batch", None),
    )
    return jax.shard_map(
        body,
        mesh=mesh,
        in_specs=placed,
        out_specs=(
            P("batch", None),
            P("batch", None),
            P("batch", None),
            P("tensor", None),
            P(),
            P(),
            P(),
            P(None, None, "tensor"),
            P(None, "tensor"),
            P("tensor", None),
            P(),
            P(),
            P(),
            P(None, "tensor"),
            P("tensor"),
            P("tensor", None),
            P(),
        ),
        check_vma=False,
    )
```

```python
import functools

import jax
import jax.numpy as jnp
from jax import lax
from jax.experimental import pallas as pl
from jax.experimental.pallas import tpu as pltpu
from jax.sharding import PartitionSpec as P

HEADS = 16
HEAD_DIM = 64
GROUP = 8
TILE = 256
FFN_TILE = 512
LOG2E = 1.4426950408889634
LN2 = 0.6931471805599453
GELU_C = 0.7978845608028654
GELU_A = 0.044715

norm_eps = 1e-05
masked_score = -1e30
bf16 = jnp.bfloat16
f32 = jnp.float32

NT = (((1,), (1,)), ((), ()))
TN = (((0,), (0,)), ((), ()))

PIECES = [0, 2, 4, 6, 1, 3, 5, 7]
COUNT = len(PIECES)


def dot(a, b):
    return jnp.dot(a, b, preferred_element_type=f32)


def dot_nt(a, b):
    return lax.dot_general(a, b, NT, preferred_element_type=f32)


def dot_tn(a, b):
    return lax.dot_general(a, b, TN, preferred_element_type=f32)


def params(ndim, mib=60):
    return pltpu.CompilerParams(
        vmem_limit_bytes=mib * 1024 * 1024, dimension_semantics=("arbitrary",) * ndim
    )


def cost(flops, moved):
    return pl.CostEstimate(
        flops=int(flops) // 10, bytes_accessed=int(moved) // 10, transcendentals=0
    )


def along(x, k):
    n = lax.axis_size("tensor")
    return lax.ppermute(x, "tensor", [(i, (i + k) % n) for i in range(n)])


def across(x, m):
    n = lax.axis_size("batch")
    return lax.ppermute(x, "batch", [(i, i ^ m) for i in range(n)])


def from_chips(held):
    return [held, across(held, 2), across(held, 4), across(held, 6)]


def from_cores(held):
    return held + [across(x, 1) for x in held]


def after(x, *earlier):
    return lax.optimization_barrier((x,) + earlier)[0]


def start_loads(info, refs, own, targets, sem):
    for first, rows, own_first, dest, place in targets:
        off = pl.multiple_of(place(info[0], 0), 16)
        pltpu.make_async_copy(
            own.at[pl.ds(own_first, rows * GROUP)], dest.at[pl.ds(off, rows * GROUP)], sem
        ).start()
    for ref, m in zip(refs, PIECES):
        for kk in range(3):
            src_t = (info[0] + 3 - kk) & 3
            src_b = info[1] ^ m
            for first, rows, _, dest, place in targets:
                off = pl.multiple_of(place(src_t, src_b), 16)
                pltpu.make_async_copy(
                    ref.at[kk, pl.ds(first, rows)], dest.at[pl.ds(off, rows)], sem
                ).start()


def wait_whole(dest, sem):
    pltpu.make_async_copy(dest, dest, sem).wait()


ANY = pl.BlockSpec(memory_space=pltpu.HBM)


def whole(shape):
    return pl.BlockSpec(shape, lambda *_: (0,) * len(shape))


def once(shape):
    return pl.BlockSpec(shape, lambda *_: (0,) * len(shape), pipeline_mode=pl.Buffered(1))


def normalise(v):
    mean = jnp.mean(v, axis=-1, keepdims=True)
    centred = v - mean
    r = lax.rsqrt(jnp.mean(centred * centred, axis=-1, keepdims=True) + norm_eps)
    return centred * r, r


def norm_back(grad, n, r, gain):
    e = grad * gain
    return r * (
        e
        - jnp.mean(e, axis=-1, keepdims=True)
        - n * jnp.mean(e * n, axis=-1, keepdims=True)
    )


def tile_length(info, i, tiles_per, tile=TILE):
    u = i // tiles_per
    return (i - u * tiles_per) * tile, info[2 + u]


def skip_targets(w):
    shard = w.shape[0] // 4
    piece = shard // GROUP
    return [(0, piece, 0, w, lambda t, b: t * shard + b * piece)]


def out_targets(w, first):
    shard = w.shape[0] // 4
    piece = shard // GROUP
    return [(first, piece, 0, w, lambda t, b: t * shard + b * piece)]


def skip_kernel(info, hid, skp, b_skip, gain, bias, *rest):
    own, refs, (state, normed, w, sem) = rest[0], rest[1 : 1 + COUNT], rest[1 + COUNT :]

    @pl.when(pl.program_id(0) == 0)
    def _():
        start_loads(info, refs, own, skip_targets(w), sem)
        wait_whole(w, sem)

    width = hid.shape[1]
    total = dot(hid[...], w[:width]) + dot(skp[...], w[width:]) + b_skip[...]
    state[...] = total.astype(bf16)
    n, _ = normalise(total)
    normed[...] = (n * gain[...] + bias[...]).astype(bf16)


def skip_call(info, hid, skp, b_skip, gain, bias, own, pieces):
    rows, d = hid.shape
    row = pl.BlockSpec((TILE, d), lambda i, s: (i, 0))
    return pl.pallas_call(
        skip_kernel,
        grid_spec=pltpu.PrefetchScalarGridSpec(
            num_scalar_prefetch=1,
            grid=(rows // TILE,),
            in_specs=[row, row, whole((1, d)), whole((1, d)), whole((1, d))] + [ANY] * (1 + COUNT),
            out_specs=[row, row],
            scratch_shapes=[pltpu.VMEM((2 * d, d), bf16), pltpu.SemaphoreType.DMA],
        ),
        out_shape=[jax.ShapeDtypeStruct((rows, d), bf16)] * 2,
        compiler_params=params(1),
        cost_estimate=cost(4 * rows * d * d, rows * d * 10 + 4 * d * d),
        name="skip_norm",
    )(info, hid, skp, b_skip, gain, bias, own, *pieces)


def qkv_targets(w):
    d = w.shape[0] // 3
    shard = d // 4
    part = shard // GROUP
    return [
        (s * part, part, s * shard, w, lambda t, b, s=s: s * d + t * shard + b * part)
        for s in range(3)
    ]


def qkv_kernel(tiles_per, info, x, b_q, b_v, *rest):
    own, refs, (q, k, v, w, sem) = rest[0], rest[1 : 1 + COUNT], rest[1 + COUNT :]
    i = pl.program_id(0)
    d = x.shape[1]

    @pl.when(i == 0)
    def _():
        start_loads(info, refs, own, qkv_targets(w), sem)
        wait_whole(w, sem)

    first, length = tile_length(info, i, tiles_per)

    @pl.when(first < length)
    def _():
        xs = x[...]
        q[...] = ((dot_nt(xs, w[:d]) + b_q[...]) * (LOG2E * HEAD_DIM**-0.5)).astype(bf16)
        k[...] = dot_nt(xs, w[d : 2 * d]).astype(bf16)
        v[...] = (dot_nt(xs, w[2 * d :]) + b_v[...]).astype(bf16)


def qkv_call(info, x, b_q, b_v, own, pieces, tiles_per):
    rows, d = x.shape
    row = pl.BlockSpec((TILE, d), lambda i, s: (i, 0))
    return pl.pallas_call(
        functools.partial(qkv_kernel, tiles_per),
        grid_spec=pltpu.PrefetchScalarGridSpec(
            num_scalar_prefetch=1,
            grid=(rows // TILE,),
            in_specs=[row, whole((1, d)), whole((1, d))] + [ANY] * (1 + COUNT),
            out_specs=[row] * 3,
            scratch_shapes=[pltpu.VMEM((3 * d, d), bf16), pltpu.SemaphoreType.DMA],
        ),
        out_shape=[jax.ShapeDtypeStruct((rows, d), bf16)] * 3,
        compiler_params=params(1),
        cost_estimate=cost(4 * rows * d * d, rows * d * 8 + 6 * d * d),
        name="qkv",
    )(info, x, b_q, b_v, own, *pieces)


def slope2(head):
    return jnp.exp2(jnp.full((1, 1), -8.0 / HEADS, f32) * (head + 1).astype(f32)) * LOG2E


def attend_kernel(info, q, k, v, mixed, lse, dist):
    u, hp = pl.program_id(0), pl.program_id(1)
    seq = q.shape[0]
    tiles = seq // TILE
    length = info[2 + u]

    @pl.when((u == 0) & (hp == 0))
    def _():
        r = lax.broadcasted_iota(jnp.int32, dist.shape, 0)
        c = lax.broadcasted_iota(jnp.int32, dist.shape, 1)
        dist[...] = jnp.abs(r - c - (seq - TILE)).astype(f32)

    lane = lax.broadcasted_iota(jnp.int32, (TILE, 128), 1)
    used = (length + TILE - 1) // TILE

    for n in range(1, tiles + 1):

        @pl.when(used == n)
        def _(n=n):
            cols = n * TILE
            valid = (
                lax.broadcasted_iota(jnp.int32, (TILE, TILE), 0) + (cols - TILE) < length
            )
            vt = v[:cols, :].astype(f32).T.astype(bf16)

            ones = jnp.ones((16, cols), bf16)
            vts = [jnp.concatenate([vt[a * 64 : (a + 1) * 64, :], ones], axis=0) for a in range(2)]
            pick = jnp.where(
                lax.broadcasted_iota(jnp.int32, (8, 128), 1) // 64
                == lax.broadcasted_iota(jnp.int32, (8, 128), 0),
                1.0,
                0.0,
            ).astype(bf16)

            def longest(x):
                x = x[:cols, :].astype(f32)
                return jnp.max(dot_nt(pick, (x * x).astype(bf16)), axis=1, keepdims=True)

            small = jnp.max(longest(q) * longest(k)) < 3400.0

            def step(small, i):
                row0 = i * TILE
                qs = q[pl.ds(row0, TILE), :]
                gap = dist[pl.ds((seq - TILE) - row0, cols), :]
                held, outs = [], []
                for a in range(2):
                    qa = jnp.where((lane < 64) == (a == 0), qs, jnp.zeros_like(qs))
                    held.append(dot_nt(k[:cols, :], qa))
                for a in range(2):
                    s = held[a] - slope2(2 * hp + a) * gap
                    last = jnp.where(valid, s[cols - TILE :, :], masked_score)
                    s = jnp.concatenate([s[: cols - TILE, :], last], axis=0) if n > 1 else last
                    m = None if small else jnp.max(s, axis=0, keepdims=True)
                    held[a] = (jnp.exp2(s if small else s - m).astype(bf16), m)
                for a in range(2):
                    p, m = held[a]
                    o = dot(vts[a], p)
                    total = jnp.maximum(o[64:65, :], 1e-30)
                    outs.append(o[:64, :] * (1.0 / total))
                    total = jnp.log2(total) if small else m + jnp.log2(total)
                    lse[pl.ds(2 * hp + a, 1), pl.ds(row0, TILE)] = total
                o = jnp.concatenate(outs, axis=0).T
                pos = lax.broadcasted_iota(jnp.int32, (TILE, 128), 0) + row0
                mixed[pl.ds(row0, TILE), :] = jnp.where(pos < length, o, 0.0).astype(bf16)

            @pl.when(small)
            def _():
                for i in range(n):
                    step(True, i)

            @pl.when(jnp.logical_not(small))
            def _():
                for i in range(n):
                    step(False, i)

            if n < tiles:
                mixed[cols:, :] = jnp.zeros((seq - cols, 128), bf16)


def attend_call(info, q, k, v, seq):
    rows, d = q.shape
    utts = rows // seq
    blk = pl.BlockSpec((seq, 128), lambda u, h, s: (u, h))
    return pl.pallas_call(
        attend_kernel,
        grid_spec=pltpu.PrefetchScalarGridSpec(
            num_scalar_prefetch=1,
            grid=(utts, d // 128),
            in_specs=[blk] * 3,
            out_specs=[blk, pl.BlockSpec((HEADS, seq), lambda u, h, s: (0, u))],
            scratch_shapes=[pltpu.VMEM((2 * seq - TILE, TILE), f32)],
        ),
        out_shape=[
            jax.ShapeDtypeStruct((rows, d), bf16),
            jax.ShapeDtypeStruct((HEADS, rows), f32),
        ],
        compiler_params=params(2),
        cost_estimate=cost(rows * seq * d * 4, rows * d * 8),
        name="attend",
    )(info, q, k, v)


def attend_back_kernel(info, q, k, v, g, o, lse, dq, dk, dv, dist, akey, aval):
    u, hp = pl.program_id(0), pl.program_id(1)
    seq = q.shape[0]
    tiles = seq // TILE
    length = info[2 + u]

    @pl.when((u == 0) & (hp == 0))
    def _():
        r = lax.broadcasted_iota(jnp.int32, dist.shape, 0)
        c = lax.broadcasted_iota(jnp.int32, dist.shape, 1)
        dist[...] = jnp.abs(r - c - (seq - TILE)).astype(f32)

    lane = lax.broadcasted_iota(jnp.int32, (TILE, 128), 1)
    used = (length + TILE - 1) // TILE

    for n in range(1, tiles + 1):

        @pl.when(used == n)
        def _(n=n):
            cols = n * TILE
            valid = (
                lax.broadcasted_iota(jnp.int32, (TILE, TILE), 0) + (cols - TILE) < length
            )
            akey[:cols, :] = jnp.zeros((cols, 128), f32)
            aval[:cols, :] = jnp.zeros((cols, 128), f32)
            kt = k[:cols, :].astype(f32).T.astype(bf16)

            def step(i, carry):
                row0 = pl.multiple_of(i * TILE, TILE)
                qs = q[pl.ds(row0, TILE), :]
                gs = g[pl.ds(row0, TILE), :]
                start = pl.multiple_of((seq - TILE) - row0, TILE)
                gap = dist[pl.ds(start, cols), :]
                both = gs.astype(f32) * o[pl.ds(row0, TILE), :].astype(f32)
                hi = both.astype(bf16)
                lo = (both - hi.astype(f32)).astype(bf16)
                grads, held = [], []
                for a in range(2):
                    mine = (lane < 64) == (a == 0)
                    qa = jnp.where(mine, qs, jnp.zeros_like(qs))
                    ga = jnp.where(mine, gs, jnp.zeros_like(gs))
                    pick = jnp.where(
                        (lax.broadcasted_iota(jnp.int32, (8, 128), 1) < 64) == (a == 0), 1.0, 0.0
                    ).astype(bf16)
                    delta = (dot_nt(pick, hi) + dot_nt(pick, lo))[:1, :]
                    held.append((qa, ga, delta, dot_nt(k[:cols, :], qa), dot_nt(v[:cols, :], ga)))
                for a in range(2):
                    qa, ga, delta, s, gw = held[a]
                    row = lse[pl.ds(2 * hp + a, 1), pl.ds(row0, TILE)]
                    s = s - (slope2(2 * hp + a) * gap + row)
                    last = jnp.where(valid, s[cols - TILE :, :], masked_score)
                    s = jnp.concatenate([s[: cols - TILE, :], last], axis=0) if n > 1 else last
                    p = jnp.exp2(s)
                    ds = (p * (gw - delta)).astype(bf16)
                    held[a] = (qa, ga, p.astype(bf16), ds)
                aval[:cols, :] += dot(held[0][2], held[0][1]) + dot(held[1][2], held[1][1])
                akey[:cols, :] += dot(held[0][3], held[0][0]) + dot(held[1][3], held[1][0])
                for a in range(2):
                    grads.append(dot(kt[a * 64 : (a + 1) * 64, :], held[a][3]))
                turned = jnp.concatenate(grads, axis=0) * HEAD_DIM**-0.5
                dq[pl.ds(row0, TILE), :] = turned.T.astype(bf16)
                return carry

            lax.fori_loop(0, n, step, 0, unroll=True)
            dk[:cols, :] = (akey[:cols, :] * LN2).astype(bf16)
            dv[:cols, :] = aval[:cols, :].astype(bf16)
            if n < tiles:
                for ref in (dq, dk, dv):
                    ref[cols:, :] = jnp.zeros((seq - cols, 128), bf16)


def attend_back_call(info, q, k, v, g, o, lse, seq):
    rows, d = q.shape
    utts = rows // seq
    blk = pl.BlockSpec((seq, 128), lambda u, h, s: (u, h))
    return pl.pallas_call(
        attend_back_kernel,
        grid_spec=pltpu.PrefetchScalarGridSpec(
            num_scalar_prefetch=1,
            grid=(utts, d // 128),
            in_specs=[blk] * 5 + [pl.BlockSpec((HEADS, seq), lambda u, h, s: (0, u))],
            out_specs=[blk] * 3,
            scratch_shapes=[
                pltpu.VMEM((2 * seq - TILE, TILE), f32),
                pltpu.VMEM((seq, 128), f32),
                pltpu.VMEM((seq, 128), f32),
            ],
        ),
        out_shape=[jax.ShapeDtypeStruct((rows, d), bf16)] * 3,
        compiler_params=params(2),
        cost_estimate=cost(rows * seq * d * 10, rows * d * 16),
        name="attend_back",
    )(info, q, k, v, g, o, lse)


def mix_kernel(tiles_per, info, mixed, state, b_out, gain, bias, *rest):
    own, refs, (state_one, normed, w, total, sem) = rest[0], rest[1 : 1 + COUNT], rest[1 + COUNT :]
    part = (own.shape[0] // GROUP) * 3
    i = pl.program_id(0)
    d = mixed.shape[1]

    @pl.when(i == 0)
    def _():
        start_loads(info, refs, own, out_targets(w, part), sem)
        wait_whole(w, sem)

    first, length = tile_length(info, i, tiles_per)
    total[...] = state[...].astype(f32) + b_out[...]

    @pl.when(first < length)
    def _():
        total[...] += dot(mixed[...], w[...])

    n, _ = normalise(total[...])
    state_one[...] = total[...].astype(bf16)
    normed[...] = (n * gain[...] + bias[...]).astype(bf16)


def mix_call(info, mixed, state, b_out, gain, bias, own, pieces, tiles_per):
    rows, d = mixed.shape
    row = pl.BlockSpec((TILE, d), lambda i, s: (i, 0))
    return pl.pallas_call(
        functools.partial(mix_kernel, tiles_per),
        grid_spec=pltpu.PrefetchScalarGridSpec(
            num_scalar_prefetch=1,
            grid=(rows // TILE,),
            in_specs=[row, row] + [whole((1, d))] * 3 + [ANY] * (1 + COUNT),
            out_specs=[row, row],
            scratch_shapes=[
                pltpu.VMEM((d, d), bf16),
                pltpu.VMEM((TILE, d), f32),
                pltpu.SemaphoreType.DMA,
            ],
        ),
        out_shape=[jax.ShapeDtypeStruct((rows, d), bf16)] * 2,
        compiler_params=params(1),
        cost_estimate=cost(2 * rows * d * d, rows * d * 12),
        name="mix_norm",
    )(info, mixed, state, b_out, gain, bias, own, *pieces)


def gelu_both(pre):
    sq = pre * pre
    t = jnp.tanh(pre * (GELU_C + GELU_C * GELU_A * sq))
    h = 0.5 + 0.5 * t
    a = pre * h
    return a, h + a * (1.0 - h) * (2.0 * GELU_C + 6.0 * GELU_C * GELU_A * sq)


def ffn_own_kernel(
    info, x, c, gact, w_up, w_down, b_up, grad, acc, g_up, g_down, g_bup, g_bdown, aup, adown, act, gpre
):
    i, tiles = pl.program_id(0), pl.num_programs(0)

    @pl.when(i == 0)
    def _():
        aup[...] = jnp.zeros_like(aup)
        adown[...] = jnp.zeros_like(adown)
        g_bup[...] = jnp.zeros_like(g_bup)
        g_bdown[...] = jnp.zeros_like(g_bdown)

    xs, cs = x[...], c[...]
    a, slope = gelu_both(dot(xs, w_up[...]) + b_up[...])
    act[...] = a.astype(bf16)
    gp = gact[...].astype(f32) * slope
    gpre[...] = gp.astype(bf16)
    g_bup[...] += jnp.sum(gp, axis=0, keepdims=True)
    adown[...] += dot_tn(act[...], cs)
    aup[...] += dot_tn(xs, gpre[...])
    grad[...] = dot_nt(gpre[...], w_up[...]).astype(bf16)
    g_bdown[...] += jnp.sum(cs.astype(f32), axis=0, keepdims=True)

    own = tiles // 4

    @pl.when((i // own) == info[0])
    def _():
        out0 = pl.multiple_of(lax.rem(i, own) * FFN_TILE, FFN_TILE)
        acc[pl.ds(out0, FFN_TILE), :] = dot(act[...], w_down[...])

    @pl.when(i == tiles - 1)
    def _():
        g_up[...] = aup[...].astype(bf16)
        g_down[...] = adown[...].astype(bf16)


def ffn_own_call(info, x, c, gact, w_up, w_down, b_up):
    rows, d = x.shape
    hid = b_up.shape[1]
    row = pl.BlockSpec((FFN_TILE, d), lambda i, s: (i, 0))
    hid_row = pl.BlockSpec((FFN_TILE, hid), lambda i, s: (i, 0))
    return pl.pallas_call(
        ffn_own_kernel,
        grid_spec=pltpu.PrefetchScalarGridSpec(
            num_scalar_prefetch=1,
            grid=(rows // FFN_TILE,),
            in_specs=[row, row, hid_row, once((d, hid)), once((hid, d)), whole((1, hid))],
            out_specs=[
                row, once((rows // 4, d)), once((d, hid)), once((hid, d)), whole((1, hid)),
                whole((1, d)),
            ],
            scratch_shapes=[
                pltpu.VMEM((d, hid), f32),
                pltpu.VMEM((hid, d), f32),
                pltpu.VMEM((FFN_TILE, hid), bf16),
                pltpu.VMEM((FFN_TILE, hid), bf16),
            ],
        ),
        out_shape=[
            jax.ShapeDtypeStruct((rows, d), bf16),
            jax.ShapeDtypeStruct((rows // 4, d), f32),
            jax.ShapeDtypeStruct((d, hid), bf16),
            jax.ShapeDtypeStruct((hid, d), bf16),
            jax.ShapeDtypeStruct((1, hid), f32),
            jax.ShapeDtypeStruct((1, d), f32),
        ],
        compiler_params=params(1),
        cost_estimate=cost(rows * d * hid * 2 * 5.25, rows * d * 8),
        name="ffn_own",
    )(info, x, c, gact, w_up, w_down, b_up)


def ffn_rest_kernel(
    tiles_per, info, x, c, b_up, state, before, acc_in, gain, b_down, out_own, *rest
):
    pair_refs, far_refs = rest[:COUNT], rest[COUNT : 2 * COUNT]
    out_refs, rest = rest[2 * COUNT : 3 * COUNT], rest[COUNT:]
    out, half, g_mixed, vecs, w, w_out, grad, acc, act, sems, out_sem = rest[2 * COUNT :]
    k, i = pl.program_id(0), pl.program_id(1)
    blocks, tiles = pl.num_programs(0), pl.num_programs(1)
    hid = w.shape[1] // 2
    piece = hid // GROUP
    slot = lax.rem(k, 2)

    def load(sources, where):
        for ref, m in zip(sources, PIECES):
            off = pl.multiple_of((info[1] ^ m) * piece, 16)
            for part in range(2):
                pltpu.make_async_copy(
                    ref.at[pl.ds(part * piece, piece)],
                    w.at[where, pl.ds(part * hid + off, piece)],
                    sems.at[where],
                ).start()

    @pl.when((k == 0) & (i == 0))
    def _():
        load([ref.at[0] for ref in pair_refs], 0)
        vecs[...] = jnp.zeros_like(vecs)
        first = (out_own.shape[0] // GROUP) * 3
        start_loads(info, out_refs, out_own, out_targets(w_out, first), out_sem)

    @pl.when(i == 0)
    def _():
        wait_whole(w.at[slot], sems.at[slot])

        @pl.when(k == 0)
        def _():
            load([ref.at[1] for ref in pair_refs], 1)

        @pl.when(k == 1)
        def _():
            load(far_refs, 0)

    @pl.when((k == blocks - 1) & (i == 0))
    def _():
        wait_whole(w_out, out_sem)

    row0 = pl.multiple_of(i * FFN_TILE, FFN_TILE)
    xs = x[pl.ds(row0, FFN_TILE), :]
    cs = c[pl.ds(row0, FFN_TILE), :]
    src_t = (info[0] + jnp.where(k == 2, 2, 3 - 2 * k)) & 3
    bias = b_up[pl.ds(src_t, 1), :]
    cut = hid // 4
    grads = []
    for h in range(4):
        at = slice(h * cut, (h + 1) * cut)
        a, slope = gelu_both(dot_nt(xs, w[slot, at]) + bias[:, at])
        act[:, at] = a.astype(bf16)
        gact = dot_nt(cs, w[slot, hid + h * cut : hid + (h + 1) * cut])
        grads.append((gact * slope).astype(bf16))
    part = dot(jnp.concatenate(grads, axis=1), w[slot, :hid])

    @pl.when(k == 0)
    def _():
        grad[pl.ds(row0, FFN_TILE), :] = before[...].astype(f32) + part

    @pl.when((k > 0) & (k < blocks - 1))
    def _():
        grad[pl.ds(row0, FFN_TILE), :] += part

    own = tiles // 4
    mine = (i // own) == info[0]
    out0 = pl.multiple_of(lax.rem(i, own) * FFN_TILE, FFN_TILE)

    @pl.when(mine & (k == 0))
    def _():
        acc[pl.ds(out0, FFN_TILE), :] = acc_in[pl.ds(out0, FFN_TILE), :] + dot(act[...], w[slot, hid:])

    @pl.when(mine & (k > 0))
    def _():
        acc[pl.ds(out0, FFN_TILE), :] += dot(act[...], w[slot, hid:])

    @pl.when(k == blocks - 1)
    def _():
        g2 = grad[pl.ds(row0, FFN_TILE), :] + part
        s1 = state[...].astype(f32)
        n, r = normalise(s1)
        g1 = cs.astype(f32) + norm_back(g2, n, r, gain[...])
        half[...] = g1.astype(bf16)
        vecs[0:1, :] += jnp.sum(g2 * n, axis=0, keepdims=True)
        vecs[1:2, :] += jnp.sum(g2, axis=0, keepdims=True)
        vecs[2:3, :] += jnp.sum(g1, axis=0, keepdims=True)

        first, length = tile_length(info, i, tiles_per * TILE // FFN_TILE, FFN_TILE)

        @pl.when(first < length)
        def _():
            pos = lax.broadcasted_iota(jnp.int32, (FFN_TILE, 1), 0) + first
            g_mixed[...] = jnp.where(
                pos < length, dot_nt(half[...], w_out[...]), 0.0
            ).astype(bf16)

        @pl.when(mine)
        def _():
            out[pl.ds(out0, FFN_TILE), :] = (
                s1 + acc[pl.ds(out0, FFN_TILE), :] + b_down[...]
            ).astype(bf16)


def ffn_rest_call(
    info, x, c, b_up, state, before, acc, gain, b_down, out_own, out_pieces, pieces, tiles_per
):
    rows, d = x.shape
    hid = b_up.shape[1]
    tiles = rows // FFN_TILE
    last = pl.BlockSpec((FFN_TILE, d), lambda k, i, s: (jnp.where(k == 2, i, 0), 0))
    early = pl.BlockSpec((FFN_TILE, d), lambda k, i, s: (jnp.where(k == 0, i, tiles - 1), 0))
    return pl.pallas_call(
        functools.partial(ffn_rest_kernel, tiles_per),
        grid_spec=pltpu.PrefetchScalarGridSpec(
            num_scalar_prefetch=1,
            grid=(3, tiles),
            in_specs=[
                once((rows, d)), once((rows, d)), whole((4, hid)), last, early,
                once((rows // 4, d)), whole((1, d)), whole((1, d)), ANY,
            ]
            + [ANY] * (3 * COUNT),
            out_specs=[once((rows // 4, d)), last, last, whole((8, d))],
            scratch_shapes=[
                pltpu.VMEM((2, 2 * hid, d), bf16),
                pltpu.VMEM((d, d), bf16),
                pltpu.VMEM((rows, d), f32),
                pltpu.VMEM((rows // 4, d), f32),
                pltpu.VMEM((FFN_TILE, hid), bf16),
                pltpu.SemaphoreType.DMA((2,)),
                pltpu.SemaphoreType.DMA,
            ],
        ),
        out_shape=[
            jax.ShapeDtypeStruct((rows // 4, d), bf16),
            jax.ShapeDtypeStruct((rows, d), bf16),
            jax.ShapeDtypeStruct((rows, d), bf16),
            jax.ShapeDtypeStruct((8, d), f32),
        ],
        compiler_params=params(2),
        cost_estimate=cost(rows * d * hid * 2 * 11, rows * d * 20),
        name="ffn_rest",
    )(info, x, c, b_up, state, before, acc, gain, b_down, out_own, *pieces, *out_pieces)


def norm_one_kernel(tiles_per, info, dq, dk, dv, state, gs, gain, *rest):
    own, refs, (half, vecs, w, grad, sem) = rest[0], rest[1 : 1 + COUNT], rest[1 + COUNT :]
    i = pl.program_id(0)
    d = dq.shape[1]

    @pl.when(i == 0)
    def _():
        start_loads(info, refs, own, qkv_targets(w), sem)
        vecs[...] = jnp.zeros_like(vecs)
        wait_whole(w, sem)

    first, length = tile_length(info, i, tiles_per)

    @pl.when(first < length)
    def _():
        grad[...] = (
            dot(dq[...], w[:d]) + dot(dk[...], w[d : 2 * d]) + dot(dv[...], w[2 * d :])
        )
        n, r = normalise(state[...].astype(f32))
        g1 = grad[...]
        g0 = gs[...].astype(f32) + norm_back(g1, n, r, gain[...])
        half[...] = g0.astype(bf16)
        vecs[0:1, :] += jnp.sum(g1 * n, axis=0, keepdims=True)
        vecs[1:2, :] += jnp.sum(g1, axis=0, keepdims=True)
        vecs[2:3, :] += jnp.sum(g0, axis=0, keepdims=True)

    @pl.when(first >= length)
    def _():
        half[...] = gs[...]
        vecs[2:3, :] += jnp.sum(gs[...].astype(f32), axis=0, keepdims=True)


def norm_one_call(info, dq, dk, dv, state, gs, gain, own, pieces, tiles_per):
    rows, d = dq.shape
    row = pl.BlockSpec((TILE, d), lambda i, s: (i, 0))
    return pl.pallas_call(
        functools.partial(norm_one_kernel, tiles_per),
        grid_spec=pltpu.PrefetchScalarGridSpec(
            num_scalar_prefetch=1,
            grid=(rows // TILE,),
            in_specs=[row] * 5 + [whole((1, d))] + [ANY] * (1 + COUNT),
            out_specs=[row, whole((8, d))],
            scratch_shapes=[
                pltpu.VMEM((3 * d, d), bf16),
                pltpu.VMEM((TILE, d), f32),
                pltpu.SemaphoreType.DMA,
            ],
        ),
        out_shape=[jax.ShapeDtypeStruct((rows, d), bf16), jax.ShapeDtypeStruct((8, d), f32)],
        compiler_params=params(1),
        cost_estimate=cost(6 * rows * d * d, rows * d * 16),
        name="norm_one_back",
    )(info, dq, dk, dv, state, gs, gain, own, *pieces)


def joined_kernel(side, info, half, *rest):
    parts, rest = (rest[:4], rest[4:]) if side == 0 else ((), rest)
    own, refs, rest = rest[0], rest[1 : 1 + COUNT], rest[1 + COUNT :]
    grad, out = (rest[0], rest[1]) if side == 0 else (rest[0], None)
    w, sem = rest[-2:]
    i = pl.program_id(0)

    @pl.when(i == 0)
    def _():
        shard = own.shape[0]
        piece = shard // GROUP

        def start(ref, t, off):
            @pl.when((t >> 1) == side)
            def _():
                place = pl.multiple_of((t & 1) * shard + off, 16)
                pltpu.make_async_copy(ref, w.at[pl.ds(place, ref.shape[0])], sem).start()

        start(own, info[0], 0)
        for ref, m in zip(refs, PIECES):
            for kk in range(3):
                start(ref.at[kk], (info[0] + 3 - kk) & 3, (info[1] ^ m) * piece)
        wait_whole(w, sem)

    grad[...] = dot_nt(half[...], w[...]).astype(bf16)
    source = (info[0] + 4 - i // (pl.num_programs(0) // 4)) & 3
    for k, ref in enumerate(parts):

        @pl.when(source == k)
        def _(ref=ref):
            out[...] = ref[...]


def joined_call(side, info, half, parts, own, pieces):
    rows, d = half.shape
    row = pl.BlockSpec((TILE, d), lambda i, s: (i, 0))
    per = rows // TILE // 4
    count = 2 if side == 0 else 1

    def part_spec(k):
        def index(i, s):
            at = i - ((s[0] + 4 - k) & 3) * per
            return jnp.clip(at, 0, per - 1), 0

        return pl.BlockSpec((TILE, d), index)

    return pl.pallas_call(
        functools.partial(joined_kernel, side),
        grid_spec=pltpu.PrefetchScalarGridSpec(
            num_scalar_prefetch=1,
            grid=(rows // TILE,),
            in_specs=[row] + [part_spec(k) for k in range(len(parts))] + [ANY] * (1 + COUNT),
            out_specs=[row] * count,
            scratch_shapes=[pltpu.VMEM((d, d), bf16), pltpu.SemaphoreType.DMA],
        ),
        out_shape=[jax.ShapeDtypeStruct((rows, d), bf16)] * count,
        compiler_params=params(1),
        cost_estimate=cost(2 * rows * d * d, rows * d * 4),
        name="joined_back",
    )(info, half, *parts, own, *pieces)


def outer(a, b):
    return lax.dot_general(a, b, TN, preferred_element_type=f32).astype(bf16)


def part_of(array, index):
    return lax.dynamic_index_in_dim(array, index, 0, keepdims=False)


def in_order(mine, other, chip, core):
    blocks = []
    for h in range(2):
        for p in range(GROUP // 2):
            a, b = part_of(mine, chip ^ p), part_of(other, chip ^ p)
            blocks.append(jnp.where(core == h, a, b).astype(f32))
    return jnp.stack(blocks)


def sum_cores(x, core):
    x = x.reshape((2, GROUP // 2) + x.shape[1:])
    total = part_of(x, core).astype(f32) + across(part_of(x, 1 - core), 1).astype(f32)
    return total.astype(bf16)


def to_chips(kept, chip):
    return [across(part_of(kept, chip ^ (m // 2)), m) for m in (2, 4, 6)]


def sum_chips(kept, arrived, chip):
    total = part_of(kept, chip).astype(f32) + sum(x.astype(f32) for x in arrived)
    return total.astype(bf16)


def together(*values):
    return lax.optimization_barrier(values)


def body(
    hidden_in,
    skip_state,
    lengths,
    w_skip,
    b_skip,
    norm1_gain,
    norm1_bias,
    w_qkv,
    b_qv,
    w_out,
    b_out,
    norm2_gain,
    norm2_bias,
    w_up,
    b_up,
    w_down,
    b_down,
    cotangent,
):
    tensor = lax.axis_index("tensor")
    member = lax.rem(lax.axis_index("batch"), GROUP)
    info = jnp.concatenate([jnp.stack([tensor, member]).astype(jnp.int32), lengths])
    rows, d = hidden_in.shape
    seq = rows // lengths.shape[0]
    tiles_per = seq // TILE
    columns = w_out.shape[0]

    core, chip = member & 1, member >> 1
    first_col = tensor * columns

    def share(array, axis=0):
        size = array.shape[axis] // GROUP
        return lax.dynamic_slice_in_dim(array, member * size, size, axis)

    def line(v):
        return v[None, :]

    biases = jnp.concatenate([b_qv.reshape(-1), b_up])
    b_hi = biases.astype(bf16)
    b_mid = (biases - b_hi.astype(f32)).astype(bf16)
    b_low = (biases - b_hi.astype(f32) - b_mid.astype(f32)).astype(bf16)
    b_rows = jnp.concatenate([b_hi, b_mid, b_low])
    b_rows = jnp.pad(b_rows, (0, 16 * d - b_rows.size)).reshape(16, d)

    first_piece = share(w_skip)
    first_z = jnp.stack([along(first_piece, k) for k in (1, 2, 3)])
    b_terms = jnp.stack([b_rows] + [along(b_rows, k) for k in (1, 2, 3)])

    qkv_own = jnp.swapaxes(w_qkv, 1, 2)
    qkv_piece = jnp.concatenate([share(qkv_own, 1).reshape(-1, d), share(w_out)], 0)
    qkv_own = qkv_own.reshape(-1, d)
    up_piece = jnp.swapaxes(share(w_up, 1), 0, 1)
    ffn_piece = jnp.concatenate([up_piece, share(w_down)], 0)
    first_z, qkv_piece, qkv_own, ffn_piece, b_terms = together(
        first_z, qkv_piece, qkv_own, ffn_piece, b_terms
    )
    qkv_z = [along(qkv_piece, k) for k in (1, 2, 3)]
    grad_act = dot_nt(cotangent, w_down).astype(bf16)
    first_chips, qkv_z, ffn_piece, grad_act = together(
        tuple(from_chips(first_z)), tuple(qkv_z), ffn_piece, grad_act
    )
    first_all = from_cores(list(first_chips))
    first_all, qkv_z, ffn_piece = together(tuple(first_all), qkv_z, ffn_piece)

    qkv_chips = from_chips(jnp.stack(qkv_z))
    up1, up3 = along(ffn_piece, 1), along(ffn_piece, 3)
    state_zero, normed_one = skip_call(
        info, hidden_in, skip_state, line(b_skip), line(norm1_gain), line(norm1_bias),
        w_skip, first_all,
    )
    terms = b_terms.reshape(4, -1).astype(f32)
    size = biases.size
    relative = terms[:, :size] + terms[:, size : 2 * size] + terms[:, 2 * size : 3 * size]
    all_biases = jnp.stack([relative[(tensor - j) & 3] for j in range(4)])
    b_q = all_biases[:, :columns].reshape(1, d)
    b_v = all_biases[:, columns : 2 * columns].reshape(1, d)
    b_up_all = all_biases[:, 2 * columns :]
    qkv_chips, up1, up3, state_zero, normed_one, b_q, b_v = together(
        tuple(qkv_chips), up1, up3, state_zero, normed_one, b_q, b_v
    )

    qkv_all = from_cores(list(qkv_chips))
    up2 = along(up1, 1)
    pair_chips = from_chips(jnp.stack([up1, up3]))
    q, k, v = qkv_call(info, normed_one, b_q, b_v, qkv_own, qkv_all, tiles_per)
    q, k, v, up2 = together(q, k, v, up2)
    far_chips = from_chips(up2)
    mixed, lse = attend_call(info, q, k, v, seq)
    mixed, pair_chips = together(mixed, tuple(pair_chips))
    state_one, normed_two = mix_call(
        info, mixed, state_zero, line(b_out), line(norm2_gain), line(norm2_bias), w_out, qkv_all,
        tiles_per,
    )
    state_one, normed_two, far_chips = together(state_one, normed_two, tuple(far_chips))
    ffn_all = from_cores(list(pair_chips)) + from_cores(list(far_chips))
    before, acc, g_up, g_down, g_bup, g_bdown = ffn_own_call(
        info, normed_two, cotangent, grad_act, w_up, w_down, line(b_up)
    )
    before, acc, ffn_all, g_up, g_down = together(before, acc, tuple(ffn_all), g_up, g_down)
    g_up = lax.psum(g_up, "batch")
    out_rows, half_one, grad_mixed, vecs_two = ffn_rest_call(
        info, normed_two, cotangent, b_up_all, state_one, before, acc, line(norm2_gain),
        line(b_down), w_out, qkv_all, ffn_all, tiles_per,
    )
    out_rows, half_one, grad_mixed, g_up, g_down = together(
        out_rows, half_one, grad_mixed, g_up, g_down
    )
    g_down = lax.psum(g_down, "batch")
    out1, out3 = along(out_rows, 1), along(out_rows, 3)

    def own(array):
        return lax.dynamic_slice_in_dim(array, first_col, columns, 1)

    dq, dk, dv = attend_back_call(info, q, k, v, grad_mixed, mixed, lse, seq)
    dq, dk, dv, g_down, half_one, out1, out3 = together(dq, dk, dv, g_down, half_one, out1, out3)
    out2 = along(out1, 1)
    g_out = outer(own(mixed), half_one)
    slices = jnp.concatenate([own(x) for x in (dq, dk, dv)], 1)
    g_qkv = outer(normed_one, slices)
    g_bqv = jnp.sum(slices, axis=0, dtype=f32)
    one_group = lax.axis_size("batch") == GROUP
    heads = g_qkv.reshape(GROUP, d // GROUP, 3 * columns)
    if one_group:
        kept_heads = sum_cores(heads, core)
        kept_heads, dq, half_one = together(kept_heads, dq, half_one)
        sent_heads = to_chips(kept_heads, chip)
    else:
        heads = lax.psum(heads, "batch")

    half_zero, vecs_one = norm_one_call(
        info, dq, dk, dv, state_zero, half_one, line(norm1_gain), qkv_own, qkv_all, tiles_per
    )
    half_zero, vecs_one, out2 = together(half_zero, vecs_one, out2)
    if one_group:
        sent_heads, half_zero = together(tuple(sent_heads), half_zero)
    shard = w_skip.shape[0]
    joined = jnp.concatenate([hidden_in, skip_state], axis=1)
    features = lax.dynamic_slice_in_dim(joined, tensor * shard, shard, 1)
    g_skip = outer(features, half_zero)
    g_bqv = jnp.concatenate([g_bqv[:columns], g_bqv[2 * columns :]])
    g_bqv = jnp.pad(line(g_bqv), ((0, 0), (0, d - g_bqv.size)))
    vectors = jnp.concatenate(
        [vecs_two[:3], g_bdown, vecs_one[:3], g_bqv, g_bup.reshape(-1, d)], axis=0
    )
    vectors = jnp.pad(vectors, ((0, 2 * GROUP - vectors.shape[0]), (0, 0))).astype(bf16)
    parts = [g_skip, g_out, vectors]
    last = jnp.concatenate([x.reshape(GROUP, -1, d) for x in parts], axis=1)
    if one_group:
        kept = sum_cores(last, core)
        kept, half_zero = together(kept, half_zero)
        sent = to_chips(kept, chip)
        total_heads = sum_chips(kept_heads, sent_heads, chip)
        out_parts = [out_rows, out1, out2, out3]
        grad_hidden, output = joined_call(0, info, half_zero, out_parts, w_skip, first_all)
        sent, total_heads, grad_hidden, output, half_zero = together(
            tuple(sent), total_heads, grad_hidden, output, half_zero
        )
        total, half_zero = together(sum_chips(kept, sent, chip), half_zero)
        sums, sums_heads = from_chips(total), from_chips(total_heads)
        (grad_skip,) = joined_call(1, info, half_zero, [], w_skip, first_all)
        sums, sums_heads, grad_skip, g_up, g_down = together(
            tuple(sums), tuple(sums_heads), grad_skip, g_up.astype(f32), g_down.astype(f32)
        )
        sums, sums_heads = jnp.stack(sums), jnp.stack(sums_heads)
        other, other_heads = across(sums, 1), across(sums_heads, 1)
        last = in_order(sums, other, chip, core)
        heads = in_order(sums_heads, other_heads, chip, core)
    else:
        last = lax.psum(last, "batch").astype(f32)
        heads = heads.astype(f32)
        out_parts = [out_rows, out1, out2, out3]
        grad_hidden, output = joined_call(0, info, half_zero, out_parts, w_skip, first_all)
        (grad_skip,) = joined_call(1, info, half_zero, [], w_skip, first_all)
        g_up, g_down = g_up.astype(f32), g_down.astype(f32)
    ends = [0]
    for x in parts:
        ends.append(ends[-1] + x.size // d // GROUP)
    g_skip, g_out, vectors = [
        last[:, a:b].reshape(-1, d) for a, b in zip(ends[:-1], ends[1:])
    ]
    heads = heads.reshape(d, 3 * columns)
    g_qkv = jnp.stack([heads[:, n * columns : (n + 1) * columns] for n in range(3)])
    return (
        output,
        grad_hidden,
        grad_skip,
        g_skip,
        vectors[6],
        vectors[4],
        vectors[5],
        g_qkv,
        vectors[7, : 2 * columns].reshape(2, columns),
        g_out,
        vectors[2],
        vectors[0],
        vectors[1],
        g_up,
        vectors[8 : 8 + g_bup.size // d].reshape(-1),
        g_down,
        vectors[3],
    )


def solution(mesh):
    placed = (
        P("batch", None),
        P("batch", None),
        P("batch"),
        P("tensor", None),
        P(),
        P(),
        P(),
        P(None, None, "tensor"),
        P(None, "tensor"),
        P("tensor", None),
        P(),
        P(),
        P(),
        P(None, "tensor"),
        P("tensor"),
        P("tensor", None),
        P(),
        P("batch", None),
    )
    return jax.shard_map(
        body,
        mesh=mesh,
        in_specs=placed,
        out_specs=(
            P("batch", None),
            P("batch", None),
            P("batch", None),
            P("tensor", None),
            P(),
            P(),
            P(),
            P(None, None, "tensor"),
            P(None, "tensor"),
            P("tensor", None),
            P(),
            P(),
            P(),
            P(None, "tensor"),
            P("tensor"),
            P("tensor", None),
            P(),
        ),
        check_vma=False,
    )
```
